256 devices in a mesh: span: 32 (over z, x), gx: 2 (over core), gy: 4 (over y).
Axes of the slice: x: 4, y: 4, z: 8, core: 2. Of those that a mesh axis runs over, the one named last changes fastest.
Arguments:
- flow_state: float32 [8, 8, 256, 320], P('gx', 'gy', 'span'), may hold values from -6 to 6
- source_term: float32 [8, 8, 256, 320], P('gx', 'gy', 'span'), may hold values from -6 to 6
- pseudo_time: float32 [8, 8, 256, 320], P('gx', 'gy', 'span'), may hold values from 1 to 4
- volume_jacobian: float32 [8, 8, 256, 3, 5, 5], P('gx', 'gy', 'span'), may hold values from -1.8 to 1.8
- side_jacobian: float32 [8, 8, 256, 4, 5, 5], P('gx', 'gy', 'span'), may hold values from -1.2 to 1.2
- span_jacobian: float32 [8, 8, 256, 2, 5, 5], P('gx', 'gy', 'span'), may hold values from -0.06 to 0.17
- line_inverse: float32 [8, 8, 320, 320], P('gx', 'gy'), may hold values from -0.02 to 1.02
- mirror_face: int32 [8, 8, 256, 4], P('gx', 'gy', 'span'), may hold values from 0 to 1
- edge_flip: int32 [8, 8, 256, 4], P('gx', 'gy', 'span'), may hold values from 0 to 1
Outputs:
- updated_state: float32 [8, 8, 256, 320], P('gx', 'gy', 'span')
- residual: float32 [8, 8, 256, 320], P('gx', 'gy', 'span')
The draws below stay inside these ranges and needn't reach their ends.
All inputs are finite; a program needn't handle non-finite values.
Results may differ from the reference program's by a relative error of at most 0.0003.
Values sent between devices are 32-bit elements; how exact they have to be, the bound alone decides.
No kernel may reach another device: no remote copies, remote signals or barrier semaphores. Data moves between devices by JAX's collectives and lax.ppermute only.
A program may use at most 128 MiB of HBM per device.

```python
import math
import jax
import jax.numpy as jnp
import numpy as np
from jax import lax

SEG = 8
BLOCK = 320
FIRST_LINES = 8
SECOND_LINES = 8
SPAN_ELEMENTS = 256


MIXING_SCALE = 0.0175


def draw_line_inverse(key, part):
    key = jax.random.fold_in(key, 11)
    diag_key, transport_key, rest_key = jax.random.split(key, 3)
    full_shape = (FIRST_LINES, SECOND_LINES, BLOCK, BLOCK)
    row_index = lax.broadcasted_iota(jnp.int32, (BLOCK, BLOCK), 0)
    col_index = lax.broadcasted_iota(jnp.int32, (BLOCK, BLOCK), 1)
    row_layer = row_index // 5 % 4
    col_layer = col_index // 5 % 4
    partner = row_index + (3 - 2 * row_layer) * 5
    transport_mask = col_index == partner
    diagonal_mask = col_index == row_index
    coupling_mask = jnp.logical_or(jnp.logical_and(row_layer == 3, col_layer == 0), jnp.logical_and(row_layer == 0, col_layer == 3))
    rest_weight = jnp.where(coupling_mask, 0.0005, 0.0028)
    diagonal = jax.random.uniform(diag_key, (FIRST_LINES, SECOND_LINES, BLOCK, 1), jnp.float32, 0.5, 1.0)
    transport = jax.random.uniform(transport_key, full_shape, jnp.float32, 0.995, 1.0)
    rest = jax.random.truncated_normal(rest_key, -4.0, 4.0, full_shape, jnp.float32)
    return jnp.where(diagonal_mask, diagonal, 0.0) + jnp.where(transport_mask, transport, 0.0) + rest_weight * rest


def draw_span_jacobian(key, part):
    key = jax.random.fold_in(key, 23)
    variant_key, gradual_mode_key, quick_mode_key, spike_key, line_depth_key, blend_key = jax.random.split(key, 6)
    full_shape = (FIRST_LINES, SECOND_LINES, SPAN_ELEMENTS, 2, 5, 5)
    rate_shape = (FIRST_LINES, SECOND_LINES, SPAN_ELEMENTS // SEG, 2, 5, 1)
    fast_share = 0.5
    slow_rate = jnp.exp(jax.random.uniform(gradual_mode_key, rate_shape, jnp.float32, math.log(0.015), math.log(0.035)))
    mixing = MIXING_SCALE * jax.random.truncated_normal(blend_key, -3.0, 3.0, full_shape, jnp.float32)
    is_fast = jax.random.uniform(variant_key, (FIRST_LINES, SECOND_LINES, 1, 2, 5, 1), jnp.float32) < fast_share
    slow_gain = 1.0 - jnp.repeat(slow_rate, SEG, axis=2)
    fast_gain = jax.random.uniform(quick_mode_key, (FIRST_LINES, SECOND_LINES, SPAN_ELEMENTS, 2, 5, 1), jnp.float32, 0.93, 0.95)
    gain = jnp.where(is_fast, fast_gain, slow_gain)
    decay_rate = jnp.sqrt((gain / 6.0) ** 2 - 4.0 * MIXING_SCALE * MIXING_SCALE)
    spike_fraction = min(0.15, 3.0 / SPAN_ELEMENTS)
    spike_amount = jax.random.uniform(spike_key, (FIRST_LINES, SECOND_LINES, SPAN_ELEMENTS, 2, 1, 1), jnp.float32) < spike_fraction
    line_depth = jax.random.uniform(line_depth_key, (FIRST_LINES, SECOND_LINES, SPAN_ELEMENTS, 2, 1, 1), jnp.float32, 0.5, 0.8)
    decay_rate = decay_rate * jnp.where(spike_amount, line_depth, 1.0)
    identity = jnp.eye(5, dtype=jnp.float32)
    return decay_rate * identity + mixing * (1.0 - identity)


def plant(entries, own_key, least, largest):
    longest = entries.shape.index(max(entries.shape))
    spots = []
    for shift in (0, 1):
        where = [jax.random.randint(jax.random.fold_in(own_key, axis), (), 0, length) for axis, length in enumerate(entries.shape)]
        where[longest] = (where[longest] + shift) % entries.shape[longest]
        spots.append(tuple(where))
    return entries.at[spots[0]].set(least).at[spots[1]].set(largest)


def steps_of(own_key, dims, cuts, smallest, top_value):
    level, own = 1.0, jax.random.fold_in(own_key, 6)
    for dim, parts in cuts:
        draws = jnp.exp(jax.random.uniform(jax.random.fold_in(own, dim), (parts,), jnp.float32, smallest / len(cuts), top_value / len(cuts)))
        level = level * jnp.repeat(draws, dims[dim] // parts).reshape([-1 if axis == dim else 1 for axis in range(len(dims))])
    return level


def noise(own_key, shape, deviation, reach, shards=(), held_as=jnp.bfloat16):
    level = steps_of(own_key, shape, shards, -0.22, 0.18) if shards else 1.0
    values = jax.random.normal(own_key, shape, jnp.float32) * deviation * level
    return jnp.minimum(jnp.maximum(values, -reach), reach).astype(held_as)


def setup_inputs(seed: int = 0) -> dict:
    seeds = jax.random.split(jax.random.key(seed), 10)
    return {
        "flow_state": noise(seeds[0], (FIRST_LINES, SECOND_LINES, SPAN_ELEMENTS, BLOCK), 1.0, 6.0, ((0, 2), (1, 4), (2, 32)), jnp.float32),
        "source_term": noise(seeds[1], (FIRST_LINES, SECOND_LINES, SPAN_ELEMENTS, BLOCK), 1.0, 6.0, ((0, 2), (1, 4), (2, 32)), jnp.float32),
        "pseudo_time": jnp.clip(jnp.exp(math.log(4.0) - 1.3862944 * jax.random.uniform(seeds[2], (FIRST_LINES, SECOND_LINES, SPAN_ELEMENTS, BLOCK), jnp.float32) ** steps_of(seeds[2], (FIRST_LINES, SECOND_LINES, SPAN_ELEMENTS, BLOCK), ((0, 2), (1, 4), (2, 32)), -0.2, 0.2)), 1.0, 4.0),
        "volume_jacobian": noise(seeds[3], (FIRST_LINES, SECOND_LINES, SPAN_ELEMENTS, 3, 5, 5), 0.3, 1.8, ((0, 2), (1, 4), (2, 32)), jnp.float32),
        "side_jacobian": noise(seeds[4], (FIRST_LINES, SECOND_LINES, SPAN_ELEMENTS, 4, 5, 5), 0.2, 1.2, ((0, 2), (1, 4), (2, 32)), jnp.float32),
        "span_jacobian": draw_span_jacobian(jax.random.fold_in(seeds[9], 71), 0),
        "line_inverse": draw_line_inverse(jax.random.fold_in(seeds[9], 71), 0),
        "mirror_face": plant(jax.random.randint(seeds[7], (FIRST_LINES, SECOND_LINES, SPAN_ELEMENTS, 4), 0, 2), jax.random.fold_in(seeds[7], 1), 0, 1).astype(jnp.int32),
        "edge_flip": plant(jax.random.randint(seeds[8], (FIRST_LINES, SECOND_LINES, SPAN_ELEMENTS, 4), 0, 2), jax.random.fold_in(seeds[8], 1), 0, 1).astype(jnp.int32),
    }


LIFT = 6.0
HIGHEST = lax.Precision.HIGHEST

def gll_derivative():
    points = np.array([-1.0, -1.0 / np.sqrt(5.0), 1.0 / np.sqrt(5.0), 1.0])
    matrix = np.zeros((4, 4))
    for target in range(4):
        for source in range(4):
            if target != source:
                numerator = 1.0
                for other_node in range(4):
                    if other_node != source and other_node != target:
                        numerator = numerator * (points[target] - points[other_node])
                denominator = 1.0
                for other_node in range(4):
                    if other_node != source:
                        denominator = denominator * (points[source] - points[other_node])
                matrix[target, source] = numerator / denominator
    for target in range(4):
        matrix[target, target] = -np.sum(matrix[target])
    return jnp.asarray(matrix, dtype=jnp.float32)

def split_nodes(field):
    return field.reshape(field.shape[:3] + (4, 4, 4, 5))

def side_traces(nodes):
    return jnp.stack([nodes[:, :, :, 0], nodes[:, :, :, 3], nodes[:, :, :, :, 0], nodes[:, :, :, :, 3]], axis=3)

def volume_term(nodes, volume_jacobian):
    derivative = gll_derivative()
    fluxes = jnp.einsum('xyzdwv,xyzabcv->xyzdabcw', volume_jacobian, nodes, precision=HIGHEST)
    along_first = jnp.einsum('pa,xyzabcw->xyzpbcw', derivative, fluxes[:, :, :, 0], precision=HIGHEST)
    along_second = jnp.einsum('pb,xyzabcw->xyzapcw', derivative, fluxes[:, :, :, 1], precision=HIGHEST)
    along_span = jnp.einsum('pc,xyzabcw->xyzabpw', derivative, fluxes[:, :, :, 2], precision=HIGHEST)
    return along_first + along_second + along_span

def face_coupling(own_sides, pairs, mirror_face, edge_flip, side_jacobian):
    lifted_faces = []
    for face_index in range(4):
        candidates = pairs[face_index]
        chosen = jnp.where(mirror_face[:, :, :, face_index, None, None, None] == 1, candidates[:, :, :, 1], candidates[:, :, :, 0])
        mirrored_edge = jnp.flip(chosen, axis=3)
        chosen = jnp.where(edge_flip[:, :, :, face_index, None, None, None] == 1, mirrored_edge, chosen)
        jump = chosen - own_sides[:, :, :, face_index]
        lifted_faces.append(LIFT * jnp.einsum('xyzwv,xyzecv->xyzecw', side_jacobian[:, :, :, face_index], jump, precision=HIGHEST))
    return lifted_faces

def apply_residual(nodes, source_term, pseudo_time, volume_jacobian, side_jacobian, span_jacobian, mirror_face, edge_flip, pairs, lower_top, upper_bottom):
    lifted_faces = face_coupling(side_traces(nodes), pairs, mirror_face, edge_flip, side_jacobian)
    bottom_layer = nodes[:, :, :, :, :, 0]
    top_layer = nodes[:, :, :, :, :, 3]
    lower_term = LIFT * jnp.einsum('xyzwv,xyzabv->xyzabw', span_jacobian[:, :, :, 0], lower_top - bottom_layer, precision=HIGHEST)
    upper_term = LIFT * jnp.einsum('xyzwv,xyzabv->xyzabw', span_jacobian[:, :, :, 1], upper_bottom - top_layer, precision=HIGHEST)
    lifted = jnp.zeros_like(nodes)
    lifted = lifted.at[:, :, :, 0].add(lifted_faces[0])
    lifted = lifted.at[:, :, :, 3].add(lifted_faces[1])
    lifted = lifted.at[:, :, :, :, 0].add(lifted_faces[2])
    lifted = lifted.at[:, :, :, :, 3].add(lifted_faces[3])
    lifted = lifted.at[:, :, :, :, :, 0].add(lower_term)
    lifted = lifted.at[:, :, :, :, :, 3].add(upper_term)
    operator_value = volume_term(nodes, volume_jacobian) - lifted
    field = nodes.reshape(source_term.shape)
    return source_term - (pseudo_time * field + operator_value.reshape(source_term.shape))

def place_layer(values, height):
    layer_grid = values.reshape(values.shape[0], 4, 4, 1, 5)
    empty_grid = jnp.zeros_like(layer_grid)
    pieces = [layer_grid if layer_index == height else empty_grid for layer_index in range(4)]
    return jnp.concatenate(pieces, axis=3).reshape(values.shape[0], 320)

def layer_trace(vector, height):
    return vector.reshape(vector.shape[0], 4, 4, 4, 5)[:, :, :, height].reshape(vector.shape[0], 80)

def couple(jacobian, trace_value):
    line_count = trace_value.shape[0]
    return LIFT * jnp.einsum('lwv,lpv->lpw', jacobian, trace_value.reshape(line_count, 16, 5), precision=HIGHEST).reshape(line_count, 80)

def reference(flow_state, source_term, pseudo_time, volume_jacobian, side_jacobian, span_jacobian, line_inverse, mirror_face, edge_flip):
    nodes = split_nodes(flow_state)
    all_sides = side_traces(nodes)
    padded = jnp.pad(all_sides, ((1, 1), (1, 1), (0, 0), (0, 0), (0, 0), (0, 0), (0, 0)))
    pairs = [padded[0:FIRST_LINES, 1:SECOND_LINES + 1, :, 0:2], padded[2:FIRST_LINES + 2, 1:SECOND_LINES + 1, :, 0:2], padded[1:FIRST_LINES + 1, 0:SECOND_LINES, :, 2:4], padded[1:FIRST_LINES + 1, 2:SECOND_LINES + 2, :, 2:4]]
    lower_top = jnp.roll(nodes[:, :, :, :, :, 3], 1, axis=2)
    upper_bottom = jnp.roll(nodes[:, :, :, :, :, 0], -1, axis=2)
    residual = apply_residual(nodes, source_term, pseudo_time, volume_jacobian, side_jacobian, span_jacobian, mirror_face, edge_flip, pairs, lower_top, upper_bottom)
    line_count = FIRST_LINES * SECOND_LINES
    lines = residual.reshape(line_count, SPAN_ELEMENTS, 320).transpose(1, 0, 2)
    inverse = line_inverse.reshape(line_count, 320, 320)
    lower_jac = span_jacobian[:, :, :, 0].reshape(line_count, SPAN_ELEMENTS, 5, 5).transpose(1, 0, 2, 3)
    upper_jac = span_jacobian[:, :, :, 1].reshape(line_count, SPAN_ELEMENTS, 5, 5).transpose(1, 0, 2, 3)

    def forward_step(running, inputs):
        residual_now, jacobian = inputs
        source = residual_now + place_layer(couple(jacobian, running), 0)
        solved = jnp.einsum('lij,lj->li', inverse, source, precision=HIGHEST)
        return (layer_trace(solved, 3), solved)
    zero_trace = jnp.zeros((line_count, 80), jnp.float32)
    forward_sweep = lax.scan(forward_step, zero_trace, (lines, lower_jac))[1]

    def backward_step(running, inputs):
        forward_now, jacobian = inputs
        solved = forward_now + jnp.einsum('lij,lj->li', inverse, place_layer(couple(jacobian, running), 3), precision=HIGHEST)
        return (layer_trace(solved, 0), solved)
    correction = lax.scan(backward_step, zero_trace, (forward_sweep, upper_jac), reverse=True)[1]
    updated_state = flow_state + correction.transpose(1, 0, 2).reshape(flow_state.shape)
    return (updated_state, residual)
```

```python
import functools

import jax
import jax.numpy as jnp
import numpy as np
from jax import lax
from jax.experimental import pallas as pl
from jax.experimental.pallas import tpu as pltpu
from jax.sharding import PartitionSpec as P

LIFT = 6.0
F32 = jnp.float32
BF16 = jnp.bfloat16
VMEM_LIMIT = 56 * 1024 * 1024
LINES = 8
SEG = 8


def derivative_matrix():
    points = np.array([-1.0, -1.0 / np.sqrt(5.0), 1.0 / np.sqrt(5.0), 1.0])
    matrix = np.zeros((4, 4))
    for target in range(4):
        for source in range(4):
            if target != source:
                numerator = 1.0
                denominator = 1.0
                for other in range(4):
                    if other != source and other != target:
                        numerator *= points[target] - points[other]
                    if other != source:
                        denominator *= points[source] - points[other]
                matrix[target, source] = numerator / denominator
    for target in range(4):
        matrix[target, target] = -np.sum(matrix[target])
    return matrix


def entry(a, b, c, v):
    return ((4 * a + b) * 4 + c) * 5 + v


@functools.cache
def constants():
    select = np.zeros((1120, 320), np.float32)
    place = np.zeros((320, 800), np.float32)
    layers = np.zeros((160, 320), np.float32)
    for v in range(5):
        for a in range(4):
            for b in range(4):
                for c in range(4):
                    row = v * 64 + a * 16 + b * 4 + c
                    select[row, entry(a, b, c, v)] = 1
                    place[entry(a, b, c, v), row] = 1
        for e in range(4):
            for c in range(4):
                row = v * 16 + e * 4 + c
                for side, plane in enumerate((0, 3)):
                    for flip in range(2):
                        along = 3 - e if flip else e
                        block = (side * 2 + flip) * 80
                        select[320 + block + row, entry(plane, along, c, v)] = 1
                        select[640 + block + row, entry(along, plane, c, v)] = 1
                    place[entry(plane, e, c, v), 320 + 80 * side + row] = -1
                    place[entry(e, plane, c, v), 480 + 80 * side + row] = -1
        for a in range(4):
            for b in range(4):
                row = v * 16 + a * 4 + b
                select[960 + row, entry(a, b, 3, v)] = 1
                select[1040 + row, entry(a, b, 0, v)] = 1
                place[entry(a, b, 0, v), 640 + row] = -1
                place[entry(a, b, 3, v), 720 + row] = -1
                layers[row, entry(a, b, 3, v)] = 1
                layers[80 + row, entry(a, b, 0, v)] = 1
    top, bottom = layers[:80].T, layers[80:].T
    columns_high = np.zeros((320, 512), np.float32)
    columns_low = np.zeros((320, 512), np.float32)
    for base, chosen in ((0, bottom), (256, top)):
        columns_high[:, base : base + 80] = chosen
        columns_high[:, base + 80 : base + 160] = chosen
        columns_low[:, base + 160 : base + 240] = chosen
    spread = np.concatenate([bottom, top], axis=1)
    eye, d = np.eye(4), derivative_matrix()
    along = np.concatenate(
        [
            np.kron(np.kron(d, eye), eye),
            np.kron(np.kron(eye, d), eye),
            np.kron(np.kron(eye, eye), d),
        ],
        axis=1,
    )
    high = along.astype(jnp.bfloat16).astype(np.float64)
    along = np.concatenate([high, high, along - high], axis=1)
    twice = np.concatenate([np.eye(64), np.eye(64)], axis=1)
    as_bf16 = lambda x: np.asarray(x, np.float32).astype(jnp.bfloat16)
    return {
        "select": as_bf16(select),
        "place": as_bf16(place),
        "layers": as_bf16(layers),
        "columns_high": as_bf16(columns_high),
        "columns_low": as_bf16(columns_low),
        "spread": as_bf16(spread),
        "along": as_bf16(along),
        "twice": as_bf16(twice),
        "eye": as_bf16(np.eye(320)),
    }


def dot(a, b):
    return lax.dot_general(a, b, (((1,), (0,)), ((), ())), preferred_element_type=F32)


def dot_nt(a, b):
    return lax.dot_general(a, b, (((1,), (1,)), ((), ())), preferred_element_type=F32)


def split(x):
    high = x.astype(BF16)
    return high, (x - high.astype(F32)).astype(BF16)


def split_3(x):
    high = x.astype(BF16)
    rest = x - high.astype(F32)
    middle = rest.astype(BF16)
    return high, middle, (rest - middle.astype(F32)).astype(BF16)


def lanes(shape):
    return lax.broadcasted_iota(jnp.int32, shape, len(shape) - 1)


def rows(shape):
    return lax.broadcasted_iota(jnp.int32, shape, len(shape) - 2)


def roll(x, amount):
    return pltpu.roll(x, amount % 128, 1)


def pair_lanes(x):
    high = x.astype(BF16).astype(F32)
    return jnp.where(lanes(x.shape) < 64, high, roll(x - high, 64)).astype(BF16)


def left_cat(x):
    high, low = split(x)
    return jnp.concatenate([high, high, low], axis=1)


def right_cat(x):
    high, low = split(x)
    return jnp.concatenate([high, low, high], axis=0)


def prepare_kernel(inverse, columns_high, columns_low, layers, high_out, low_out, fwd_out, bwd_out):
    for line in range(LINES):
        high, low = split(inverse[line])
        high_out[line] = high
        low_out[line] = low
        columns = dot(high, columns_high[...]) + dot(low, columns_low[...])
        chosen = dot(layers[...], columns.astype(BF16)).astype(BF16)
        fwd_out[line] = chosen[:, :256]
        bwd_out[line] = chosen[80:, 256:]


def mix(coefficient, slabs):
    out = []
    for w in range(5):
        total = coefficient(w, 0) * slabs[0]
        for v in range(1, 5):
            total = total + coefficient(w, v) * slabs[v]
        out.append(total)
    return out


def slabs_of(x, size):
    return [x[v * size : (v + 1) * size] for v in range(5)]


def sweep_kernel(
    flags,
    span_scalars,
    flow,
    gx_low,
    gx_high,
    gy_low,
    gy_high,
    below,
    above,
    source,
    pseudo,
    tables,
    inverse_high,
    inverse_low,
    fwd,
    bwd,
    select,
    place,
    layers,
    along,
    twice,
    eye,
    residual_out,
    turned_out,
    maps_out,
    z_high,
    z_low,
    v_high,
    v_low,
    extended,
    flux,
    started,
    t_state,
    w_state,
    bottoms,
):
    first_lo, first_hi = flags[0].astype(F32), flags[1].astype(F32)
    second_lo, second_hi = flags[2].astype(F32), flags[3].astype(F32)
    u = flow[...]
    extended[0:64] = u
    extended[64:80] = gx_high[...] * first_hi
    extended[80:112] = jnp.zeros((32, 320), F32)
    extended[112:128] = gx_low[...] * first_lo
    for i in range(4):
        extended[128 + 16 * i : 136 + 16 * i] = gy_low[8 * i : 8 * i + 8] * second_lo
        extended[136 + 16 * i : 144 + 16 * i] = gy_high[8 * i : 8 * i + 8] * second_hi
    position = rows((8, 320))
    for line in range(LINES):
        extended[192 + 8 * line : 200 + 8 * line] = jnp.where(
            position == 0,
            below[line : line + 1],
            jnp.where(position == 7, above[line : line + 1], 0.0),
        )
    parts = split_3(extended[...])
    chosen = sum(dot_nt(select[...], part) for part in parts)
    near, far = chosen[:, :128], chosen[:, 128:]
    lane = lanes((1, 128))
    table = lambda r: tables[r : r + 1, :]

    by_variable = slabs_of(near[0:320], 64)
    for d in range(3):
        mixed = mix(lambda w, v: table(d * 25 + w * 5 + v), by_variable)
        for w in range(5):
            flux[d * 64 : d * 64 + 64, w * 128 : w * 128 + 128] = mixed[w]
    volume = dot(along[...], right_cat(flux[...]))
    pieces = [volume[:, w * 128 : w * 128 + 128] for w in range(5)]

    for f in range(4):
        base = 320 + 320 * (f // 2)
        candidates = [near[base + 80 * n : base + 80 * n + 80] for n in range(4)]
        outer = [far[base + 80 * n : base + 80 * n + 80] for n in range(4)]
        own = candidates[2 * (f % 2)]
        if f == 0:
            shifted = [roll(x, 16) for x in candidates]
        elif f == 1:
            shifted = [roll(x, -16) for x in candidates]
        elif f == 2:
            shifted = [
                jnp.where((lane // 8) % 2 == 1, roll(x, 8), y) for x, y in zip(candidates, outer)
            ]
        else:
            shifted = [
                jnp.where((lane // 8) % 2 == 0, roll(x, -8), y) for x, y in zip(candidates, outer)
            ]
        mirrored = table(225 + f) > 0.5
        flipped = table(229 + f) > 0.5
        neighbour = jnp.where(
            flipped,
            jnp.where(mirrored, shifted[3], shifted[1]),
            jnp.where(mirrored, shifted[2], shifted[0]),
        )
        jump = LIFT * (neighbour - own)
        pieces += mix(lambda w, v: table(75 + f * 25 + w * 5 + v), slabs_of(jump, 16))

    top, bottom = near[960:1040], near[1040:1120]
    outer_top, outer_bottom = roll(far[960:1040], 64), roll(far[1040:1120], 64)
    lower_jump = LIFT * (jnp.where(lane % 8 == 0, outer_top, roll(top, 1)) - bottom)
    upper_jump = LIFT * (jnp.where(lane % 8 == 7, outer_bottom, roll(bottom, -1)) - top)
    pieces += mix(lambda w, v: table(175 + w * 5 + v), slabs_of(lower_jump, 16))
    pieces += mix(lambda w, v: table(200 + w * 5 + v), slabs_of(upper_jump, 16))
    stacked = jnp.concatenate(pieces, axis=0)
    operator = dot(place[...], pair_lanes(stacked))
    operator_high, operator_low = split(operator)
    operator_rows = dot_nt(twice[...], operator_high) + dot_nt(twice[...], operator_low)
    residual = source[...] - (pseudo[...] * u + operator_rows)
    residual_out[...] = residual

    high, low = split(residual)
    turned = dot_nt(eye[...], jnp.concatenate([high, low], axis=0))
    turned_out[...] = turned + roll(turned, 64)
    turned = turned.astype(BF16)
    wide_lane = lanes((320, 128)) % 64
    direct = jnp.zeros((320, 128), F32)
    for line in range(LINES):
        applied = dot(inverse_high[line], turned) + dot(inverse_low[line], turned)
        direct = jnp.where(wide_lane // 8 == line, applied, direct)
    direct = direct + roll(direct, 64)
    traces = dot(layers[...], pair_lanes(direct))
    traces = traces + roll(traces, 64)

    trace_lane = lanes((160, 128))
    small_lane, small_row = lanes((80, 128)), rows((80, 128))
    for line in range(LINES):
        moved = roll(traces, 80 - 8 * line)
        started[line] = jnp.where((trace_lane >= 80) & (trace_lane < 88), moved, 0.0)
        t_state[line] = jnp.where(small_lane == small_row, 1.0, 0.0)
        w_state[line] = jnp.where(lanes((80, 256)) == rows((80, 256)) + 88, 1.0, 0.0)

    def forward(k, carry):
        mine = small_lane == 80 + k
        for line in range(LINES):
            at = (line * SEG + k) * 50
            z = jnp.concatenate(
                mix(lambda w, v: span_scalars[at + w * 5 + v], slabs_of(t_state[line], 16)),
                axis=0,
            )
            z_hi, z_lo = split(z)
            z_high[line, k] = z_hi
            z_low[line, k] = z_lo
            y = dot(fwd[line, :, 0:240], jnp.concatenate([z_hi, z_lo, z_hi], axis=0))
            t_state[line] = y[:80] + jnp.where(mine, started[line, 0:80], 0.0)
            bottoms[line, k] = y[80:] + jnp.where(mine, started[line, 80:160], 0.0)
        return carry

    lax.fori_loop(0, SEG, forward, 0)

    def backward(step, carry):
        k = SEG - 1 - step
        for line in range(LINES):
            at = (line * SEG + k) * 50 + 25
            z = jnp.concatenate(
                mix(lambda w, v: span_scalars[at + w * 5 + v], slabs_of(w_state[line], 16)),
                axis=0,
            )
            z_hi, z_lo = split(z)
            v_high[line, k] = z_hi
            v_low[line, k] = z_lo
            y = dot(bwd[line, :, 0:240], jnp.concatenate([z_hi, z_lo, z_hi], axis=0))
            w_state[line, :, 0:128] = y[:, :128] + bottoms[line, k]
            w_state[line, :, 128:256] = y[:, 128:]
        return carry

    lax.fori_loop(0, SEG, backward, 0)
    for line in range(LINES):
        maps_out[line, :, 0:128] = w_state[line, :, 0:128]
        maps_out[line, :, 128:256] = w_state[line, :, 128:256] + roll(t_state[line], 40)


def compose_kernel(maps, t_out, w_out, whole_out):
    lane = lanes((80, 128))
    tall_lane, tall_row = lanes((128, 128)), rows((128, 128))
    zero = jnp.zeros((48, 128), F32)
    fixed = jnp.where((tall_row < 80) & (tall_lane == tall_row), 1.0, 0.0)
    ones = jnp.where((tall_row >= 80) & (tall_row < 88) & (tall_lane == 80), 1.0, 0.0)
    state = fixed + ones
    coupled = []
    for e in range(SEG):
        t_out[e] = state
        left, right = maps[e, :, 0:128], maps[e, :, 128:256]
        state_cat = right_cat(state)
        both = jnp.concatenate([jnp.where(lane < 88, roll(right, 88), 0.0), jnp.where(lane < 88, left, 0.0)], axis=0)
        y = dot(left_cat(both), state_cat)
        coupled.append(y[80:])
        state = jnp.concatenate([y[:80], ones[80:]], axis=0)
    last = state[:80]
    w0 = jnp.where(tall_lane == tall_row + 81, 1.0, 0.0)
    w1 = jnp.where((tall_lane == tall_row - 47) & (tall_row < 80), 1.0, 0.0)
    for e in range(SEG - 1, -1, -1):
        w_out[e, :, 0:128] = w0
        w_out[e, :, 128:256] = w1
        left, right = maps[e, :, 0:128], maps[e, :, 128:256]
        back = jnp.where(lane < 40, roll(left, 40), jnp.where(lane < 80, roll(right, 40), 0.0))
        back_cat = left_cat(back)
        y0 = dot(back_cat, right_cat(w0)) + coupled[e]
        y1 = dot(back_cat, right_cat(w1))
        w0 = jnp.concatenate([y0, zero], axis=0)
        w1 = jnp.concatenate([y1, zero], axis=0)
    second = w1[:80] + roll(last, 33)
    for copy in range(whole_out.shape[0]):
        whole_out[copy, :, 0:128] = w0[:80]
        whole_out[copy, :, 128:256] = second


def solve_kernel(flags, wholes, t_in, w_in, out):
    groups = wholes.shape[0]
    lane = lanes((80, 128))
    tall_row = rows((128, 128))
    one = jnp.where(tall_row == 80, 1.0, 0.0)
    zero = jnp.zeros((48, 128), F32)

    def pieces(group):
        left, right = wholes[group, :, 0:128], wholes[group, :, 128:256]
        forward = jnp.where(lane < 81, roll(right, -33), 0.0)
        cross = jnp.where(lane < 81, left, 0.0)
        back = jnp.where(lane < 47, roll(left, 47), jnp.where(lane < 80, roll(right, 47), 0.0))
        return forward, cross, back

    parts = [pieces(group) for group in range(groups)]
    traces = [one]
    for group in range(groups - 1):
        y = dot(left_cat(parts[group][0]), right_cat(traces[-1]))
        traces.append(jnp.concatenate([y, zero], axis=0) + one)
    backs = [jnp.zeros((128, 128), F32)]
    for group in range(groups - 1, 0, -1):
        y = dot(left_cat(parts[group][1]), right_cat(traces[group]))
        y = y + dot(left_cat(parts[group][2]), right_cat(backs[0]))
        backs.insert(0, jnp.concatenate([y, zero], axis=0))
    mine = flags[4]
    trace, back = traces[0], backs[0]
    for group in range(1, groups):
        trace = jnp.where(mine == group, traces[group], trace)
        back = jnp.where(mine == group, backs[group], back)
    trace_row = jnp.transpose(trace)[0:8]
    back_row = roll(jnp.transpose(back)[0:8], 81)
    line_lane = lanes((8, 128))
    y0 = jnp.where(line_lane < 81, trace_row, back_row)
    y1 = jnp.where(line_lane < 33, back_row, 0.0)
    trace_cat = left_cat(trace_row)
    y_cat = left_cat(jnp.concatenate([y0, y1], axis=1))
    for e in range(SEG):
        high, low = split(t_in[e])
        t_row = dot_nt(trace_cat, jnp.concatenate([high, low, high], axis=1))
        high, low = split(w_in[e])
        c_row = roll(dot_nt(y_cat, jnp.concatenate([high, low, high], axis=1)), 88)
        first = jnp.where(line_lane < 80, t_row, jnp.where(line_lane < 88, 1.0, c_row))
        second = jnp.where(line_lane < 40, c_row, 0.0)
        out[e : e + 1, 0:128] = first[0:1]
        out[e : e + 1, 128:256] = second[0:1]


def finish_kernel(
    incoming,
    z_high,
    z_low,
    v_high,
    v_low,
    turned,
    inverse_high,
    inverse_low,
    flow,
    spread,
    twice,
    out,
):
    y = incoming[...]
    y = jnp.broadcast_to(y[:, None, :], (8, 8, 256)).reshape(64, 256)
    high, low = split(y)
    y = jnp.concatenate([high, low], axis=0)
    small_lane = lanes((80, 128)) % 64
    lower = jnp.zeros((80, 128), F32)
    upper = jnp.zeros((80, 128), F32)
    for line in range(LINES):
        z_hi, z_lo = z_high[line].reshape(640, 128), z_low[line].reshape(640, 128)
        v_hi, v_lo = v_high[line].reshape(640, 256), v_low[line].reshape(640, 256)
        c = dot_nt(z_hi, y[:, :128]) + dot_nt(z_lo, y[:, :128])
        d = dot_nt(v_hi, y) + dot_nt(v_lo, y)
        for k in range(SEG):
            mine = small_lane == line * SEG + k
            lower = jnp.where(mine, c[80 * k : 80 * k + 80], lower)
            upper = jnp.where(mine, d[80 * k : 80 * k + 80], upper)
    both = jnp.concatenate([lower, upper], axis=0)
    both = both + roll(both, 64)
    added = dot(spread[...], pair_lanes(both))
    load = pair_lanes(turned[...] + added + roll(added, 64))
    wide_lane = lanes((320, 128)) % 64
    total = jnp.zeros((320, 128), F32)
    for line in range(LINES):
        applied = dot(inverse_high[line], load) + dot(inverse_low[line], load)
        total = jnp.where(wide_lane // 8 == line, applied, total)
    high, low = split(total)
    out[...] = flow[...] + dot_nt(twice[...], high) + dot_nt(twice[...], low)


def call(kernel, out_shape, in_specs, scratch=(), flops=0, moved=0, name=None):
    return pl.pallas_call(
        kernel,
        out_shape=out_shape,
        in_specs=in_specs,
        out_specs=jax.tree.map(lambda _: pl.BlockSpec(memory_space=pltpu.VMEM), out_shape),
        scratch_shapes=list(scratch),
        compiler_params=pltpu.CompilerParams(vmem_limit_bytes=VMEM_LIMIT),
        cost_estimate=pl.CostEstimate(flops=flops, bytes_accessed=moved, transcendentals=0),
        name=name,
    )


VM = pl.BlockSpec(memory_space=pltpu.VMEM)
SM = pl.BlockSpec(memory_space=pltpu.SMEM)


def shape(*dims, dtype=F32):
    return jax.ShapeDtypeStruct(dims, dtype)


def on_device(
    flow_state,
    source_term,
    pseudo_time,
    volume_jacobian,
    side_jacobian,
    span_jacobian,
    line_inverse,
    mirror_face,
    edge_flip,
):
    const = {name: jnp.asarray(value) for name, value in constants().items()}
    span_size, gx_size, gy_size = (lax.axis_size(a) for a in ("span", "gx", "gy"))
    groups = span_size // SEG
    span_at, gx_at, gy_at = (lax.axis_index(a) for a in ("span", "gx", "gy"))
    flags = jnp.stack(
        [
            (gx_at > 0).astype(jnp.int32),
            (gx_at < gx_size - 1).astype(jnp.int32),
            (gy_at > 0).astype(jnp.int32),
            (gy_at < gy_size - 1).astype(jnp.int32),
            (span_at // SEG).astype(jnp.int32),
        ]
    )

    def ring(value, axis, step):
        count = lax.axis_size(axis)
        return lax.ppermute(value, axis, [(i, (i + step) % count) for i in range(count)])

    with jax.named_scope("halo"):
        gx_high = ring(flow_state[0], "gx", -1).reshape(16, 320)
        gx_low = ring(flow_state[3], "gx", 1).reshape(16, 320)
        gy_low = ring(flow_state[:, 1], "gy", 1).reshape(32, 320)
        gy_high = ring(flow_state[:, 0], "gy", -1).reshape(32, 320)
        below = ring(flow_state[:, :, SEG - 1], "span", 1).reshape(8, 320)
        above = ring(flow_state[:, :, 0], "span", -1).reshape(8, 320)

    with jax.named_scope("tables"):
        turn = lambda x: jnp.moveaxis(x.reshape(64, -1), 0, 1).astype(F32)
        tables = jnp.concatenate(
            [
                turn(x)
                for x in (volume_jacobian, side_jacobian, span_jacobian, mirror_face, edge_flip)
            ],
            axis=0,
        )
        tables = jnp.pad(tables, ((0, 0), (0, 64)))
        span_scalars = (LIFT * span_jacobian).reshape(3200)

    flow = flow_state.reshape(64, 320)
    inverse = line_inverse.reshape(LINES, 320, 320)
    inverse_high, inverse_low, fwd, bwd = call(
        prepare_kernel,
        (
            shape(LINES, 320, 320, dtype=BF16),
            shape(LINES, 320, 320, dtype=BF16),
            shape(LINES, 160, 256, dtype=BF16),
            shape(LINES, 80, 256, dtype=BF16),
        ),
        [VM] * 4,
        flops=4_000_000_000,
        moved=8_000_000,
        name="prepare",
    )(inverse, const["columns_high"], const["columns_low"], const["layers"])

    residual, turned, maps, z_high, z_low, v_high, v_low = call(
        sweep_kernel,
        (
            shape(64, 320),
            shape(320, 128),
            shape(LINES, 80, 256),
            shape(LINES, SEG, 80, 128, dtype=BF16),
            shape(LINES, SEG, 80, 128, dtype=BF16),
            shape(LINES, SEG, 80, 256, dtype=BF16),
            shape(LINES, SEG, 80, 256, dtype=BF16),
        ),
        [SM, SM] + [VM] * 20,
        scratch=[
            pltpu.VMEM((256, 320), F32),
            pltpu.VMEM((192, 640), F32),
            pltpu.VMEM((LINES, 160, 128), F32),
            pltpu.VMEM((LINES, 80, 128), F32),
            pltpu.VMEM((LINES, 80, 256), F32),
            pltpu.VMEM((LINES, SEG, 80, 128), F32),
        ],
        flops=10_000_000_000,
        moved=20_000_000,
        name="sweep",
    )(
        flags,
        span_scalars,
        flow,
        gx_low,
        gx_high,
        gy_low,
        gy_high,
        below,
        above,
        source_term.reshape(64, 320),
        pseudo_time.reshape(64, 320),
        tables,
        inverse_high,
        inverse_low,
        fwd,
        bwd,
        const["select"],
        const["place"],
        const["layers"],
        const["along"],
        const["twice"],
        const["eye"],
    )

    within = [[SEG * g + m for m in range(SEG)] for g in range(groups)]
    across = [[SEG * g + m for g in range(groups)] for m in range(SEG)]

    def exchange(value, members):
        return lax.all_to_all(value, "span", 0, 0, axis_index_groups=members, tiled=True)

    maps = exchange(maps, within)
    t_maps, w_maps, whole = call(
        compose_kernel,
        (shape(SEG, 128, 128), shape(SEG, 128, 256), shape(groups, 80, 256)),
        [VM],
        name="compose",
    )(maps)
    wholes = exchange(whole, across)
    answers = call(solve_kernel, shape(SEG, 256), [SM] + [VM] * 3, name="solve")(
        flags, wholes, t_maps, w_maps
    )
    incoming = exchange(answers, within)
    updated = call(finish_kernel, shape(64, 320), [VM] * 11, name="finish")(
        incoming,
        z_high,
        z_low,
        v_high,
        v_low,
        turned,
        inverse_high,
        inverse_low,
        flow,
        const["spread"],
        const["twice"],
    )
    return updated.reshape(flow_state.shape), residual.reshape(flow_state.shape)


def solution(mesh):
    lines = P("gx", "gy", "span", None)
    blocks = P("gx", "gy", "span", None, None, None)
    return jax.shard_map(
        on_device,
        mesh=mesh,
        in_specs=(lines, lines, lines, blocks, blocks, blocks, P("gx", "gy", None, None), lines, lines),
        out_specs=(lines, lines),
        check_vma=False,
    )
```

```python
import functools

import jax
import jax.numpy as jnp
import numpy as np
from jax import lax
from jax.experimental import pallas as pl
from jax.experimental.pallas import tpu as pltpu
from jax.sharding import PartitionSpec as P

LIFT = 6.0
F32 = jnp.float32
BF16 = jnp.bfloat16
LINES = 8
SEG = 8


def derivative_matrix():
    points = np.array([-1.0, -1.0 / np.sqrt(5.0), 1.0 / np.sqrt(5.0), 1.0])
    matrix = np.zeros((4, 4))
    for target in range(4):
        for source in range(4):
            if target != source:
                numerator = 1.0
                denominator = 1.0
                for other in range(4):
                    if other != source and other != target:
                        numerator *= points[target] - points[other]
                    if other != source:
                        denominator *= points[source] - points[other]
                matrix[target, source] = numerator / denominator
    for target in range(4):
        matrix[target, target] = -np.sum(matrix[target])
    return matrix


def entry(a, b, c, v):
    return ((4 * a + b) * 4 + c) * 5 + v


@functools.cache
def constants():
    select = np.zeros((1120, 320), np.float32)
    place = np.zeros((320, 800), np.float32)
    layers = np.zeros((160, 320), np.float32)
    for v in range(5):
        for a in range(4):
            for b in range(4):
                for c in range(4):
                    row = v * 64 + a * 16 + b * 4 + c
                    select[row, entry(a, b, c, v)] = 1
                    place[entry(a, b, c, v), row] = 1
        for e in range(4):
            for c in range(4):
                row = v * 16 + e * 4 + c
                for side, plane in enumerate((0, 3)):
                    for flip in range(2):
                        along = 3 - e if flip else e
                        block = (side * 2 + flip) * 80
                        select[320 + block + row, entry(plane, along, c, v)] = 1
                        select[640 + block + row, entry(along, plane, c, v)] = 1
                    place[entry(plane, e, c, v), 320 + 80 * side + row] = -1
                    place[entry(e, plane, c, v), 480 + 80 * side + row] = -1
        for a in range(4):
            for b in range(4):
                row = v * 16 + a * 4 + b
                select[960 + row, entry(a, b, 3, v)] = 1
                select[1040 + row, entry(a, b, 0, v)] = 1
                place[entry(a, b, 0, v), 640 + row] = -1
                place[entry(a, b, 3, v), 720 + row] = -1
                layers[row, entry(a, b, 3, v)] = 1
                layers[80 + row, entry(a, b, 0, v)] = 1
    top, bottom = layers[:80].T, layers[80:].T
    columns_high = np.zeros((320, 512), np.float32)
    columns_low = np.zeros((320, 512), np.float32)
    for base, chosen in ((0, bottom), (256, top)):
        columns_high[:, base : base + 80] = chosen
        columns_high[:, base + 80 : base + 160] = chosen
        columns_low[:, base + 160 : base + 240] = chosen
    spread = np.concatenate([bottom, top], axis=1)
    eye, d = np.eye(4), derivative_matrix()
    along = np.concatenate(
        [
            np.kron(np.kron(d, eye), eye),
            np.kron(np.kron(eye, d), eye),
            np.kron(np.kron(eye, eye), d),
        ],
        axis=1,
    )
    high = along.astype(jnp.bfloat16).astype(np.float64)
    along = np.concatenate([high, high, along - high], axis=1)
    twice = np.concatenate([np.eye(64), np.eye(64)], axis=1)
    eye_320 = np.eye(320)
    blocks = [
        select,
        place[:, :320],
        place[:, 320:640],
        place[:, 640:],
        along[:, :192],
        along[:, 384:],
        twice,
        eye_320,
        spread,
    ]
    fixed = np.zeros((sum(len(block) for block in blocks), 320), np.float32)
    at = 0
    for block in blocks:
        fixed[at : at + len(block), : block.shape[1]] = block
        at += len(block)
    early = np.zeros((800, 512), np.float32)
    early[:320], early[320:640], early[640:, :320] = columns_high, columns_low, layers
    return early.astype(jnp.bfloat16), fixed.astype(jnp.bfloat16)


SELECT, PLACE_A, PLACE_B, PLACE_C = slice(0, 1120), slice(1120, 1440), slice(1440, 1760), slice(1760, 2080)
ALONG_HIGH, ALONG_LOW, TWICE = slice(2080, 2144), slice(2144, 2208), slice(2208, 2272)
EYE, SPREAD = slice(2272, 2592), slice(2592, 2912)
SIDE, SPAN, MIRROR, FLIP = 80, 184, 240, 244


def dot(a, b):
    return lax.dot_general(a, b, (((1,), (0,)), ((), ())), preferred_element_type=F32)


def dot_nt(a, b):
    return lax.dot_general(a, b, (((1,), (1,)), ((), ())), preferred_element_type=F32)


def split(x):
    high = x.astype(BF16)
    return high, (x - high.astype(F32)).astype(BF16)


def split_3(x):
    high = x.astype(BF16)
    rest = x - high.astype(F32)
    middle = rest.astype(BF16)
    return high, middle, (rest - middle.astype(F32)).astype(BF16)


def lanes(shape):
    return lax.broadcasted_iota(jnp.int32, shape, len(shape) - 1)


def rows(shape):
    return lax.broadcasted_iota(jnp.int32, shape, len(shape) - 2)


def roll(x, amount):
    return pltpu.roll(x, amount % 128, 1)


def pair_lanes(x):
    high = x.astype(BF16).astype(F32)
    return jnp.where(lanes(x.shape) < 64, high, roll(x - high, 64)).astype(BF16)


def left_cat(x):
    high, low = split(x)
    return jnp.concatenate([high, high, low], axis=1)


def right_cat(x):
    high, low = split(x)
    return jnp.concatenate([high, low, high], axis=0)


def pack_kernel(flow, plane_out, up_out, down_out, last_out, first_out):
    at = pl.multiple_of((1 - lax.axis_index("gx")) * 48, 16)
    plane_out[...] = flow[pl.ds(at, 16)]
    for i in range(4):
        down_out[8 * i : 8 * i + 8] = flow[16 * i : 16 * i + 8]
        up_out[8 * i : 8 * i + 8] = flow[16 * i + 8 : 16 * i + 16]
    for line in range(LINES):
        first_out[line : line + 1] = flow[8 * line : 8 * line + 1]
        last_out[line : line + 1] = flow[8 * line + 7 : 8 * line + 8]


def prepare_kernel(
    inverse,
    early,
    volume_jacobian,
    side_jacobian,
    span_jacobian,
    mirror_face,
    edge_flip,
    high_out,
    low_out,
    rows_high,
    rows_low,
    fwd_out,
    bwd_out,
    tables,
    wide,
    held,
    arrived,
):
    copies = [
        pltpu.make_async_copy(inverse.at[line], held.at[line], arrived.at[line])
        for line in range(LINES)
    ]
    for copy in copies:
        copy.start()
    for line in range(LINES):
        here = slice(8 * line, 8 * line + 8)
        tables[0:75, here] = volume_jacobian[line // 2, :, line % 2, :]
        tables[SIDE : SIDE + 100, here] = side_jacobian[line].reshape(100, 8)
        span = LIFT * span_jacobian[line].reshape(50, 8)
        tables[SPAN : SPAN + 50, here] = span
        tables[MIRROR : MIRROR + 4, here] = mirror_face[line].astype(F32)
        tables[FLIP : FLIP + 4, here] = edge_flip[line].astype(F32)
        for k in range(SEG):
            wide[line, k] = jnp.broadcast_to(span[:, k : k + 1], (50, 128))
    for line in range(LINES):
        copies[line].wait()
        high, low = split(held[line])
        high_out[line] = high
        low_out[line] = low
        layers = early[640:800, 0:320]
        chosen_high = dot(layers, high).astype(BF16)
        chosen_low = dot(layers, low).astype(BF16)
        rows_high[line] = chosen_high
        rows_low[line] = chosen_low
        both = (dot(chosen_high, early[0:320]) + dot(chosen_low, early[320:640])).astype(BF16)
        fwd_out[line] = both[:, :256]
        bwd_out[line] = both[80:, 256:]


def mix(coefficient, slabs):
    out = []
    for w in range(5):
        total = coefficient(w, 0) * slabs[0]
        for v in range(1, 5):
            total = total + coefficient(w, v) * slabs[v]
        out.append(total)
    return out


def slabs_of(x, size):
    return [x[v * size : (v + 1) * size] for v in range(5)]


def sweep_kernel(
    flow,
    plane,
    gy_low,
    gy_high,
    below,
    above,
    source,
    pseudo,
    tables,
    wide,
    rows_high,
    rows_low,
    fwd,
    bwd,
    fixed,
    residual_out,
    turned_out,
    maps_out,
    z_high,
    z_low,
    v_high,
    v_low,
    extended,
    flux,
    started,
    t_state,
    w_state,
    bottoms,
):
    gx_at, gy_at = lax.axis_index("gx"), lax.axis_index("gy")
    first_lo = (gx_at > 0).astype(F32)
    second_lo = (gy_at > 0).astype(F32)
    second_hi = (gy_at < lax.axis_size("gy") - 1).astype(F32)
    u = flow[...]
    extended[0:64] = u
    extended[64:80] = plane[...] * (1.0 - first_lo)
    extended[80:112] = jnp.zeros((32, 320), F32)
    extended[112:128] = plane[...] * first_lo
    for i in range(4):
        extended[128 + 16 * i : 136 + 16 * i] = gy_low[8 * i : 8 * i + 8] * second_lo
        extended[136 + 16 * i : 144 + 16 * i] = gy_high[8 * i : 8 * i + 8] * second_hi
    position = rows((8, 320))
    for line in range(LINES):
        extended[192 + 8 * line : 200 + 8 * line] = jnp.where(
            position == 0,
            below[line : line + 1],
            jnp.where(position == 7, above[line : line + 1], 0.0),
        )
    chosen = sum(dot_nt(fixed[SELECT], part) for part in split(extended[...]))
    near, far = chosen[:, :128], chosen[:, 128:]
    lane = lanes((1, 128))
    table = lambda r: tables[r : r + 1, :]

    by_variable = slabs_of(near[0:320], 64)
    for d in range(3):
        mixed = mix(lambda w, v: table(d * 25 + w * 5 + v), by_variable)
        for w in range(5):
            flux[d * 64 : d * 64 + 64, w * 128 : w * 128 + 128] = mixed[w]
    flux_high, flux_low = split(flux[...])
    volume = dot(fixed[ALONG_HIGH, 0:192], flux_high) + dot(fixed[ALONG_HIGH, 0:192], flux_low)
    volume = volume + dot(fixed[ALONG_LOW, 0:192], flux_high)
    pieces = [volume[:, w * 128 : w * 128 + 128] for w in range(5)]

    for f in range(4):
        base = 320 + 320 * (f // 2)
        candidates = [near[base + 80 * n : base + 80 * n + 80] for n in range(4)]
        outer = [far[base + 80 * n : base + 80 * n + 80] for n in range(4)]
        own = candidates[2 * (f % 2)]
        if f == 0:
            shifted = [roll(x, 16) for x in candidates]
        elif f == 1:
            shifted = [roll(x, -16) for x in candidates]
        elif f == 2:
            shifted = [
                jnp.where((lane // 8) % 2 == 1, roll(x, 8), y) for x, y in zip(candidates, outer)
            ]
        else:
            shifted = [
                jnp.where((lane // 8) % 2 == 0, roll(x, -8), y) for x, y in zip(candidates, outer)
            ]
        mirrored = table(MIRROR + f) > 0.5
        flipped = table(FLIP + f) > 0.5
        neighbour = jnp.where(
            flipped,
            jnp.where(mirrored, shifted[3], shifted[1]),
            jnp.where(mirrored, shifted[2], shifted[0]),
        )
        jump = LIFT * (neighbour - own)
        pieces += mix(lambda w, v: table(SIDE + (w * 5 + v) * 4 + f), slabs_of(jump, 16))

    top, bottom = near[960:1040], near[1040:1120]
    outer_top, outer_bottom = roll(far[960:1040], 64), roll(far[1040:1120], 64)
    lower_jump = jnp.where(lane % 8 == 0, outer_top, roll(top, 1)) - bottom
    upper_jump = jnp.where(lane % 8 == 7, outer_bottom, roll(bottom, -1)) - top
    pieces += mix(lambda w, v: table(SPAN + (w * 5 + v) * 2), slabs_of(lower_jump, 16))
    pieces += mix(lambda w, v: table(SPAN + (w * 5 + v) * 2 + 1), slabs_of(upper_jump, 16))
    pieces = [
        pair_lanes(jnp.concatenate(group, axis=0)) for group in (pieces[:5], pieces[5:25], pieces[25:])
    ]
    operator = dot(fixed[PLACE_A], pieces[0]) + dot(fixed[PLACE_B], pieces[1])
    operator = operator + dot(fixed[PLACE_C, 0:160], pieces[2])
    operator_high, operator_low = split(operator)
    twice = fixed[TWICE, 0:128]
    operator_rows = dot_nt(twice, operator_high) + dot_nt(twice, operator_low)
    residual = source[...] - (pseudo[...] * u + operator_rows)
    residual_out[...] = residual

    high, low = split(residual)
    turned = dot_nt(fixed[EYE], jnp.concatenate([high, low], axis=0))
    turned_out[...] = turned + roll(turned, 64)
    turned = turned.astype(BF16)
    trace_lane = lanes((160, 128))
    traces = jnp.zeros((160, 128), F32)
    for line in range(LINES):
        applied = dot(rows_high[line], turned) + dot(rows_low[line], turned)
        traces = jnp.where(trace_lane % 64 // 8 == line, applied, traces)
    traces = traces + roll(traces, 64)

    small_lane, small_row = lanes((80, 128)), rows((80, 128))
    for line in range(LINES):
        moved = roll(traces, 80 - 8 * line)
        started[line] = jnp.where((trace_lane >= 80) & (trace_lane < 88), moved, 0.0)
        t_state[line] = jnp.where(small_lane == small_row, 1.0, 0.0)
        w_state[line] = jnp.where(lanes((80, 256)) == rows((80, 256)) + 88, 1.0, 0.0)

    def forward(k, carry):
        mine = small_lane == 80 + k
        for line in range(LINES):
            z = jnp.concatenate(
                mix(lambda w, v: wide[line, k, pl.ds((w * 5 + v) * 2, 1)], slabs_of(t_state[line], 16)),
                axis=0,
            )
            z_hi, z_lo = split(z)
            z_high[line, k] = z_hi
            z_low[line, k] = z_lo
            y = dot(fwd[line, :, 0:240], jnp.concatenate([z_hi, z_lo, z_hi], axis=0))
            t_state[line] = y[:80] + jnp.where(mine, started[line, 0:80], 0.0)
            bottoms[line, k] = y[80:] + jnp.where(mine, started[line, 80:160], 0.0)
        return carry

    lax.fori_loop(0, SEG, forward, 0)

    def backward(step, carry):
        k = SEG - 1 - step
        for line in range(LINES):
            z = jnp.concatenate(
                [
                    jnp.concatenate(
                        mix(
                            lambda w, v: wide[line, k, pl.ds((w * 5 + v) * 2 + 1, 1)],
                            slabs_of(w_state[line, :, half], 16),
                        ),
                        axis=0,
                    )
                    for half in (slice(0, 128), slice(128, 256))
                ],
                axis=1,
            )
            z_hi, z_lo = split(z)
            v_high[line, k] = z_hi
            v_low[line, k] = z_lo
            y = dot(bwd[line, :, 0:240], jnp.concatenate([z_hi, z_lo, z_hi], axis=0))
            w_state[line, :, 0:128] = y[:, :128] + bottoms[line, k]
            w_state[line, :, 128:256] = y[:, 128:]
        return carry

    lax.fori_loop(0, SEG, backward, 0)
    for line in range(LINES):
        maps_out[line, :, 0:128] = w_state[line, :, 0:128]
        maps_out[line, :, 128:256] = w_state[line, :, 128:256] + roll(t_state[line], 40)


def compose_kernel(maps, t_out, w_out, whole_out):
    lane = lanes((80, 128))
    tall_lane, tall_row = lanes((128, 128)), rows((128, 128))
    zero = jnp.zeros((48, 128), F32)
    fixed = jnp.where((tall_row < 80) & (tall_lane == tall_row), 1.0, 0.0)
    ones = jnp.where((tall_row >= 80) & (tall_row < 88) & (tall_lane == 80), 1.0, 0.0)
    state = fixed + ones
    coupled = []
    for e in range(SEG):
        t_out[e] = state
        left, right = maps[e, :, 0:128], maps[e, :, 128:256]
        state_cat = right_cat(state)
        both = jnp.concatenate([jnp.where(lane < 88, roll(right, 88), 0.0), jnp.where(lane < 88, left, 0.0)], axis=0)
        y = dot(left_cat(both), state_cat)
        coupled.append(y[80:])
        state = jnp.concatenate([y[:80], ones[80:]], axis=0)
    last = state[:80]
    w0 = jnp.where(tall_lane == tall_row + 81, 1.0, 0.0)
    w1 = jnp.where((tall_lane == tall_row - 47) & (tall_row < 80), 1.0, 0.0)
    for e in range(SEG - 1, -1, -1):
        w_out[e, :, 0:128] = w0
        w_out[e, :, 128:256] = w1
        left, right = maps[e, :, 0:128], maps[e, :, 128:256]
        back = jnp.where(lane < 40, roll(left, 40), jnp.where(lane < 80, roll(right, 40), 0.0))
        back_cat = left_cat(back)
        y0 = dot(back_cat, right_cat(w0)) + coupled[e]
        y1 = dot(back_cat, right_cat(w1))
        w0 = jnp.concatenate([y0, zero], axis=0)
        w1 = jnp.concatenate([y1, zero], axis=0)
    second = w1[:80] + roll(last, 33)
    whole_out[:, 0:128] = w0[:80]
    whole_out[:, 128:256] = second


def solve_kernel(*refs):
    *parts, t_in, w_in, out, wholes = refs
    groups = len(parts)
    mine = lax.axis_index("span") // SEG
    for distance, part in enumerate(parts):
        wholes[lax.rem(mine - distance + groups, groups)] = part[...]
    lane = lanes((80, 128))
    tall_row = rows((128, 128))
    one = jnp.where(tall_row == 80, 1.0, 0.0)
    zero = jnp.zeros((48, 128), F32)

    def pieces(group):
        left, right = wholes[group, :, 0:128], wholes[group, :, 128:256]
        forward = jnp.where(lane < 81, roll(right, -33), 0.0)
        cross = jnp.where(lane < 81, left, 0.0)
        back = jnp.where(lane < 47, roll(left, 47), jnp.where(lane < 80, roll(right, 47), 0.0))
        return forward, cross, back

    parts = [pieces(group) for group in range(groups)]
    traces = [one]
    for group in range(groups - 1):
        y = dot(left_cat(parts[group][0]), right_cat(traces[-1]))
        traces.append(jnp.concatenate([y, zero], axis=0) + one)
    backs = [jnp.zeros((128, 128), F32)]
    for group in range(groups - 1, 0, -1):
        y = dot(left_cat(parts[group][1]), right_cat(traces[group]))
        y = y + dot(left_cat(parts[group][2]), right_cat(backs[0]))
        backs.insert(0, jnp.concatenate([y, zero], axis=0))
    trace, back = traces[0], backs[0]
    for group in range(1, groups):
        trace = jnp.where(mine == group, traces[group], trace)
        back = jnp.where(mine == group, backs[group], back)
    trace_row = jnp.transpose(trace)[0:8]
    back_row = roll(jnp.transpose(back)[0:8], 81)
    line_lane = lanes((8, 128))
    y0 = jnp.where(line_lane < 81, trace_row, back_row)
    y1 = jnp.where(line_lane < 33, back_row, 0.0)
    trace_cat = left_cat(trace_row)
    y_cat = left_cat(jnp.concatenate([y0, y1], axis=1))
    for e in range(SEG):
        high, low = split(t_in[e])
        t_row = dot_nt(trace_cat, jnp.concatenate([high, low, high], axis=1))
        high, low = split(w_in[e])
        c_row = roll(dot_nt(y_cat, jnp.concatenate([high, low, high], axis=1)), 88)
        first = jnp.where(line_lane < 80, t_row, jnp.where(line_lane < 88, 1.0, c_row))
        second = jnp.where(line_lane < 40, c_row, 0.0)
        out[e, :, 0:128] = first
        out[e, :, 128:256] = second


def finish_kernel(
    incoming,
    z_high,
    z_low,
    v_high,
    v_low,
    turned,
    inverse_high,
    inverse_low,
    flow,
    fixed,
    out,
):
    high, low = split(incoming[...].reshape(64, 256))
    y = jnp.concatenate([high, low], axis=0)
    small_lane = lanes((80, 128)) % 64
    lower = jnp.zeros((80, 128), F32)
    upper = jnp.zeros((80, 128), F32)
    for line in range(LINES):
        z_hi, z_lo = z_high[line].reshape(640, 128), z_low[line].reshape(640, 128)
        v_hi, v_lo = v_high[line].reshape(640, 256), v_low[line].reshape(640, 256)
        c = dot_nt(z_hi, y[:, :128]) + dot_nt(z_lo, y[:, :128])
        d = dot_nt(v_hi, y) + dot_nt(v_lo, y)
        for k in range(SEG):
            mine = small_lane == line * SEG + k
            lower = jnp.where(mine, c[80 * k : 80 * k + 80], lower)
            upper = jnp.where(mine, d[80 * k : 80 * k + 80], upper)
    both = jnp.concatenate([lower, upper], axis=0)
    both = both + roll(both, 64)
    added = dot(fixed[SPREAD, 0:160], pair_lanes(both))
    load = pair_lanes(turned[...] + added + roll(added, 64))
    wide_lane = lanes((320, 128)) % 64
    total = jnp.zeros((320, 128), F32)
    for line in range(LINES):
        applied = dot(inverse_high[line], load) + dot(inverse_low[line], load)
        total = jnp.where(wide_lane // 8 == line, applied, total)
    high, low = split(total)
    twice = fixed[TWICE, 0:128]
    out[...] = flow[...] + dot_nt(twice, high) + dot_nt(twice, low)


def call(kernel, out_shape, in_specs, scratch=(), limit=16, flops=0, moved=0, name=None):
    return pl.pallas_call(
        kernel,
        out_shape=out_shape,
        in_specs=in_specs,
        out_specs=jax.tree.map(lambda _: pl.BlockSpec(memory_space=pltpu.VMEM), out_shape),
        scratch_shapes=list(scratch),
        compiler_params=pltpu.CompilerParams(vmem_limit_bytes=limit * 1024 * 1024),
        cost_estimate=pl.CostEstimate(flops=flops, bytes_accessed=moved, transcendentals=0),
        name=name,
    )


VM = pl.BlockSpec(memory_space=pltpu.VMEM)
HBM = pl.BlockSpec(memory_space=pl.ANY)


def shape(*dims, dtype=F32):
    return jax.ShapeDtypeStruct(dims, dtype)


def on_device(
    flow_state,
    source_term,
    pseudo_time,
    volume_jacobian,
    side_jacobian,
    span_jacobian,
    line_inverse,
    mirror_face,
    edge_flip,
):
    early, fixed = (jnp.asarray(value) for value in constants())
    groups = lax.axis_size("span") // SEG

    def ring(value, axis, step):
        count = lax.axis_size(axis)
        return lax.ppermute(value, axis, [(i, (i + step) % count) for i in range(count)])

    flow = flow_state.reshape(64, 320)
    plane, up, down, last, first = call(
        pack_kernel,
        (shape(16, 320), shape(32, 320), shape(32, 320), shape(8, 320), shape(8, 320)),
        [VM],
        limit=4,
        name="pack",
    )(flow)
    with jax.named_scope("halo"):
        below, above = ring(last, "span", 1), ring(first, "span", -1)
        gy_low, gy_high = ring(up, "gy", 1), ring(down, "gy", -1)
        plane = ring(plane, "gx", 1)

    inverse = line_inverse.reshape(LINES, 320, 320)
    inverse_high, inverse_low, rows_high, rows_low, fwd, bwd, tables, wide = call(
        prepare_kernel,
        (
            shape(LINES, 320, 320, dtype=BF16),
            shape(LINES, 320, 320, dtype=BF16),
            shape(LINES, 160, 320, dtype=BF16),
            shape(LINES, 160, 320, dtype=BF16),
            shape(LINES, 160, 256, dtype=BF16),
            shape(LINES, 80, 256, dtype=BF16),
            shape(248, 128),
            shape(LINES, SEG, 50, 128),
        ),
        [HBM] + [VM] * 6,
        scratch=[pltpu.VMEM((LINES, 320, 320), F32), pltpu.SemaphoreType.DMA((LINES,))],
        limit=24,
        flops=4_000_000_000,
        moved=8_000_000,
        name="prepare",
    )(
        inverse,
        early,
        volume_jacobian.transpose(0, 3, 4, 5, 1, 2).reshape(4, 75, 2, SEG),
        side_jacobian.transpose(0, 1, 4, 5, 3, 2).reshape(LINES, 25, 4, SEG),
        span_jacobian.transpose(0, 1, 4, 5, 3, 2).reshape(LINES, 25, 2, SEG),
        mirror_face.transpose(0, 1, 3, 2).reshape(LINES, 4, SEG),
        edge_flip.transpose(0, 1, 3, 2).reshape(LINES, 4, SEG),
    )

    residual, turned, maps, z_high, z_low, v_high, v_low = call(
        sweep_kernel,
        (
            shape(64, 320),
            shape(320, 128),
            shape(LINES, 80, 256),
            shape(LINES, SEG, 80, 128, dtype=BF16),
            shape(LINES, SEG, 80, 128, dtype=BF16),
            shape(LINES, SEG, 80, 256, dtype=BF16),
            shape(LINES, SEG, 80, 256, dtype=BF16),
        ),
        [VM] * 15,
        scratch=[
            pltpu.VMEM((256, 320), F32),
            pltpu.VMEM((192, 640), F32),
            pltpu.VMEM((LINES, 160, 128), F32),
            pltpu.VMEM((LINES, 80, 128), F32),
            pltpu.VMEM((LINES, 80, 256), F32),
            pltpu.VMEM((LINES, SEG, 80, 128), F32),
        ],
        limit=28,
        flops=10_000_000_000,
        moved=20_000_000,
        name="sweep",
    )(
        flow,
        plane,
        gy_low,
        gy_high,
        below,
        above,
        source_term.reshape(64, 320),
        pseudo_time.reshape(64, 320),
        tables,
        wide,
        rows_high,
        rows_low,
        fwd,
        bwd,
        fixed,
    )

    within = [[SEG * g + m for m in range(SEG)] for g in range(groups)]

    def exchange(value):
        return lax.all_to_all(value, "span", 0, 0, axis_index_groups=within, tiled=True)

    maps = exchange(maps)
    t_maps, w_maps, whole = call(
        compose_kernel,
        (shape(SEG, 128, 128), shape(SEG, 128, 256), shape(80, 256)),
        [VM],
        limit=8,
        name="compose",
    )(maps)
    wholes = [whole] + [ring(whole, "span", SEG * distance) for distance in range(1, groups)]
    answers = call(
        solve_kernel,
        shape(SEG, 8, 256),
        [VM] * (groups + 2),
        scratch=[pltpu.VMEM((groups, 80, 256), F32)],
        limit=8,
        name="solve",
    )(*wholes, t_maps, w_maps)
    incoming = exchange(answers)
    updated = call(finish_kernel, shape(64, 320), [VM] * 10, limit=20, name="finish")(
        incoming, z_high, z_low, v_high, v_low, turned, inverse_high, inverse_low, flow, fixed
    )
    return updated.reshape(flow_state.shape), residual.reshape(flow_state.shape)


def solution(mesh):
    lines = P("gx", "gy", "span", None)
    blocks = P("gx", "gy", "span", None, None, None)
    return jax.shard_map(
        on_device,
        mesh=mesh,
        in_specs=(lines, lines, lines, blocks, blocks, blocks, P("gx", "gy", None, None), lines, lines),
        out_specs=(lines, lines),
        check_vma=False,
    )
```

```python
import functools

import jax
import jax.numpy as jnp
import numpy as np
from jax import lax
from jax.experimental import pallas as pl
from jax.experimental.pallas import tpu as pltpu
from jax.sharding import PartitionSpec as P

LIFT = 6.0
F32 = jnp.float32
BF16 = jnp.bfloat16
LINES = 8
SEG = 8


def derivative_matrix():
    points = np.array([-1.0, -1.0 / np.sqrt(5.0), 1.0 / np.sqrt(5.0), 1.0])
    matrix = np.zeros((4, 4))
    for target in range(4):
        for source in range(4):
            if target != source:
                numerator = 1.0
                denominator = 1.0
                for other in range(4):
                    if other != source and other != target:
                        numerator *= points[target] - points[other]
                    if other != source:
                        denominator *= points[source] - points[other]
                matrix[target, source] = numerator / denominator
    for target in range(4):
        matrix[target, target] = -np.sum(matrix[target])
    return matrix


def entry(a, b, c, v):
    return ((4 * a + b) * 4 + c) * 5 + v


@functools.cache
def constants():
    select = np.zeros((1120, 320), np.float32)
    place = np.zeros((320, 800), np.float32)
    layers = np.zeros((160, 320), np.float32)
    for v in range(5):
        for a in range(4):
            for b in range(4):
                for c in range(4):
                    row = v * 64 + a * 16 + b * 4 + c
                    select[row, entry(a, b, c, v)] = 1
                    place[entry(a, b, c, v), row] = 1
        for e in range(4):
            for c in range(4):
                row = v * 16 + e * 4 + c
                for side, plane in enumerate((0, 3)):
                    for flip in range(2):
                        along = 3 - e if flip else e
                        block = (side * 2 + flip) * 80
                        select[320 + block + row, entry(plane, along, c, v)] = 1
                        select[640 + block + row, entry(along, plane, c, v)] = 1
                    place[entry(plane, e, c, v), 320 + 80 * side + row] = -1
                    place[entry(e, plane, c, v), 480 + 80 * side + row] = -1
        for a in range(4):
            for b in range(4):
                row = v * 16 + a * 4 + b
                select[960 + row, entry(a, b, 3, v)] = 1
                select[1040 + row, entry(a, b, 0, v)] = 1
                place[entry(a, b, 0, v), 640 + row] = -1
                place[entry(a, b, 3, v), 720 + row] = -1
                layers[row, entry(a, b, 3, v)] = 1
                layers[80 + row, entry(a, b, 0, v)] = 1
    top, bottom = layers[:80].T, layers[80:].T
    columns_high = np.zeros((320, 512), np.float32)
    columns_low = np.zeros((320, 512), np.float32)
    for base, chosen in ((0, bottom), (256, top)):
        columns_high[:, base : base + 80] = chosen
        columns_high[:, base + 80 : base + 160] = chosen
        columns_low[:, base + 160 : base + 240] = chosen
    spread = np.concatenate([bottom, top], axis=1)
    eye, d = np.eye(4), derivative_matrix()
    along = np.concatenate(
        [
            np.kron(np.kron(d, eye), eye),
            np.kron(np.kron(eye, d), eye),
            np.kron(np.kron(eye, eye), d),
        ],
        axis=1,
    )
    high = along.astype(jnp.bfloat16).astype(np.float64)
    along = np.concatenate([high, high, along - high], axis=1)
    twice = np.concatenate([np.eye(64), np.eye(64)], axis=1)
    eye_320 = np.eye(320)
    blocks = [
        select,
        place[:, :320],
        place[:, 320:640],
        place[:, 640:],
        along[:, :192],
        along[:, 384:],
        twice,
        eye_320,
        spread,
    ]
    fixed = np.zeros((sum(len(block) for block in blocks), 320), np.float32)
    at = 0
    for block in blocks:
        fixed[at : at + len(block), : block.shape[1]] = block
        at += len(block)
    early = np.zeros((800, 512), np.float32)
    early[:320], early[320:640], early[640:, :320] = columns_high, columns_low, layers
    return early.astype(jnp.bfloat16), fixed.astype(jnp.bfloat16)


SELECT, PLACE_A, PLACE_B, PLACE_C = slice(0, 1120), slice(1120, 1440), slice(1440, 1760), slice(1760, 2080)
ALONG_HIGH, ALONG_LOW, TWICE = slice(2080, 2144), slice(2144, 2208), slice(2208, 2272)
EYE, SPREAD = slice(2272, 2592), slice(2592, 2912)
SIDE, SPAN, MIRROR, FLIP = 80, 184, 240, 244


def dot(a, b):
    return lax.dot_general(a, b, (((1,), (0,)), ((), ())), preferred_element_type=F32)


def dot_nt(a, b):
    return lax.dot_general(a, b, (((1,), (1,)), ((), ())), preferred_element_type=F32)


def split(x):
    high = x.astype(BF16)
    return high, (x - high.astype(F32)).astype(BF16)


def split_3(x):
    high = x.astype(BF16)
    rest = x - high.astype(F32)
    middle = rest.astype(BF16)
    return high, middle, (rest - middle.astype(F32)).astype(BF16)


def lanes(shape):
    return lax.broadcasted_iota(jnp.int32, shape, len(shape) - 1)


def rows(shape):
    return lax.broadcasted_iota(jnp.int32, shape, len(shape) - 2)


def roll(x, amount):
    return pltpu.roll(x, amount % 128, 1)


def pair_lanes(x):
    high = x.astype(BF16).astype(F32)
    return jnp.where(lanes(x.shape) < 64, high, roll(x - high, 64)).astype(BF16)


def left_cat(x):
    high, low = split(x)
    return jnp.concatenate([high, high, low], axis=1)


def right_cat(x):
    high, low = split(x)
    return jnp.concatenate([high, low, high], axis=0)


def pack_kernel(flow, plane_out, up_out, down_out, last_out, first_out):
    at = pl.multiple_of((1 - lax.axis_index("gx")) * 48, 16)
    plane_out[...] = flow[pl.ds(at, 16)]
    for i in range(4):
        down_out[8 * i : 8 * i + 8] = flow[16 * i : 16 * i + 8]
        up_out[8 * i : 8 * i + 8] = flow[16 * i + 8 : 16 * i + 16]
    for line in range(LINES):
        first_out[line : line + 1] = flow[8 * line : 8 * line + 1]
        last_out[line : line + 1] = flow[8 * line + 7 : 8 * line + 8]


def prepare_kernel(
    inverse,
    early_in,
    volume_in,
    side_in,
    span_in,
    mirror_in,
    flip_in,
    high_out,
    low_out,
    rows_high,
    rows_low,
    fwd_out,
    bwd_out,
    tables,
    held,
    early,
    volume_jacobian,
    side_jacobian,
    span_jacobian,
    mirror_face,
    edge_flip,
    arrived,
):
    pairs = [
        (volume_in, volume_jacobian),
        (side_in, side_jacobian),
        (span_in, span_jacobian),
        (mirror_in, mirror_face),
        (flip_in, edge_flip),
        (early_in, early),
    ]
    pairs += [(inverse.at[line], held.at[line]) for line in range(LINES)]
    copies = [
        pltpu.make_async_copy(source, target, arrived.at[at])
        for at, (source, target) in enumerate(pairs)
    ]
    for copy in copies:
        copy.start()
    for copy in copies[:6]:
        copy.wait()
    for line in range(LINES):
        here = slice(8 * line, 8 * line + 8)
        tables[0:75, here] = volume_jacobian[line // 2, :, line % 2, :]
        tables[SIDE : SIDE + 100, here] = side_jacobian[line].reshape(100, 8)
        tables[SPAN : SPAN + 50, here] = LIFT * span_jacobian[line].reshape(50, 8)
        tables[MIRROR : MIRROR + 4, here] = mirror_face[line].astype(F32)
        tables[FLIP : FLIP + 4, here] = edge_flip[line].astype(F32)
    for line in range(LINES):
        copies[6 + line].wait()
        high, low = split(held[line])
        high_out[line] = high
        low_out[line] = low
        layers = early[640:800, 0:320]
        rows_high[line] = dot(layers, high).astype(BF16)
        rows_low[line] = dot(layers, low).astype(BF16)
    mine = lax.rem(lax.axis_index("span"), LINES)
    both = dot(rows_high[mine], early[0:320]) + dot(rows_low[mine], early[320:640])
    both = both.astype(BF16)
    fwd_out[...] = both[:, :256]
    bwd_out[...] = both[80:, 256:]


def mix(coefficient, slabs):
    out = []
    for w in range(5):
        total = coefficient(w, 0) * slabs[0]
        for v in range(1, 5):
            total = total + coefficient(w, v) * slabs[v]
        out.append(total)
    return out


def slabs_of(x, size):
    return [x[v * size : (v + 1) * size] for v in range(5)]


def sweep_kernel(
    flow,
    plane,
    gy_low,
    gy_high,
    below,
    above,
    source,
    pseudo,
    tables,
    rows_high,
    rows_low,
    fixed,
    residual_out,
    turned_out,
    sent_out,
    extended,
    flux,
):
    gx_at, gy_at = lax.axis_index("gx"), lax.axis_index("gy")
    first_lo = (gx_at > 0).astype(F32)
    second_lo = (gy_at > 0).astype(F32)
    second_hi = (gy_at < lax.axis_size("gy") - 1).astype(F32)
    u = flow[...]
    extended[0:64] = u
    extended[64:80] = plane[...] * (1.0 - first_lo)
    extended[80:112] = jnp.zeros((32, 320), F32)
    extended[112:128] = plane[...] * first_lo
    for i in range(4):
        extended[128 + 16 * i : 136 + 16 * i] = gy_low[8 * i : 8 * i + 8] * second_lo
        extended[136 + 16 * i : 144 + 16 * i] = gy_high[8 * i : 8 * i + 8] * second_hi
    position = rows((8, 320))
    for line in range(LINES):
        extended[192 + 8 * line : 200 + 8 * line] = jnp.where(
            position == 0,
            below[line : line + 1],
            jnp.where(position == 7, above[line : line + 1], 0.0),
        )
    chosen = sum(dot_nt(fixed[SELECT], part) for part in split(extended[...]))
    near, far = chosen[:, :128], chosen[:, 128:]
    lane = lanes((1, 128))
    table = lambda r: tables[r : r + 1, :]

    by_variable = slabs_of(near[0:320], 64)
    for d in range(3):
        mixed = mix(lambda w, v: table(d * 25 + w * 5 + v), by_variable)
        for w in range(5):
            flux[d * 64 : d * 64 + 64, w * 128 : w * 128 + 128] = mixed[w]
    flux_high, flux_low = split(flux[...])
    volume = dot(fixed[ALONG_HIGH, 0:192], flux_high) + dot(fixed[ALONG_HIGH, 0:192], flux_low)
    volume = volume + dot(fixed[ALONG_LOW, 0:192], flux_high)
    pieces = [volume[:, w * 128 : w * 128 + 128] for w in range(5)]

    for f in range(4):
        base = 320 + 320 * (f // 2)
        candidates = [near[base + 80 * n : base + 80 * n + 80] for n in range(4)]
        outer = [far[base + 80 * n : base + 80 * n + 80] for n in range(4)]
        own = candidates[2 * (f % 2)]
        if f == 0:
            shifted = [roll(x, 16) for x in candidates]
        elif f == 1:
            shifted = [roll(x, -16) for x in candidates]
        elif f == 2:
            shifted = [
                jnp.where((lane // 8) % 2 == 1, roll(x, 8), y) for x, y in zip(candidates, outer)
            ]
        else:
            shifted = [
                jnp.where((lane // 8) % 2 == 0, roll(x, -8), y) for x, y in zip(candidates, outer)
            ]
        mirrored = table(MIRROR + f) > 0.5
        flipped = table(FLIP + f) > 0.5
        neighbour = jnp.where(
            flipped,
            jnp.where(mirrored, shifted[3], shifted[1]),
            jnp.where(mirrored, shifted[2], shifted[0]),
        )
        jump = LIFT * (neighbour - own)
        pieces += mix(lambda w, v: table(SIDE + (w * 5 + v) * 4 + f), slabs_of(jump, 16))

    top, bottom = near[960:1040], near[1040:1120]
    outer_top, outer_bottom = roll(far[960:1040], 64), roll(far[1040:1120], 64)
    lower_jump = jnp.where(lane % 8 == 0, outer_top, roll(top, 1)) - bottom
    upper_jump = jnp.where(lane % 8 == 7, outer_bottom, roll(bottom, -1)) - top
    pieces += mix(lambda w, v: table(SPAN + (w * 5 + v) * 2), slabs_of(lower_jump, 16))
    pieces += mix(lambda w, v: table(SPAN + (w * 5 + v) * 2 + 1), slabs_of(upper_jump, 16))
    pieces = [
        pair_lanes(jnp.concatenate(group, axis=0)) for group in (pieces[:5], pieces[5:25], pieces[25:])
    ]
    operator = dot(fixed[PLACE_A], pieces[0]) + dot(fixed[PLACE_B], pieces[1])
    operator = operator + dot(fixed[PLACE_C, 0:160], pieces[2])
    operator_high, operator_low = split(operator)
    twice = fixed[TWICE, 0:128]
    operator_rows = dot_nt(twice, operator_high) + dot_nt(twice, operator_low)
    residual = source[...] - (pseudo[...] * u + operator_rows)
    residual_out[...] = residual

    high, low = split(residual)
    turned = dot_nt(fixed[EYE], jnp.concatenate([high, low], axis=0))
    turned_out[...] = turned + roll(turned, 64)
    turned = turned.astype(BF16)
    trace_lane = lanes((160, 128))
    traces = jnp.zeros((160, 128), F32)
    for line in range(LINES):
        applied = dot(rows_high[line], turned) + dot(rows_low[line], turned)
        traces = jnp.where(trace_lane % 64 // 8 == line, applied, traces)
    traces = traces + roll(traces, 64)

    sent = jnp.concatenate([traces, tables[SPAN : SPAN + 56], jnp.zeros((40, 128), F32)], axis=0)
    sent_out[...] = jnp.transpose(sent)[:64]


def maps_kernel(
    received,
    fwd,
    bwd,
    z_high,
    z_low,
    v_high,
    v_low,
    t_out,
    w_out,
    whole_out,
    wide,
    started,
    t_state,
    w_state,
    bottoms,
    maps,
):
    turned = jnp.transpose(jnp.concatenate([received[...], jnp.zeros((64, 256), F32)], axis=0))
    jacobians = turned[160:210]
    trace_lane = lanes((160, 128))
    small_lane, small_row = lanes((80, 128)), rows((80, 128))
    for e in range(SEG):
        for k in range(SEG):
            at = e * SEG + k
            wide[e, k] = jnp.broadcast_to(jacobians[:, at : at + 1], (50, 128))
        moved = roll(turned[0:160], 80 - 8 * e)
        started[e] = jnp.where((trace_lane >= 80) & (trace_lane < 88), moved, 0.0)
        t_state[e] = jnp.where(small_lane == small_row, 1.0, 0.0)
        w_state[e] = jnp.where(lanes((80, 256)) == rows((80, 256)) + 88, 1.0, 0.0)

    def coupled(e, k, side, state):
        out = mix(lambda w, v: wide[e, k, pl.ds((w * 5 + v) * 2 + side, 1)], slabs_of(state, 16))
        return jnp.concatenate(out, axis=0)

    def forward(k, carry):
        mine = small_lane == 80 + k
        for pair in range(0, SEG, 2):
            cats = []
            for e in (pair, pair + 1):
                z_hi, z_lo = split(coupled(e, k, 0, t_state[e]))
                z_high[e, k] = z_hi
                z_low[e, k] = z_lo
                cats.append(jnp.concatenate([z_hi, z_lo, z_hi], axis=0))
            both = dot(fwd[:, 0:240], jnp.concatenate(cats, axis=1))
            for e, y in ((pair, both[:, :128]), (pair + 1, both[:, 128:])):
                t_state[e] = y[:80] + jnp.where(mine, started[e, 0:80], 0.0)
                bottoms[e, k] = y[80:] + jnp.where(mine, started[e, 80:160], 0.0)
        return carry

    lax.fori_loop(0, SEG, forward, 0)

    def backward(step, carry):
        k = SEG - 1 - step
        for e in range(SEG):
            z = [coupled(e, k, 1, w_state[e, :, half]) for half in (slice(0, 128), slice(128, 256))]
            z_hi, z_lo = split(jnp.concatenate(z, axis=1))
            v_high[e, k] = z_hi
            v_low[e, k] = z_lo
            y = dot(bwd[:, 0:240], jnp.concatenate([z_hi, z_lo, z_hi], axis=0))
            w_state[e, :, 0:128] = y[:, :128] + bottoms[e, k]
            w_state[e, :, 128:256] = y[:, 128:]
        return carry

    lax.fori_loop(0, SEG, backward, 0)
    for e in range(SEG):
        maps[e, :, 0:128] = w_state[e, :, 0:128]
        maps[e, :, 128:256] = w_state[e, :, 128:256] + roll(t_state[e], 40)
    compose(maps, t_out, w_out, whole_out)


def compose(maps, t_out, w_out, whole_out):
    lane = lanes((80, 128))
    tall_lane, tall_row = lanes((128, 128)), rows((128, 128))
    zero = jnp.zeros((48, 128), F32)
    fixed = jnp.where((tall_row < 80) & (tall_lane == tall_row), 1.0, 0.0)
    ones = jnp.where((tall_row >= 80) & (tall_row < 88) & (tall_lane == 80), 1.0, 0.0)
    state = fixed + ones
    coupled = []
    for e in range(SEG):
        t_out[e] = state
        left, right = maps[e, :, 0:128], maps[e, :, 128:256]
        state_cat = right_cat(state)
        both = jnp.concatenate([jnp.where(lane < 88, roll(right, 88), 0.0), jnp.where(lane < 88, left, 0.0)], axis=0)
        y = dot(left_cat(both), state_cat)
        coupled.append(y[80:])
        state = jnp.concatenate([y[:80], ones[80:]], axis=0)
    last = state[:80]
    w0 = jnp.where(tall_lane == tall_row + 81, 1.0, 0.0)
    w1 = jnp.where((tall_lane == tall_row - 47) & (tall_row < 80), 1.0, 0.0)
    for e in range(SEG - 1, -1, -1):
        w_out[e, :, 0:128] = w0
        w_out[e, :, 128:256] = w1
        left, right = maps[e, :, 0:128], maps[e, :, 128:256]
        back = jnp.where(lane < 40, roll(left, 40), jnp.where(lane < 80, roll(right, 40), 0.0))
        back_cat = left_cat(back)
        y0 = dot(back_cat, right_cat(w0)) + coupled[e]
        y1 = dot(back_cat, right_cat(w1))
        w0 = jnp.concatenate([y0, zero], axis=0)
        w1 = jnp.concatenate([y1, zero], axis=0)
    second = w1[:80] + roll(last, 33)
    whole_out[:, 0:128] = w0[:80]
    whole_out[:, 128:256] = second


def solve_kernel(*refs):
    *parts, t_in, w_in, z_high, z_low, v_high, v_low, out, wholes = refs
    groups = len(parts)
    mine = lax.axis_index("span") // SEG
    for distance, part in enumerate(parts):
        wholes[lax.rem(mine - distance + groups, groups)] = part[...]
    lane = lanes((80, 128))
    tall_row = rows((128, 128))
    one = jnp.where(tall_row == 80, 1.0, 0.0)
    zero = jnp.zeros((48, 128), F32)

    def pieces(group):
        left, right = wholes[group, :, 0:128], wholes[group, :, 128:256]
        forward = jnp.where(lane < 81, roll(right, -33), 0.0)
        cross = jnp.where(lane < 81, left, 0.0)
        back = jnp.where(lane < 47, roll(left, 47), jnp.where(lane < 80, roll(right, 47), 0.0))
        return forward, cross, back

    parts = [pieces(group) for group in range(groups)]
    traces = [one]
    for group in range(groups - 1):
        y = dot(left_cat(parts[group][0]), right_cat(traces[-1]))
        traces.append(jnp.concatenate([y, zero], axis=0) + one)
    backs = [jnp.zeros((128, 128), F32)]
    for group in range(groups - 1, 0, -1):
        y = dot(left_cat(parts[group][1]), right_cat(traces[group]))
        y = y + dot(left_cat(parts[group][2]), right_cat(backs[0]))
        backs.insert(0, jnp.concatenate([y, zero], axis=0))
    trace, back = traces[0], backs[0]
    for group in range(1, groups):
        trace = jnp.where(mine == group, traces[group], trace)
        back = jnp.where(mine == group, backs[group], back)
    trace_row = jnp.transpose(trace)[0:8]
    back_row = roll(jnp.transpose(back)[0:8], 81)
    line_lane = lanes((8, 128))
    y0 = jnp.where(line_lane < 81, trace_row, back_row)
    y1 = jnp.where(line_lane < 33, back_row, 0.0)
    trace_cat = left_cat(trace_row)
    y_cat = left_cat(jnp.concatenate([y0, y1], axis=1))
    answers = []
    for e in range(SEG):
        high, low = split(t_in[e])
        t_row = dot_nt(trace_cat, jnp.concatenate([high, low, high], axis=1))
        high, low = split(w_in[e])
        c_row = roll(dot_nt(y_cat, jnp.concatenate([high, low, high], axis=1)), 88)
        first = jnp.where(line_lane < 80, t_row, jnp.where(line_lane < 88, 1.0, c_row))
        second = jnp.where(line_lane < 40, c_row, 0.0)
        answers.append(jnp.concatenate([first, second], axis=1))
    high, low = split(jnp.concatenate(answers, axis=0))
    y = jnp.concatenate([high, low], axis=0)
    small_lane = lane % 64
    lower = jnp.zeros((80, 128), F32)
    upper = jnp.zeros((80, 128), F32)
    for e in range(SEG):
        z_hi, z_lo = z_high[e].reshape(640, 128), z_low[e].reshape(640, 128)
        v_hi, v_lo = v_high[e].reshape(640, 256), v_low[e].reshape(640, 256)
        c = dot_nt(z_hi, y[:, :128]) + dot_nt(z_lo, y[:, :128])
        d = dot_nt(v_hi, y) + dot_nt(v_lo, y)
        for k in range(SEG):
            mine = small_lane == e * SEG + k
            lower = jnp.where(mine, c[80 * k : 80 * k + 80], lower)
            upper = jnp.where(mine, d[80 * k : 80 * k + 80], upper)
    both = jnp.concatenate([lower, upper, jnp.zeros((96, 128), F32)], axis=0)
    out[...] = jnp.transpose(both + roll(both, 64))[:64]


def finish_kernel(incoming, turned, inverse_high, inverse_low, flow, fixed, out):
    high, low = split(incoming[...])
    added = dot_nt(fixed[SPREAD, 0:160], jnp.concatenate([high, low], axis=0)[:, 0:160])
    load = pair_lanes(turned[...] + added + roll(added, 64))
    wide_lane = lanes((320, 128)) % 64
    total = jnp.zeros((320, 128), F32)
    for line in range(LINES):
        applied = dot(inverse_high[line], load) + dot(inverse_low[line], load)
        total = jnp.where(wide_lane // 8 == line, applied, total)
    high, low = split(total)
    twice = fixed[TWICE, 0:128]
    out[...] = flow[...] + dot_nt(twice, high) + dot_nt(twice, low)


def call(kernel, out_shape, in_specs, scratch=(), limit=16, flops=0, moved=0, name=None):
    return pl.pallas_call(
        kernel,
        out_shape=out_shape,
        in_specs=in_specs,
        out_specs=jax.tree.map(lambda _: pl.BlockSpec(memory_space=pltpu.VMEM), out_shape),
        scratch_shapes=list(scratch),
        compiler_params=pltpu.CompilerParams(vmem_limit_bytes=limit * 1024 * 1024),
        cost_estimate=pl.CostEstimate(flops=flops, bytes_accessed=moved, transcendentals=0),
        name=name,
    )


VM = pl.BlockSpec(memory_space=pltpu.VMEM)
HBM = pl.BlockSpec(memory_space=pltpu.HBM)


def shape(*dims, dtype=F32):
    return jax.ShapeDtypeStruct(dims, dtype)


def on_device(
    flow_state,
    source_term,
    pseudo_time,
    volume_jacobian,
    side_jacobian,
    span_jacobian,
    line_inverse,
    mirror_face,
    edge_flip,
):
    early, fixed = (jnp.asarray(value) for value in constants())
    groups = lax.axis_size("span") // SEG

    def ring(value, axis, step):
        count = lax.axis_size(axis)
        return lax.ppermute(value, axis, [(i, (i + step) % count) for i in range(count)])

    flow = flow_state.reshape(64, 320)
    plane, up, down, last, first = call(
        pack_kernel,
        (shape(16, 320), shape(32, 320), shape(32, 320), shape(8, 320), shape(8, 320)),
        [VM],
        limit=4,
        name="pack",
    )(flow)
    with jax.named_scope("halo"):
        below, above = ring(last, "span", 1), ring(first, "span", -1)
        gy_low, gy_high = ring(up, "gy", 1), ring(down, "gy", -1)
        plane = ring(plane, "gx", 1)

    inverse = line_inverse.reshape(LINES, 320, 320)
    natural = [
        volume_jacobian.transpose(0, 3, 4, 5, 1, 2).reshape(4, 75, 2, SEG),
        side_jacobian.transpose(0, 1, 4, 5, 3, 2).reshape(LINES, 25, 4, SEG),
        span_jacobian.transpose(0, 1, 4, 5, 3, 2).reshape(LINES, 25, 2, SEG),
        mirror_face.transpose(0, 1, 3, 2).reshape(LINES, 4, SEG),
        edge_flip.transpose(0, 1, 3, 2).reshape(LINES, 4, SEG),
    ]
    inverse_high, inverse_low, rows_high, rows_low, fwd, bwd, tables = call(
        prepare_kernel,
        (
            shape(LINES, 320, 320, dtype=BF16),
            shape(LINES, 320, 320, dtype=BF16),
            shape(LINES, 160, 320, dtype=BF16),
            shape(LINES, 160, 320, dtype=BF16),
            shape(160, 256, dtype=BF16),
            shape(80, 256, dtype=BF16),
            shape(248, 128),
        ),
        [HBM] * 7,
        scratch=[pltpu.VMEM((LINES, 320, 320), F32), pltpu.VMEM(early.shape, BF16)]
        + [pltpu.VMEM(x.shape, x.dtype) for x in natural]
        + [pltpu.SemaphoreType.DMA((LINES + 6,))],
        limit=24,
        flops=4_000_000_000,
        moved=8_000_000,
        name="prepare",
    )(*(pltpu.with_memory_space_constraint(x, pltpu.HBM) for x in (inverse, early, *natural)))

    residual, turned, sent = call(
        sweep_kernel,
        (shape(64, 320), shape(320, 128), shape(64, 256)),
        [VM] * 12,
        scratch=[pltpu.VMEM((256, 320), F32), pltpu.VMEM((192, 640), F32)],
        limit=20,
        flops=3_000_000_000,
        moved=8_000_000,
        name="sweep",
    )(
        flow,
        plane,
        gy_low,
        gy_high,
        below,
        above,
        source_term.reshape(64, 320),
        pseudo_time.reshape(64, 320),
        tables,
        rows_high,
        rows_low,
        fixed,
    )

    within = [[SEG * g + m for m in range(SEG)] for g in range(groups)]

    def exchange(value):
        value = value.reshape(SEG, 8, 256)
        value = lax.all_to_all(value, "span", 0, 0, axis_index_groups=within, tiled=True)
        return value.reshape(64, 256)

    z_high, z_low, v_high, v_low, t_maps, w_maps, whole = call(
        maps_kernel,
        (
            shape(SEG, SEG, 80, 128, dtype=BF16),
            shape(SEG, SEG, 80, 128, dtype=BF16),
            shape(SEG, SEG, 80, 256, dtype=BF16),
            shape(SEG, SEG, 80, 256, dtype=BF16),
            shape(SEG, 128, 128),
            shape(SEG, 128, 256),
            shape(80, 256),
        ),
        [VM] * 3,
        scratch=[
            pltpu.VMEM((SEG, SEG, 50, 128), F32),
            pltpu.VMEM((SEG, 160, 128), F32),
            pltpu.VMEM((SEG, 80, 128), F32),
            pltpu.VMEM((SEG, 80, 256), F32),
            pltpu.VMEM((SEG, SEG, 80, 128), F32),
            pltpu.VMEM((SEG, 80, 256), F32),
        ],
        limit=28,
        name="maps",
    )(exchange(sent), fwd, bwd)
    wholes = [whole] + [ring(whole, "span", SEG * distance) for distance in range(1, groups)]
    answers = call(
        solve_kernel,
        shape(64, 256),
        [VM] * (groups + 6),
        scratch=[pltpu.VMEM((groups, 80, 256), F32)],
        limit=24,
        name="solve",
    )(*wholes, t_maps, w_maps, z_high, z_low, v_high, v_low)
    updated = call(finish_kernel, shape(64, 320), [VM] * 6, limit=20, name="finish")(
        exchange(answers), turned, inverse_high, inverse_low, flow, fixed
    )
    return updated.reshape(flow_state.shape), residual.reshape(flow_state.shape)


def solution(mesh):
    lines = P("gx", "gy", "span", None)
    blocks = P("gx", "gy", "span", None, None, None)
    return jax.shard_map(
        on_device,
        mesh=mesh,
        in_specs=(lines, lines, lines, blocks, blocks, blocks, P("gx", "gy", None, None), lines, lines),
        out_specs=(lines, lines),
        check_vma=False,
    )
```

```python
import functools

import jax
import jax.numpy as jnp
import numpy as np
from jax import lax
from jax.experimental import pallas as pl
from jax.experimental.pallas import tpu as pltpu
from jax.sharding import PartitionSpec as P

LIFT = 6.0
F32 = jnp.float32
BF16 = jnp.bfloat16
LINES = 8
SEG = 8


def derivative_matrix():
    points = np.array([-1.0, -1.0 / np.sqrt(5.0), 1.0 / np.sqrt(5.0), 1.0])
    matrix = np.zeros((4, 4))
    for target in range(4):
        for source in range(4):
            if target != source:
                numerator = 1.0
                denominator = 1.0
                for other in range(4):
                    if other != source and other != target:
                        numerator *= points[target] - points[other]
                    if other != source:
                        denominator *= points[source] - points[other]
                matrix[target, source] = numerator / denominator
    for target in range(4):
        matrix[target, target] = -np.sum(matrix[target])
    return matrix


def entry(a, b, c, v):
    return ((4 * a + b) * 4 + c) * 5 + v


@functools.cache
def constants():
    select = np.zeros((1120, 320), np.float32)
    place = np.zeros((320, 800), np.float32)
    layers = np.zeros((160, 320), np.float32)
    for v in range(5):
        for a in range(4):
            for b in range(4):
                for c in range(4):
                    row = v * 64 + a * 16 + b * 4 + c
                    select[row, entry(a, b, c, v)] = 1
                    place[entry(a, b, c, v), row] = 1
        for e in range(4):
            for c in range(4):
                row = v * 16 + e * 4 + c
                for side, plane in enumerate((0, 3)):
                    for flip in range(2):
                        along = 3 - e if flip else e
                        block = (side * 2 + flip) * 80
                        select[320 + block + row, entry(plane, along, c, v)] = 1
                        select[640 + block + row, entry(along, plane, c, v)] = 1
                    place[entry(plane, e, c, v), 320 + 80 * side + row] = -1
                    place[entry(e, plane, c, v), 480 + 80 * side + row] = -1
        for a in range(4):
            for b in range(4):
                row = v * 16 + a * 4 + b
                select[960 + row, entry(a, b, 3, v)] = 1
                select[1040 + row, entry(a, b, 0, v)] = 1
                place[entry(a, b, 0, v), 640 + row] = -1
                place[entry(a, b, 3, v), 720 + row] = -1
                layers[row, entry(a, b, 3, v)] = 1
                layers[80 + row, entry(a, b, 0, v)] = 1
    top, bottom = layers[:80].T, layers[80:].T
    columns_high = np.zeros((320, 512), np.float32)
    columns_low = np.zeros((320, 512), np.float32)
    for base, chosen in ((0, bottom), (256, top)):
        columns_high[:, base : base + 80] = chosen
        columns_high[:, base + 80 : base + 160] = chosen
        columns_low[:, base + 160 : base + 240] = chosen
    spread = np.concatenate([bottom, top], axis=1)
    eye, d = np.eye(4), derivative_matrix()
    along = np.concatenate(
        [
            np.kron(np.kron(d, eye), eye),
            np.kron(np.kron(eye, d), eye),
            np.kron(np.kron(eye, eye), d),
        ],
        axis=1,
    )
    high = along.astype(jnp.bfloat16).astype(np.float64)
    along = np.concatenate([high, high, along - high], axis=1)
    twice = np.concatenate([np.eye(64), np.eye(64)], axis=1)
    eye_320 = np.eye(320)
    blocks = [
        select,
        place[:, :320],
        place[:, 320:640],
        place[:, 640:],
        along[:, :192],
        along[:, 384:],
        twice,
        eye_320,
        spread,
    ]
    fixed = np.zeros((sum(len(block) for block in blocks), 320), np.float32)
    at = 0
    for block in blocks:
        fixed[at : at + len(block), : block.shape[1]] = block
        at += len(block)
    early = np.zeros((800, 512), np.float32)
    early[:320], early[320:640], early[640:, :320] = columns_high, columns_low, layers
    return early.astype(jnp.bfloat16), fixed.astype(jnp.bfloat16)


SELECT, PLACE_A, PLACE_B, PLACE_C = slice(0, 1120), slice(1120, 1440), slice(1440, 1760), slice(1760, 2080)
ALONG_HIGH, ALONG_LOW, TWICE = slice(2080, 2144), slice(2144, 2208), slice(2208, 2272)
EYE, SPREAD = slice(2272, 2592), slice(2592, 2912)
SIDE, SPAN, MIRROR, FLIP = 80, 184, 240, 244


def dot(a, b):
    return lax.dot_general(a, b, (((1,), (0,)), ((), ())), preferred_element_type=F32)


def dot_nt(a, b):
    return lax.dot_general(a, b, (((1,), (1,)), ((), ())), preferred_element_type=F32)


def split(x):
    high = x.astype(BF16)
    return high, (x - high.astype(F32)).astype(BF16)


def split_3(x):
    high = x.astype(BF16)
    rest = x - high.astype(F32)
    middle = rest.astype(BF16)
    return high, middle, (rest - middle.astype(F32)).astype(BF16)


def lanes(shape):
    return lax.broadcasted_iota(jnp.int32, shape, len(shape) - 1)


def rows(shape):
    return lax.broadcasted_iota(jnp.int32, shape, len(shape) - 2)


def roll(x, amount):
    return pltpu.roll(x, amount % 128, 1)


def pair_lanes(x):
    high = x.astype(BF16).astype(F32)
    return jnp.where(lanes(x.shape) < 64, high, roll(x - high, 64)).astype(BF16)


def against_both(x):
    paired = pair_lanes(x)
    first = jnp.where(lanes(x.shape) < 64, paired.astype(F32), 0.0).astype(BF16)
    return jnp.concatenate([paired, first], axis=0)


def left_cat(x):
    high, low = split(x)
    return jnp.concatenate([high, high, low], axis=1)


def right_cat(x):
    high, low = split(x)
    return jnp.concatenate([high, low, high], axis=0)


def pack_kernel(flow, plane_out, up_out, down_out, last_out, first_out):
    at = pl.multiple_of((1 - lax.axis_index("gx")) * 48, 16)
    plane_out[...] = flow[pl.ds(at, 16)]
    for i in range(4):
        down_out[8 * i : 8 * i + 8] = flow[16 * i : 16 * i + 8]
        up_out[8 * i : 8 * i + 8] = flow[16 * i + 8 : 16 * i + 16]
    for line in range(LINES):
        first_out[line : line + 1] = flow[8 * line : 8 * line + 1]
        last_out[line : line + 1] = flow[8 * line + 7 : 8 * line + 8]


def prepare_kernel(
    inverse,
    early_in,
    volume_in,
    side_in,
    span_in,
    mirror_in,
    flip_in,
    rows_high,
    rows_low,
    fwd_out,
    bwd_out,
    tables,
    held,
    early,
    volume_jacobian,
    side_jacobian,
    span_jacobian,
    mirror_face,
    edge_flip,
    arrived,
):
    pairs = [
        (volume_in, volume_jacobian),
        (side_in, side_jacobian),
        (span_in, span_jacobian),
        (mirror_in, mirror_face),
        (flip_in, edge_flip),
        (early_in, early),
    ]
    pairs += [(inverse.at[line], held.at[line]) for line in range(LINES)]
    copies = [
        pltpu.make_async_copy(source, target, arrived.at[at])
        for at, (source, target) in enumerate(pairs)
    ]
    for copy in copies:
        copy.start()
    for copy in copies[:6]:
        copy.wait()
    for line in range(LINES):
        here = slice(8 * line, 8 * line + 8)
        tables[0:75, here] = volume_jacobian[line // 2, :, line % 2, :]
        tables[SIDE : SIDE + 100, here] = side_jacobian[line].reshape(100, 8)
        tables[SPAN : SPAN + 50, here] = LIFT * span_jacobian[line].reshape(50, 8)
        tables[MIRROR : MIRROR + 4, here] = mirror_face[line].astype(F32)
        tables[FLIP : FLIP + 4, here] = edge_flip[line].astype(F32)
    for line in range(LINES):
        copies[6 + line].wait()
        high, low = split(held[line])
        layers = early[640:800, 0:320]
        rows_high[line] = dot(layers, high).astype(BF16)
        rows_low[line] = dot(layers, low).astype(BF16)
    mine = lax.rem(lax.axis_index("span"), LINES)
    both = dot(rows_high[mine], early[0:320]) + dot(rows_low[mine], early[320:640])
    both = both.astype(BF16)
    fwd_out[...] = both[:, :256]
    bwd_out[...] = both[80:, 256:]


def base_kernel(inverse, turned, flow, fixed, base_out, columns_high, columns_low, held, arrived):
    copies = [
        pltpu.make_async_copy(inverse.at[line], held.at[line], arrived.at[line])
        for line in range(LINES)
    ]
    for copy in copies:
        copy.start()
    load = pair_lanes(turned[...])
    spread = fixed[SPREAD, 0:160]
    wide_lane = lanes((320, 128)) % 64
    total = jnp.zeros((320, 128), F32)
    for line in range(LINES):
        copies[line].wait()
        high, low = split(held[line])
        total = jnp.where(wide_lane // 8 == line, dot(high, load) + dot(low, load), total)
        columns_high[line] = dot(high, spread).astype(BF16)
        columns_low[line] = dot(low, spread).astype(BF16)
    high, low = split(total)
    twice = fixed[TWICE, 0:128]
    base_out[...] = flow[...] + dot_nt(twice, high) + dot_nt(twice, low)


def unpack(left, right):
    lane = lanes((80, 128))
    forward = jnp.where(lane < 88, roll(right, 88), 0.0)
    cross = jnp.where(lane < 88, left, 0.0)
    back = jnp.where(lane < 40, roll(left, 40), jnp.where(lane < 80, roll(right, 40), 0.0))
    return forward, cross, back


def mix(coefficient, slabs):
    out = []
    for w in range(5):
        total = coefficient(w, 0) * slabs[0]
        for v in range(1, 5):
            total = total + coefficient(w, v) * slabs[v]
        out.append(total)
    return out


def slabs_of(x, size):
    return [x[v * size : (v + 1) * size] for v in range(5)]


def sweep_kernel(
    flow,
    plane,
    gy_low,
    gy_high,
    below,
    above,
    source,
    pseudo,
    tables,
    rows_high,
    rows_low,
    fixed,
    residual_out,
    turned_out,
    sent_out,
    extended,
    flux,
):
    gx_at, gy_at = lax.axis_index("gx"), lax.axis_index("gy")
    first_lo = (gx_at > 0).astype(F32)
    second_lo = (gy_at > 0).astype(F32)
    second_hi = (gy_at < lax.axis_size("gy") - 1).astype(F32)
    u = flow[...]
    extended[0:64] = u
    extended[64:80] = plane[...] * (1.0 - first_lo)
    extended[80:112] = jnp.zeros((32, 320), F32)
    extended[112:128] = plane[...] * first_lo
    for i in range(4):
        extended[128 + 16 * i : 136 + 16 * i] = gy_low[8 * i : 8 * i + 8] * second_lo
        extended[136 + 16 * i : 144 + 16 * i] = gy_high[8 * i : 8 * i + 8] * second_hi
    position = rows((8, 320))
    for line in range(LINES):
        extended[192 + 8 * line : 200 + 8 * line] = jnp.where(
            position == 0,
            below[line : line + 1],
            jnp.where(position == 7, above[line : line + 1], 0.0),
        )
    chosen = sum(dot_nt(fixed[SELECT], part) for part in split(extended[...]))
    near, far = chosen[:, :128], chosen[:, 128:]
    lane = lanes((1, 128))
    table = lambda r: tables[r : r + 1, :]

    by_variable = slabs_of(near[0:320], 64)
    for d in range(3):
        mixed = mix(lambda w, v: table(d * 25 + w * 5 + v), by_variable)
        for w in range(5):
            flux[d * 64 : d * 64 + 64, w * 128 : w * 128 + 128] = mixed[w]
    flux_high, flux_low = split(flux[...])
    volume = dot(fixed[ALONG_HIGH, 0:192], flux_high) + dot(fixed[ALONG_HIGH, 0:192], flux_low)
    volume = volume + dot(fixed[ALONG_LOW, 0:192], flux_high)
    pieces = [volume[:, w * 128 : w * 128 + 128] for w in range(5)]

    for f in range(4):
        base = 320 + 320 * (f // 2)
        candidates = [near[base + 80 * n : base + 80 * n + 80] for n in range(4)]
        outer = [far[base + 80 * n : base + 80 * n + 80] for n in range(4)]
        own = candidates[2 * (f % 2)]
        if f == 0:
            shifted = [roll(x, 16) for x in candidates]
        elif f == 1:
            shifted = [roll(x, -16) for x in candidates]
        elif f == 2:
            shifted = [
                jnp.where((lane // 8) % 2 == 1, roll(x, 8), y) for x, y in zip(candidates, outer)
            ]
        else:
            shifted = [
                jnp.where((lane // 8) % 2 == 0, roll(x, -8), y) for x, y in zip(candidates, outer)
            ]
        mirrored = table(MIRROR + f) > 0.5
        flipped = table(FLIP + f) > 0.5
        neighbour = jnp.where(
            flipped,
            jnp.where(mirrored, shifted[3], shifted[1]),
            jnp.where(mirrored, shifted[2], shifted[0]),
        )
        jump = LIFT * (neighbour - own)
        pieces += mix(lambda w, v: table(SIDE + (w * 5 + v) * 4 + f), slabs_of(jump, 16))

    top, bottom = near[960:1040], near[1040:1120]
    outer_top, outer_bottom = roll(far[960:1040], 64), roll(far[1040:1120], 64)
    lower_jump = jnp.where(lane % 8 == 0, outer_top, roll(top, 1)) - bottom
    upper_jump = jnp.where(lane % 8 == 7, outer_bottom, roll(bottom, -1)) - top
    pieces += mix(lambda w, v: table(SPAN + (w * 5 + v) * 2), slabs_of(lower_jump, 16))
    pieces += mix(lambda w, v: table(SPAN + (w * 5 + v) * 2 + 1), slabs_of(upper_jump, 16))
    pieces = [
        pair_lanes(jnp.concatenate(group, axis=0)) for group in (pieces[:5], pieces[5:25], pieces[25:])
    ]
    operator = dot(fixed[PLACE_A], pieces[0]) + dot(fixed[PLACE_B], pieces[1])
    operator = operator + dot(fixed[PLACE_C, 0:160], pieces[2])
    operator_high, operator_low = split(operator)
    twice = fixed[TWICE, 0:128]
    operator_rows = dot_nt(twice, operator_high) + dot_nt(twice, operator_low)
    residual = source[...] - (pseudo[...] * u + operator_rows)
    residual_out[...] = residual

    high, low = split(residual)
    turned = dot_nt(fixed[EYE], jnp.concatenate([high, low], axis=0))
    turned_out[...] = turned + roll(turned, 64)
    turned = turned.astype(BF16)
    trace_lane = lanes((160, 128))
    traces = jnp.zeros((160, 128), F32)
    for line in range(LINES):
        applied = dot(rows_high[line], turned) + dot(rows_low[line], turned)
        traces = jnp.where(trace_lane % 64 // 8 == line, applied, traces)
    traces = traces + roll(traces, 64)

    sent = jnp.concatenate([traces, tables[SPAN : SPAN + 56], jnp.zeros((40, 128), F32)], axis=0)
    sent_out[...] = jnp.transpose(sent)[:64]


def maps_kernel(
    received,
    fwd,
    bwd,
    z_both,
    v_high,
    v_low,
    t_out,
    w_out,
    whole_out,
    wide,
    started,
    t_state,
    w_state,
    bottoms,
    maps,
):
    turned = jnp.transpose(jnp.concatenate([received[...], jnp.zeros((64, 256), F32)], axis=0))
    jacobians = turned[160:210]
    trace_lane = lanes((160, 128))
    small_lane, small_row = lanes((80, 128)), rows((80, 128))
    for e in range(SEG):
        for k in range(SEG):
            at = e * SEG + k
            wide[e, k] = jnp.broadcast_to(jacobians[:, at : at + 1], (50, 128))
        moved = roll(turned[0:160], 80 - 8 * e)
        started[e] = jnp.where((trace_lane >= 80) & (trace_lane < 88), moved, 0.0)
        t_state[e] = jnp.where(small_lane == small_row, 1.0, 0.0)
        w_state[e] = jnp.where(lanes((80, 256)) == rows((80, 256)) + 88, 1.0, 0.0)

    def coupled(e, k, side, state):
        out = mix(lambda w, v: wide[e, k, pl.ds((w * 5 + v) * 2 + side, 1)], slabs_of(state, 16))
        return jnp.concatenate(out, axis=0)

    def forward(k, carry):
        mine = small_lane == 80 + k
        for pair in range(0, SEG, 2):
            cats = []
            for e in (pair, pair + 1):
                z_hi, z_lo = split(coupled(e, k, 0, t_state[e]))
                z_both[e, k, :, 0:128] = z_hi
                z_both[e, k, :, 128:256] = z_lo
                cats.append(jnp.concatenate([z_hi, z_lo, z_hi], axis=0))
            both = dot(fwd[:, 0:240], jnp.concatenate(cats, axis=1))
            for e, y in ((pair, both[:, :128]), (pair + 1, both[:, 128:])):
                t_state[e] = y[:80] + jnp.where(mine, started[e, 0:80], 0.0)
                bottoms[e, k] = y[80:] + jnp.where(mine, started[e, 80:160], 0.0)
        return carry

    lax.fori_loop(0, SEG, forward, 0, unroll=True)

    def backward(step, carry):
        k = SEG - 1 - step
        for e in range(SEG):
            z = [coupled(e, k, 1, w_state[e, :, half]) for half in (slice(0, 128), slice(128, 256))]
            z_hi, z_lo = split(jnp.concatenate(z, axis=1))
            v_high[e, k] = z_hi
            v_low[e, k] = z_lo
            y = dot(bwd[:, 0:240], jnp.concatenate([z_hi, z_lo, z_hi], axis=0))
            w_state[e, :, 0:128] = y[:, :128] + bottoms[e, k]
            w_state[e, :, 128:256] = y[:, 128:]
        return carry

    lax.fori_loop(0, SEG, backward, 0, unroll=True)
    for e in range(SEG):
        maps[e, :, 0:128] = w_state[e, :, 0:128]
        maps[e, :, 128:256] = w_state[e, :, 128:256] + roll(t_state[e], 40)
    compose(maps, t_out, w_out, whole_out)


def compose(maps, t_out, w_out, whole_out):
    tall_lane, tall_row = lanes((128, 128)), rows((128, 128))
    zero = jnp.zeros((48, 128), F32)
    parts = [unpack(maps[e, :, 0:128], maps[e, :, 128:256]) for e in range(SEG)]
    fixed = jnp.where((tall_row < 80) & (tall_lane == tall_row), 1.0, 0.0)
    ones = jnp.where((tall_row >= 80) & (tall_row < 88) & (tall_lane == 80), 1.0, 0.0)
    state = fixed + ones
    coupled = []
    for e in range(SEG):
        t_out[e] = jnp.concatenate(split(state[:80]), axis=1)
        y = dot(left_cat(jnp.concatenate(parts[e][:2], axis=0)), right_cat(state))
        coupled.append(y[80:])
        state = jnp.concatenate([y[:80], ones[80:]], axis=0)
    last = state[:80]
    w0 = jnp.where(tall_lane == tall_row + 88, 1.0, 0.0)
    w1 = jnp.where((tall_lane == tall_row - 40) & (tall_row < 80), 1.0, 0.0)
    for e in range(SEG - 1, -1, -1):
        w_out[e] = jnp.concatenate(split(jnp.concatenate([w0[:80], w1[:80]], axis=1)), axis=1)
        w = jnp.concatenate([right_cat(w0), right_cat(w1)], axis=1)
        y = dot(left_cat(parts[e][2]), w)
        w0 = jnp.concatenate([y[:, :128] + coupled[e], zero], axis=0)
        w1 = jnp.concatenate([y[:, 128:], zero], axis=0)
    whole_out[:, 0:128] = w0[:80]
    whole_out[:, 128:256] = w1[:80] + roll(last, 40)


def solve_kernel(*refs):
    *parts, t_in, w_in, z_both, v_high, v_low, out, wholes = refs
    groups = len(parts)
    mine = lax.axis_index("span") // SEG
    for distance, part in enumerate(parts):
        wholes[lax.rem(mine - distance + groups, groups)] = part[...]
    lane = lanes((80, 128))
    one = jnp.where(rows((128, 128)) == 80, 1.0, 0.0)
    zero = jnp.zeros((48, 128), F32)
    parts = [unpack(wholes[g, :, 0:128], wholes[g, :, 128:256]) for g in range(groups)]
    traces = [one]
    for group in range(groups - 1):
        y = dot(left_cat(parts[group][0]), right_cat(traces[-1]))
        traces.append(jnp.concatenate([y, zero], axis=0) + one)
    backs = [jnp.zeros((128, 128), F32)]
    for group in range(groups - 1, 0, -1):
        y = dot(left_cat(parts[group][1]), right_cat(traces[group]))
        y = y + dot(left_cat(parts[group][2]), right_cat(backs[0]))
        backs.insert(0, jnp.concatenate([y, zero], axis=0))
    trace, back = traces[0], backs[0]
    for group in range(1, groups):
        trace = jnp.where(mine == group, traces[group], trace)
        back = jnp.where(mine == group, backs[group], back)
    both = jnp.concatenate([trace[:88], back[:80], jnp.zeros((88, 128), F32)], axis=0)
    lower_in = dot(t_in[...].reshape(640, 256), against_both(trace))
    upper_in = dot(w_in[...].reshape(640, 512), against_both(both))
    small_lane = lane % 64
    lower = jnp.zeros((80, 128), F32)
    upper = jnp.zeros((80, 128), F32)
    for e in range(SEG):
        mine = small_lane // 8 == e
        lower = jnp.where(mine, lower_in[80 * e : 80 * e + 80], lower)
        upper = jnp.where(mine, upper_in[80 * e : 80 * e + 80], upper)
    lower, upper = lower + roll(lower, 64), upper + roll(upper, 64)
    y = jnp.concatenate([lower, jnp.ones((8, 128), F32), upper, jnp.zeros((88, 128), F32)], axis=0)
    y_both = against_both(y[:128])
    y = pair_lanes(y)
    lower = jnp.zeros((80, 128), F32)
    upper = jnp.zeros((80, 128), F32)
    for e in range(SEG):
        v_hi, v_lo = v_high[e].reshape(640, 256), v_low[e].reshape(640, 256)
        c = dot(z_both[e].reshape(640, 256), y_both)
        d = dot(v_hi, y) + dot(v_lo, y)
        for k in range(SEG):
            mine = small_lane == e * SEG + k
            lower = jnp.where(mine, c[80 * k : 80 * k + 80], lower)
            upper = jnp.where(mine, d[80 * k : 80 * k + 80], upper)
    both = jnp.concatenate([lower, upper, jnp.zeros((96, 128), F32)], axis=0)
    out[...] = jnp.transpose(both + roll(both, 64))[:64]


def finish_kernel(incoming, base, columns_high, columns_low, fixed, out):
    high, low = split(incoming[...])
    load = jnp.concatenate([high, low], axis=0)[:, 0:160]
    wide_lane = lanes((320, 128)) % 64
    total = jnp.zeros((320, 128), F32)
    for line in range(LINES):
        applied = dot_nt(columns_high[line], load) + dot_nt(columns_low[line], load)
        total = jnp.where(wide_lane // 8 == line, applied, total)
    high, low = split(total)
    twice = fixed[TWICE, 0:128]
    out[...] = base[...] + dot_nt(twice, high) + dot_nt(twice, low)


def call(kernel, out_shape, in_specs, scratch=(), limit=16, flops=0, moved=0, name=None):
    return pl.pallas_call(
        kernel,
        out_shape=out_shape,
        in_specs=in_specs,
        out_specs=jax.tree.map(lambda _: pl.BlockSpec(memory_space=pltpu.VMEM), out_shape),
        scratch_shapes=list(scratch),
        compiler_params=pltpu.CompilerParams(vmem_limit_bytes=limit * 1024 * 1024),
        cost_estimate=pl.CostEstimate(flops=flops, bytes_accessed=moved, transcendentals=0),
        name=name,
    )


VM = pl.BlockSpec(memory_space=pltpu.VMEM)
HBM = pl.BlockSpec(memory_space=pltpu.HBM)


def shape(*dims, dtype=F32):
    return jax.ShapeDtypeStruct(dims, dtype)


def on_device(
    flow_state,
    source_term,
    pseudo_time,
    volume_jacobian,
    side_jacobian,
    span_jacobian,
    line_inverse,
    mirror_face,
    edge_flip,
):
    early, fixed = (jnp.asarray(value) for value in constants())
    groups = lax.axis_size("span") // SEG

    def ring(value, axis, step):
        count = lax.axis_size(axis)
        return lax.ppermute(value, axis, [(i, (i + step) % count) for i in range(count)])

    flow = flow_state.reshape(64, 320)
    plane, up, down, last, first = call(
        pack_kernel,
        (shape(16, 320), shape(32, 320), shape(32, 320), shape(8, 320), shape(8, 320)),
        [VM],
        limit=4,
        name="pack",
    )(flow)
    with jax.named_scope("halo"):
        below, above = ring(last, "span", 1), ring(first, "span", -1)
        gy_low, gy_high = ring(up, "gy", 1), ring(down, "gy", -1)
        plane = ring(plane, "gx", 1)

    inverse = line_inverse.reshape(LINES, 320, 320)
    natural = [
        volume_jacobian.transpose(0, 3, 4, 5, 1, 2).reshape(4, 75, 2, SEG),
        side_jacobian.transpose(0, 1, 4, 5, 3, 2).reshape(LINES, 25, 4, SEG),
        span_jacobian.transpose(0, 1, 4, 5, 3, 2).reshape(LINES, 25, 2, SEG),
        mirror_face.transpose(0, 1, 3, 2).reshape(LINES, 4, SEG),
        edge_flip.transpose(0, 1, 3, 2).reshape(LINES, 4, SEG),
    ]
    rows_high, rows_low, fwd, bwd, tables = call(
        prepare_kernel,
        (
            shape(LINES, 160, 320, dtype=BF16),
            shape(LINES, 160, 320, dtype=BF16),
            shape(160, 256, dtype=BF16),
            shape(80, 256, dtype=BF16),
            shape(248, 128),
        ),
        [HBM] * 7,
        scratch=[pltpu.VMEM((LINES, 320, 320), F32), pltpu.VMEM(early.shape, BF16)]
        + [pltpu.VMEM(x.shape, x.dtype) for x in natural]
        + [pltpu.SemaphoreType.DMA((LINES + 6,))],
        limit=24,
        flops=4_000_000_000,
        moved=8_000_000,
        name="prepare",
    )(*(pltpu.with_memory_space_constraint(x, pltpu.HBM) for x in (inverse, early, *natural)))

    residual, turned, sent = call(
        sweep_kernel,
        (shape(64, 320), shape(320, 128), shape(64, 256)),
        [VM] * 12,
        scratch=[pltpu.VMEM((256, 320), F32), pltpu.VMEM((192, 640), F32)],
        limit=20,
        flops=3_000_000_000,
        moved=8_000_000,
        name="sweep",
    )(
        flow,
        plane,
        gy_low,
        gy_high,
        below,
        above,
        source_term.reshape(64, 320),
        pseudo_time.reshape(64, 320),
        tables,
        rows_high,
        rows_low,
        fixed,
    )

    within = [[SEG * g + m for m in range(SEG)] for g in range(groups)]

    def exchange(value):
        value = value.reshape(SEG, 8, 256)
        value = lax.all_to_all(value, "span", 0, 0, axis_index_groups=within, tiled=True)
        return value.reshape(64, 256)

    z_both, v_high, v_low, t_maps, w_maps, whole = call(
        maps_kernel,
        (
            shape(SEG, SEG, 80, 256, dtype=BF16),
            shape(SEG, SEG, 80, 256, dtype=BF16),
            shape(SEG, SEG, 80, 256, dtype=BF16),
            shape(SEG, 80, 256, dtype=BF16),
            shape(SEG, 80, 512, dtype=BF16),
            shape(80, 256),
        ),
        [VM] * 3,
        scratch=[
            pltpu.VMEM((SEG, SEG, 50, 128), F32),
            pltpu.VMEM((SEG, 160, 128), F32),
            pltpu.VMEM((SEG, 80, 128), F32),
            pltpu.VMEM((SEG, 80, 256), F32),
            pltpu.VMEM((SEG, SEG, 80, 128), F32),
            pltpu.VMEM((SEG, 80, 256), F32),
        ],
        limit=28,
        name="maps",
    )(exchange(sent), fwd, bwd)
    wholes = [whole] + [ring(whole, "span", SEG * distance) for distance in range(1, groups)]
    late, turned, _ = lax.optimization_barrier((inverse, turned, whole))
    base, columns_high, columns_low = call(
        base_kernel,
        (
            shape(64, 320),
            shape(LINES, 320, 160, dtype=BF16),
            shape(LINES, 320, 160, dtype=BF16),
        ),
        [HBM] + [VM] * 3,
        scratch=[pltpu.VMEM((LINES, 320, 320), F32), pltpu.SemaphoreType.DMA((LINES,))],
        limit=16,
        flops=3_000_000_000,
        moved=16_000_000,
        name="base",
    )(pltpu.with_memory_space_constraint(late, pltpu.HBM), turned, flow, fixed)
    base, columns_high, columns_low, *wholes = lax.optimization_barrier(
        (base, columns_high, columns_low, *wholes)
    )
    answers = call(
        solve_kernel,
        shape(64, 256),
        [VM] * (groups + 5),
        scratch=[pltpu.VMEM((groups, 80, 256), F32)],
        limit=24,
        name="solve",
    )(*wholes, t_maps, w_maps, z_both, v_high, v_low)
    updated = call(finish_kernel, shape(64, 320), [VM] * 5, limit=16, name="finish")(
        exchange(answers), base, columns_high, columns_low, fixed
    )
    return updated.reshape(flow_state.shape), residual.reshape(flow_state.shape)


def solution(mesh):
    lines = P("gx", "gy", "span", None)
    blocks = P("gx", "gy", "span", None, None, None)
    return jax.shard_map(
        on_device,
        mesh=mesh,
        in_specs=(lines, lines, lines, blocks, blocks, blocks, P("gx", "gy", None, None), lines, lines),
        out_specs=(lines, lines),
        check_vma=False,
    )
```

```python
import functools

import jax
import jax.numpy as jnp
import numpy as np
from jax import lax
from jax.experimental import pallas as pl
from jax.experimental.pallas import tpu as pltpu
from jax.sharding import PartitionSpec as P

LIFT = 6.0
F32 = jnp.float32
BF16 = jnp.bfloat16
LINES = 8
SEG = 8


def derivative_matrix():
    points = np.array([-1.0, -1.0 / np.sqrt(5.0), 1.0 / np.sqrt(5.0), 1.0])
    matrix = np.zeros((4, 4))
    for target in range(4):
        for source in range(4):
            if target != source:
                numerator = 1.0
                denominator = 1.0
                for other in range(4):
                    if other != source and other != target:
                        numerator *= points[target] - points[other]
                    if other != source:
                        denominator *= points[source] - points[other]
                matrix[target, source] = numerator / denominator
    for target in range(4):
        matrix[target, target] = -np.sum(matrix[target])
    return matrix


def entry(a, b, c, v):
    return ((4 * a + b) * 4 + c) * 5 + v


@functools.cache
def constants():
    select = np.zeros((1120, 320), np.float32)
    place = np.zeros((320, 800), np.float32)
    layers = np.zeros((160, 320), np.float32)
    for v in range(5):
        for a in range(4):
            for b in range(4):
                for c in range(4):
                    row = v * 64 + a * 16 + b * 4 + c
                    select[row, entry(a, b, c, v)] = 1
                    place[entry(a, b, c, v), row] = 1
        for e in range(4):
            for c in range(4):
                row = v * 16 + e * 4 + c
                for side, plane in enumerate((0, 3)):
                    for flip in range(2):
                        along = 3 - e if flip else e
                        block = (side * 2 + flip) * 80
                        select[320 + block + row, entry(plane, along, c, v)] = 1
                        select[640 + block + row, entry(along, plane, c, v)] = 1
                    place[entry(plane, e, c, v), 320 + 80 * side + row] = -1
                    place[entry(e, plane, c, v), 480 + 80 * side + row] = -1
        for a in range(4):
            for b in range(4):
                row = v * 16 + a * 4 + b
                select[960 + row, entry(a, b, 3, v)] = 1
                select[1040 + row, entry(a, b, 0, v)] = 1
                place[entry(a, b, 0, v), 640 + row] = -1
                place[entry(a, b, 3, v), 720 + row] = -1
                layers[row, entry(a, b, 3, v)] = 1
                layers[80 + row, entry(a, b, 0, v)] = 1
    top, bottom = layers[:80].T, layers[80:].T
    columns_high = np.zeros((320, 512), np.float32)
    columns_low = np.zeros((320, 512), np.float32)
    for base, chosen in ((0, bottom), (256, top)):
        columns_high[:, base : base + 80] = chosen
        columns_high[:, base + 80 : base + 160] = chosen
        columns_low[:, base + 160 : base + 240] = chosen
    spread = np.concatenate([bottom, top], axis=1)
    eye, d = np.eye(4), derivative_matrix()
    along = np.concatenate(
        [
            np.kron(np.kron(d, eye), eye),
            np.kron(np.kron(eye, d), eye),
            np.kron(np.kron(eye, eye), d),
        ],
        axis=1,
    )
    high = along.astype(jnp.bfloat16).astype(np.float64)
    along = np.concatenate([high, high, along - high], axis=1)
    twice = np.concatenate([np.eye(64), np.eye(64)], axis=1)
    eye_320 = np.eye(320)
    blocks = [
        select,
        place[:, :320],
        place[:, 320:640],
        place[:, 640:],
        along[:, :192],
        along[:, 384:],
        twice,
        eye_320,
        spread,
        layers,
    ]
    fixed = np.zeros((sum(len(block) for block in blocks), 320), np.float32)
    at = 0
    for block in blocks:
        fixed[at : at + len(block), : block.shape[1]] = block
        at += len(block)
    early = np.zeros((800, 512), np.float32)
    early[:320], early[320:640], early[640:, :320] = columns_high, columns_low, layers
    return early.astype(jnp.bfloat16), fixed.astype(jnp.bfloat16)


SELECT_VOLUME, SELECT_A, SELECT_B, SELECT_LAYERS = (
    slice(0, 320),
    slice(320, 640),
    slice(640, 960),
    slice(960, 1120),
)
SELECT, PLACE_A, PLACE_B, PLACE_C = slice(0, 1120), slice(1120, 1440), slice(1440, 1760), slice(1760, 2080)
ALONG, ALONG_HIGH, ALONG_LOW = slice(2080, 2208), slice(2080, 2144), slice(2144, 2208)
TWICE = slice(2208, 2272)
EYE, SPREAD, LAYERS = slice(2272, 2592), slice(2592, 2912), slice(2912, 3072)
SIDE, SPAN, MIRROR, FLIP = 80, 184, 240, 244


def dot(a, b):
    return lax.dot_general(a, b, (((1,), (0,)), ((), ())), preferred_element_type=F32)


def dot_nt(a, b):
    return lax.dot_general(a, b, (((1,), (1,)), ((), ())), preferred_element_type=F32)


def split(x):
    high = x.astype(BF16)
    return high, (x - high.astype(F32)).astype(BF16)


def split_3(x):
    high = x.astype(BF16)
    rest = x - high.astype(F32)
    middle = rest.astype(BF16)
    return high, middle, (rest - middle.astype(F32)).astype(BF16)


def lanes(shape):
    return lax.broadcasted_iota(jnp.int32, shape, len(shape) - 1)


def rows(shape):
    return lax.broadcasted_iota(jnp.int32, shape, len(shape) - 2)


def roll(x, amount):
    return pltpu.roll(x, amount % 128, 1)


def pair_lanes(x):
    high = x.astype(BF16).astype(F32)
    return jnp.where(lanes(x.shape) < 64, high, roll(x - high, 64)).astype(BF16)


def against_both(x):
    paired = pair_lanes(x)
    first = jnp.where(lanes(x.shape) < 64, paired.astype(F32), 0.0).astype(BF16)
    return jnp.concatenate([paired, first], axis=0)


def left_cat(x):
    high, low = split(x)
    return jnp.concatenate([high, high, low], axis=1)


def right_cat(x):
    high, low = split(x)
    return jnp.concatenate([high, low, high], axis=0)


def pack_kernel(flow, plane_out, up_out, down_out, last_out, first_out):
    at = pl.multiple_of((1 - lax.axis_index("gx")) * 48, 16)
    plane_out[...] = flow[pl.ds(at, 16)]
    for i in range(4):
        down_out[8 * i : 8 * i + 8] = flow[16 * i : 16 * i + 8]
        up_out[8 * i : 8 * i + 8] = flow[16 * i + 8 : 16 * i + 16]
    for line in range(LINES):
        first_out[line : line + 1] = flow[8 * line : 8 * line + 1]
        last_out[line : line + 1] = flow[8 * line + 7 : 8 * line + 8]


def prepare_kernel(
    inverse,
    early_in,
    fixed_in,
    flow_in,
    volume_in,
    side_in,
    span_in,
    mirror_in,
    flip_in,
    high_out,
    low_out,
    rows_high,
    rows_low,
    fwd_out,
    bwd_out,
    tables,
    own_out,
    volume_out,
    held,
    early,
    fixed,
    flow,
    volume_jacobian,
    side_jacobian,
    span_jacobian,
    mirror_face,
    edge_flip,
    flux,
    arrived,
):
    pairs = [
        (volume_in, volume_jacobian),
        (side_in, side_jacobian),
        (span_in, span_jacobian),
        (mirror_in, mirror_face),
        (flip_in, edge_flip),
        (flow_in, flow),
        (fixed_in.at[SELECT], fixed.at[SELECT]),
        (fixed_in.at[ALONG], fixed.at[ALONG]),
    ]
    pairs += [(inverse.at[lax.rem(lax.axis_index("span"), LINES)], held), (early_in, early)]
    copies = [
        pltpu.make_async_copy(source, target, arrived.at[at])
        for at, (source, target) in enumerate(pairs)
    ]
    for copy in copies:
        copy.start()
    for copy in copies[:5]:
        copy.wait()
    for line in range(LINES):
        here = slice(8 * line, 8 * line + 8)
        tables[0:75, here] = volume_jacobian[line // 2, :, line % 2, :]
        tables[SIDE : SIDE + 100, here] = side_jacobian[line].reshape(100, 8)
        tables[SPAN : SPAN + 50, here] = LIFT * span_jacobian[line].reshape(50, 8)
        tables[MIRROR : MIRROR + 4, here] = mirror_face[line].astype(F32)
        tables[FLIP : FLIP + 4, here] = edge_flip[line].astype(F32)
    for copy in copies[5:8]:
        copy.wait()

    padded = jnp.concatenate([flow[...], jnp.zeros((64, 320), F32)], axis=0)
    own = sum(dot_nt(fixed[SELECT], part) for part in split(padded))
    own_out[...] = own[320:]
    by_variable = slabs_of(own[0:320], 64)
    for d in range(3):
        mixed = mix(lambda w, v: tables[d * 25 + w * 5 + v : d * 25 + w * 5 + v + 1, :], by_variable)
        for w in range(5):
            flux[d * 64 : d * 64 + 64, w * 128 : w * 128 + 128] = mixed[w]
    flux_high, flux_low = split(flux[...])
    volume = dot(fixed[ALONG_HIGH, 0:192], flux_high) + dot(fixed[ALONG_HIGH, 0:192], flux_low)
    volume = volume + dot(fixed[ALONG_LOW, 0:192], flux_high)
    for w in range(5):
        volume_out[w * 64 : w * 64 + 64] = volume[:, w * 128 : w * 128 + 128]

    for copy in copies[8:]:
        copy.wait()
    high_out[...], low_out[...] = split(held[...])
    layers = early[640:800, 0:320]
    rows_high[...] = dot(layers, high_out[...]).astype(BF16)
    rows_low[...] = dot(layers, low_out[...]).astype(BF16)
    both = dot(rows_high[...], early[0:320]) + dot(rows_low[...], early[320:640])
    both = both.astype(BF16)
    fwd_out[...] = both[:, :256]
    bwd_out[...] = both[80:, 256:]


def unpack(left, right):
    lane = lanes((80, 128))
    forward = jnp.where(lane < 88, roll(right, 88), 0.0)
    cross = jnp.where(lane < 88, left, 0.0)
    back = jnp.where(lane < 40, roll(left, 40), jnp.where(lane < 80, roll(right, 40), 0.0))
    return forward, cross, back


def mix(coefficient, slabs):
    out = []
    for w in range(5):
        total = coefficient(w, 0) * slabs[0]
        for v in range(1, 5):
            total = total + coefficient(w, v) * slabs[v]
        out.append(total)
    return out


def slabs_of(x, size):
    return [x[v * size : (v + 1) * size] for v in range(5)]


def sweep_kernel(
    flow,
    plane,
    gy_low,
    gy_high,
    below,
    above,
    source,
    pseudo,
    tables,
    own_in,
    volume_in,
    fixed,
    residual_out,
    sent_out,
    extended,
):
    gx_at, gy_at = lax.axis_index("gx"), lax.axis_index("gy")
    first_lo = (gx_at > 0).astype(F32)
    second_lo = (gy_at > 0).astype(F32)
    second_hi = (gy_at < lax.axis_size("gy") - 1).astype(F32)
    u = flow[...]
    nothing = jnp.zeros((64, 320), F32)
    extended[0:64] = nothing
    extended[64:80] = plane[...] * (1.0 - first_lo)
    extended[80:112] = nothing[:32]
    extended[112:128] = plane[...] * first_lo
    for i in range(4):
        extended[128 + 16 * i : 136 + 16 * i] = gy_low[8 * i : 8 * i + 8] * second_lo
        extended[136 + 16 * i : 144 + 16 * i] = gy_high[8 * i : 8 * i + 8] * second_hi
    extended[192:256] = nothing
    position = rows((8, 320))
    for line in range(LINES):
        extended[256 + 8 * line : 264 + 8 * line] = jnp.where(
            position == 0,
            below[line : line + 1],
            jnp.where(position == 7, above[line : line + 1], 0.0),
        )
    extended[320:384] = nothing

    def outside(chosen, at):
        return sum(dot_nt(fixed[chosen], part) for part in split(extended[at : at + 128]))

    near_a = own_in[0:320] + outside(SELECT_A, 0)
    near_b, far_b = own_in[320:640], outside(SELECT_B, 128)
    far_layers = outside(SELECT_LAYERS, 256)
    lane = lanes((1, 128))
    table = lambda r: tables[r : r + 1, :]
    pieces = []

    for f in range(4):
        near = near_a if f < 2 else near_b
        candidates = [near[80 * n : 80 * n + 80] for n in range(4)]
        outer = [far_b[80 * n : 80 * n + 80] for n in range(4)]
        own = candidates[2 * (f % 2)]
        if f == 0:
            shifted = [roll(x, 16) for x in candidates]
        elif f == 1:
            shifted = [roll(x, -16) for x in candidates]
        elif f == 2:
            shifted = [
                jnp.where((lane // 8) % 2 == 1, roll(x, 8), y) for x, y in zip(candidates, outer)
            ]
        else:
            shifted = [
                jnp.where((lane // 8) % 2 == 0, roll(x, -8), y) for x, y in zip(candidates, outer)
            ]
        mirrored = table(MIRROR + f) > 0.5
        flipped = table(FLIP + f) > 0.5
        neighbour = jnp.where(
            flipped,
            jnp.where(mirrored, shifted[3], shifted[1]),
            jnp.where(mirrored, shifted[2], shifted[0]),
        )
        jump = LIFT * (neighbour - own)
        pieces += mix(lambda w, v: table(SIDE + (w * 5 + v) * 4 + f), slabs_of(jump, 16))

    top, bottom = own_in[640:720], own_in[720:800]
    outer_top, outer_bottom = far_layers[0:80], far_layers[80:160]
    lower_jump = jnp.where(lane % 8 == 0, outer_top, roll(top, 1)) - bottom
    upper_jump = jnp.where(lane % 8 == 7, outer_bottom, roll(bottom, -1)) - top
    pieces += mix(lambda w, v: table(SPAN + (w * 5 + v) * 2), slabs_of(lower_jump, 16))
    pieces += mix(lambda w, v: table(SPAN + (w * 5 + v) * 2 + 1), slabs_of(upper_jump, 16))
    pieces = [
        pair_lanes(volume_in[...]),
        pair_lanes(jnp.concatenate(pieces[:20], axis=0)),
        pair_lanes(jnp.concatenate(pieces[20:], axis=0)),
    ]
    operator = dot(fixed[PLACE_A], pieces[0]) + dot(fixed[PLACE_B], pieces[1])
    operator = operator + dot(fixed[PLACE_C, 0:160], pieces[2])
    operator_high, operator_low = split(operator)
    twice = fixed[TWICE, 0:128]
    operator_rows = dot_nt(twice, operator_high) + dot_nt(twice, operator_low)
    residual = source[...] - (pseudo[...] * u + operator_rows)
    residual_out[...] = residual

    turned = [jnp.zeros((64, 128), F32), tables[SPAN : SPAN + 56], jnp.zeros((8, 128), F32)]
    sent_out[:, 256:384] = jnp.transpose(jnp.concatenate(turned, axis=0))[:64]
    sent_out[:, 0:320] = residual


def maps_kernel(
    received,
    rows_high,
    rows_low,
    fwd,
    bwd,
    fixed,
    z_both,
    v_both,
    t_out,
    w_out,
    whole_out,
    turned_out,
    wide,
    started,
    t_state,
    w_state,
    bottoms,
    maps,
):
    last = jnp.concatenate([received[:, 256:384], jnp.zeros((64, 128), F32)], axis=0)
    jacobians = jnp.transpose(last)[64:114]
    high, low = split(received[:, 0:320])
    turned = dot_nt(fixed[EYE], jnp.concatenate([high, low], axis=0))
    turned_out[...] = turned + roll(turned, 64)
    turned = turned.astype(BF16)
    traces = dot(rows_high[...], turned) + dot(rows_low[...], turned)
    traces = traces + roll(traces, 64)
    trace_lane = lanes((160, 128))
    small_lane, small_row = lanes((80, 128)), rows((80, 128))
    for e in range(SEG):
        for k in range(SEG):
            at = e * SEG + k
            wide[e, k] = jnp.broadcast_to(jacobians[:, at : at + 1], (50, 128))
        moved = roll(traces, 80 - 8 * e)
        started[e] = jnp.where((trace_lane >= 80) & (trace_lane < 88), moved, 0.0)
        t_state[e] = jnp.where(small_lane == small_row, 1.0, 0.0)
        w_state[e] = jnp.where(lanes((80, 256)) == rows((80, 256)) + 88, 1.0, 0.0)

    def coupled(e, k, side, state):
        out = mix(lambda w, v: wide[e, k, pl.ds((w * 5 + v) * 2 + side, 1)], slabs_of(state, 16))
        return jnp.concatenate(out, axis=0)

    def forward(k, carry):
        mine = small_lane == 80 + k
        for pair in range(0, SEG, 2):
            cats = []
            for e in (pair, pair + 1):
                z_hi, z_lo = split(coupled(e, k, 0, t_state[e]))
                z_both[e, k, :, 0:128] = z_hi
                z_both[e, k, :, 128:256] = z_lo
                cats.append(jnp.concatenate([z_hi, z_lo, z_hi], axis=0))
            both = dot(fwd[:, 0:240], jnp.concatenate(cats, axis=1))
            for e, y in ((pair, both[:, :128]), (pair + 1, both[:, 128:])):
                t_state[e] = y[:80] + jnp.where(mine, started[e, 0:80], 0.0)
                bottoms[e, k] = y[80:] + jnp.where(mine, started[e, 80:160], 0.0)
        return carry

    lax.fori_loop(0, SEG, forward, 0, unroll=True)

    def backward(step, carry):
        k = SEG - 1 - step
        for e in range(SEG):
            z = [coupled(e, k, 1, w_state[e, :, half]) for half in (slice(0, 128), slice(128, 256))]
            z_hi, z_lo = split(jnp.concatenate(z, axis=1))
            v_both[e, k, :, 0:256] = z_hi
            v_both[e, k, :, 256:512] = z_lo
            y = dot(bwd[:, 0:240], jnp.concatenate([z_hi, z_lo, z_hi], axis=0))
            w_state[e, :, 0:128] = y[:, :128] + bottoms[e, k]
            w_state[e, :, 128:256] = y[:, 128:]
        return carry

    lax.fori_loop(0, SEG, backward, 0, unroll=True)
    for e in range(SEG):
        maps[e, :, 0:128] = w_state[e, :, 0:128]
        maps[e, :, 128:256] = w_state[e, :, 128:256] + roll(t_state[e], 40)
    compose(maps, t_out, w_out, whole_out)


def compose(maps, t_out, w_out, whole_out):
    tall_lane, tall_row = lanes((128, 128)), rows((128, 128))
    zero = jnp.zeros((48, 128), F32)
    parts = [unpack(maps[e, :, 0:128], maps[e, :, 128:256]) for e in range(SEG)]
    fixed = jnp.where((tall_row < 80) & (tall_lane == tall_row), 1.0, 0.0)
    ones = jnp.where((tall_row >= 80) & (tall_row < 88) & (tall_lane == 80), 1.0, 0.0)
    state = fixed + ones
    coupled = []
    for e in range(SEG):
        t_out[e] = jnp.concatenate(split(state[:80]), axis=1)
        y = dot(left_cat(jnp.concatenate(parts[e][:2], axis=0)), right_cat(state))
        coupled.append(y[80:])
        state = jnp.concatenate([y[:80], ones[80:]], axis=0)
    last = state[:80]
    w0 = jnp.where(tall_lane == tall_row + 88, 1.0, 0.0)
    w1 = jnp.where((tall_lane == tall_row - 40) & (tall_row < 80), 1.0, 0.0)
    for e in range(SEG - 1, -1, -1):
        w_out[e] = jnp.concatenate(split(jnp.concatenate([w0[:80], w1[:80]], axis=1)), axis=1)
        w = jnp.concatenate([right_cat(w0), right_cat(w1)], axis=1)
        y = dot(left_cat(parts[e][2]), w)
        w0 = jnp.concatenate([y[:, :128] + coupled[e], zero], axis=0)
        w1 = jnp.concatenate([y[:, 128:], zero], axis=0)
    whole_out[:, 0:128] = w0[:80]
    whole_out[:, 128:256] = w1[:80] + roll(last, 40)


def solve_kernel(*refs):
    *parts, t_in, w_in, z_both, v_both, turned, high, low, fixed, out, wholes = refs
    groups = len(parts)
    mine = lax.axis_index("span") // SEG
    for distance, part in enumerate(parts):
        wholes[lax.rem(mine - distance + groups, groups)] = part[...]
    lane = lanes((80, 128))
    one = jnp.where(rows((128, 128)) == 80, 1.0, 0.0)
    zero = jnp.zeros((48, 128), F32)
    parts = [unpack(wholes[g, :, 0:128], wholes[g, :, 128:256]) for g in range(groups)]
    traces = [one]
    for group in range(groups - 1):
        y = dot(left_cat(parts[group][0]), right_cat(traces[-1]))
        traces.append(jnp.concatenate([y, zero], axis=0) + one)
    backs = [jnp.zeros((128, 128), F32)]
    for group in range(groups - 1, 0, -1):
        y = dot(left_cat(parts[group][1]), right_cat(traces[group]))
        y = y + dot(left_cat(parts[group][2]), right_cat(backs[0]))
        backs.insert(0, jnp.concatenate([y, zero], axis=0))
    trace, back = traces[0], backs[0]
    for group in range(1, groups):
        trace = jnp.where(mine == group, traces[group], trace)
        back = jnp.where(mine == group, backs[group], back)
    both = jnp.concatenate([trace[:88], back[:80], jnp.zeros((88, 128), F32)], axis=0)
    lower_in = dot(t_in[...].reshape(640, 256), against_both(trace))
    upper_in = dot(w_in[...].reshape(640, 512), against_both(both))
    small_lane = lane % 64
    lower = jnp.zeros((80, 128), F32)
    upper = jnp.zeros((80, 128), F32)
    for e in range(SEG):
        mine = small_lane // 8 == e
        lower = jnp.where(mine, lower_in[80 * e : 80 * e + 80], lower)
        upper = jnp.where(mine, upper_in[80 * e : 80 * e + 80], upper)
    lower, upper = lower + roll(lower, 64), upper + roll(upper, 64)
    y = jnp.concatenate([lower, jnp.ones((8, 128), F32), upper, jnp.zeros((88, 128), F32)], axis=0)
    y_both, y_all = against_both(y[:128]), against_both(y)
    lower = jnp.zeros((80, 128), F32)
    upper = jnp.zeros((80, 128), F32)
    for e in range(SEG):
        c = dot(z_both[e].reshape(640, 256), y_both)
        d = dot(v_both[e].reshape(640, 512), y_all)
        for k in range(SEG):
            mine = small_lane == e * SEG + k
            lower = jnp.where(mine, c[80 * k : 80 * k + 80], lower)
            upper = jnp.where(mine, d[80 * k : 80 * k + 80], upper)
    both = jnp.concatenate([lower, upper], axis=0)
    added = dot(fixed[SPREAD, 0:160], pair_lanes(both + roll(both, 64)))
    load = pair_lanes(turned[...] + added + roll(added, 64))
    total_high, total_low = split(dot(high[...], load) + dot(low[...], load))
    twice = fixed[TWICE, 0:128]
    out[:, 0:320] = dot_nt(twice, total_high) + dot_nt(twice, total_low)
    out[:, 320:384] = jnp.zeros((64, 64), F32)


def finish_kernel(incoming, flow, out):
    out[...] = flow[...] + incoming[:, 0:320]


def call(kernel, out_shape, in_specs, scratch=(), limit=16, flops=0, moved=0, name=None):
    return pl.pallas_call(
        kernel,
        out_shape=out_shape,
        in_specs=in_specs,
        out_specs=jax.tree.map(lambda _: pl.BlockSpec(memory_space=pltpu.VMEM), out_shape),
        scratch_shapes=list(scratch),
        compiler_params=pltpu.CompilerParams(vmem_limit_bytes=limit * 1024 * 1024),
        cost_estimate=pl.CostEstimate(flops=flops, bytes_accessed=moved, transcendentals=0),
        name=name,
    )


VM = pl.BlockSpec(memory_space=pltpu.VMEM)
HBM = pl.BlockSpec(memory_space=pltpu.HBM)


def shape(*dims, dtype=F32):
    return jax.ShapeDtypeStruct(dims, dtype)


def on_device(
    flow_state,
    source_term,
    pseudo_time,
    volume_jacobian,
    side_jacobian,
    span_jacobian,
    line_inverse,
    mirror_face,
    edge_flip,
):
    early, fixed = (jnp.asarray(value) for value in constants())
    groups = lax.axis_size("span") // SEG

    def ring(value, axis, step):
        count = lax.axis_size(axis)
        return lax.ppermute(value, axis, [(i, (i + step) % count) for i in range(count)])

    flow = flow_state.reshape(64, 320)
    plane, up, down, last, first = call(
        pack_kernel,
        (shape(16, 320), shape(32, 320), shape(32, 320), shape(8, 320), shape(8, 320)),
        [VM],
        limit=4,
        name="pack",
    )(flow)
    with jax.named_scope("halo"):
        below, above = ring(last, "span", 1), ring(first, "span", -1)
        gy_low, gy_high = ring(up, "gy", 1), ring(down, "gy", -1)
        plane = ring(plane, "gx", 1)

    inverse = line_inverse.reshape(LINES, 320, 320)
    natural = [
        volume_jacobian.transpose(0, 3, 4, 5, 1, 2).reshape(4, 75, 2, SEG),
        side_jacobian.transpose(0, 1, 4, 5, 3, 2).reshape(LINES, 25, 4, SEG),
        span_jacobian.transpose(0, 1, 4, 5, 3, 2).reshape(LINES, 25, 2, SEG),
        mirror_face.transpose(0, 1, 3, 2).reshape(LINES, 4, SEG),
        edge_flip.transpose(0, 1, 3, 2).reshape(LINES, 4, SEG),
    ]
    high, low, rows_high, rows_low, fwd, bwd, tables, own, volume = call(
        prepare_kernel,
        (
            shape(320, 320, dtype=BF16),
            shape(320, 320, dtype=BF16),
            shape(160, 320, dtype=BF16),
            shape(160, 320, dtype=BF16),
            shape(160, 256, dtype=BF16),
            shape(80, 256, dtype=BF16),
            shape(248, 128),
            shape(800, 128),
            shape(320, 128),
        ),
        [HBM] * 9,
        scratch=[
            pltpu.VMEM((320, 320), F32),
            pltpu.VMEM(early.shape, BF16),
            pltpu.VMEM(fixed.shape, BF16),
            pltpu.VMEM(flow.shape, F32),
        ]
        + [pltpu.VMEM(x.shape, x.dtype) for x in natural]
        + [pltpu.VMEM((192, 640), F32), pltpu.SemaphoreType.DMA((10,))],
        limit=28,
        flops=4_000_000_000,
        moved=8_000_000,
        name="prepare",
    )(
        *(
            pltpu.with_memory_space_constraint(x, pltpu.HBM)
            for x in (inverse, early, fixed, flow, *natural)
        )
    )

    residual, sent = call(
        sweep_kernel,
        (shape(64, 320), shape(64, 384)),
        [VM] * 12,
        scratch=[pltpu.VMEM((384, 320), F32)],
        limit=24,
        flops=3_000_000_000,
        moved=8_000_000,
        name="sweep",
    )(
        flow,
        plane,
        gy_low,
        gy_high,
        below,
        above,
        source_term.reshape(64, 320),
        pseudo_time.reshape(64, 320),
        tables,
        own,
        volume,
        fixed,
    )

    within = [[SEG * g + m for m in range(SEG)] for g in range(groups)]

    def exchange(value):
        value = value.reshape(SEG, 8, 384)
        value = lax.all_to_all(value, "span", 0, 0, axis_index_groups=within, tiled=True)
        return value.reshape(64, 384)

    z_both, v_both, t_maps, w_maps, whole, turned = call(
        maps_kernel,
        (
            shape(SEG, SEG, 80, 256, dtype=BF16),
            shape(SEG, SEG, 80, 512, dtype=BF16),
            shape(SEG, 80, 256, dtype=BF16),
            shape(SEG, 80, 512, dtype=BF16),
            shape(80, 256),
            shape(320, 128),
        ),
        [VM] * 6,
        scratch=[
            pltpu.VMEM((SEG, SEG, 50, 128), F32),
            pltpu.VMEM((SEG, 160, 128), F32),
            pltpu.VMEM((SEG, 80, 128), F32),
            pltpu.VMEM((SEG, 80, 256), F32),
            pltpu.VMEM((SEG, SEG, 80, 128), F32),
            pltpu.VMEM((SEG, 80, 256), F32),
        ],
        limit=28,
        name="maps",
    )(exchange(sent), rows_high, rows_low, fwd, bwd, fixed)
    wholes = [whole] + [ring(whole, "span", SEG * distance) for distance in range(1, groups)]
    answers = call(
        solve_kernel,
        shape(64, 384),
        [VM] * (groups + 8),
        scratch=[pltpu.VMEM((groups, 80, 256), F32)],
        limit=24,
        name="solve",
    )(*wholes, t_maps, w_maps, z_both, v_both, turned, high, low, fixed)
    updated = call(finish_kernel, shape(64, 320), [VM] * 2, limit=4, name="finish")(
        exchange(answers), flow
    )
    return updated.reshape(flow_state.shape), residual.reshape(flow_state.shape)


def solution(mesh):
    lines = P("gx", "gy", "span", None)
    blocks = P("gx", "gy", "span", None, None, None)
    return jax.shard_map(
        on_device,
        mesh=mesh,
        in_specs=(lines, lines, lines, blocks, blocks, blocks, P("gx", "gy", None, None), lines, lines),
        out_specs=(lines, lines),
        check_vma=False,
    )
```

```python
import functools

import jax
import jax.numpy as jnp
import numpy as np
from jax import lax
from jax.experimental import pallas as pl
from jax.experimental.pallas import tpu as pltpu
from jax.sharding import PartitionSpec as P

LIFT = 6.0
F32 = jnp.float32
BF16 = jnp.bfloat16
LINES = 8
SEG = 8


def derivative_matrix():
    points = np.array([-1.0, -1.0 / np.sqrt(5.0), 1.0 / np.sqrt(5.0), 1.0])
    matrix = np.zeros((4, 4))
    for target in range(4):
        for source in range(4):
            if target != source:
                numerator = 1.0
                denominator = 1.0
                for other in range(4):
                    if other != source and other != target:
                        numerator *= points[target] - points[other]
                    if other != source:
                        denominator *= points[source] - points[other]
                matrix[target, source] = numerator / denominator
    for target in range(4):
        matrix[target, target] = -np.sum(matrix[target])
    return matrix


def entry(a, b, c, v):
    return ((4 * a + b) * 4 + c) * 5 + v


@functools.cache
def constants():
    select = np.zeros((1120, 320), np.float32)
    place = np.zeros((320, 800), np.float32)
    layers = np.zeros((160, 320), np.float32)
    for v in range(5):
        for a in range(4):
            for b in range(4):
                for c in range(4):
                    row = v * 64 + a * 16 + b * 4 + c
                    select[row, entry(a, b, c, v)] = 1
                    place[entry(a, b, c, v), row] = 1
        for e in range(4):
            for c in range(4):
                row = v * 16 + e * 4 + c
                for side, plane in enumerate((0, 3)):
                    for flip in range(2):
                        along = 3 - e if flip else e
                        block = (side * 2 + flip) * 80
                        select[320 + block + row, entry(plane, along, c, v)] = 1
                        select[640 + block + row, entry(along, plane, c, v)] = 1
                    place[entry(plane, e, c, v), 320 + 80 * side + row] = -1
                    place[entry(e, plane, c, v), 480 + 80 * side + row] = -1
        for a in range(4):
            for b in range(4):
                row = v * 16 + a * 4 + b
                select[960 + row, entry(a, b, 3, v)] = 1
                select[1040 + row, entry(a, b, 0, v)] = 1
                place[entry(a, b, 0, v), 640 + row] = -1
                place[entry(a, b, 3, v), 720 + row] = -1
                layers[row, entry(a, b, 3, v)] = 1
                layers[80 + row, entry(a, b, 0, v)] = 1
    top, bottom = layers[:80].T, layers[80:].T
    columns_high = np.zeros((320, 512), np.float32)
    columns_low = np.zeros((320, 512), np.float32)
    for base, chosen in ((0, bottom), (256, top)):
        columns_high[:, base : base + 80] = chosen
        columns_high[:, base + 80 : base + 160] = chosen
        columns_low[:, base + 160 : base + 240] = chosen
    spread = np.zeros((320, 256))
    spread[:, :80], spread[:, 128:208] = bottom, top
    eye, d = np.eye(4), derivative_matrix()
    along = np.concatenate(
        [
            np.kron(np.kron(d, eye), eye),
            np.kron(np.kron(eye, d), eye),
            np.kron(np.kron(eye, eye), d),
        ],
        axis=1,
    )
    high = along.astype(jnp.bfloat16).astype(np.float64)
    along = np.concatenate([high, high, along - high], axis=1)
    twice = np.concatenate([np.eye(64), np.eye(64)], axis=1)
    ordered = np.zeros((64, 128))
    for e in range(8):
        for k in range(8):
            ordered[8 * e + k, [8 * k + e, 64 + 8 * k + e]] = 1
    eye_320 = np.eye(320)
    blocks = [
        select,
        place[:, :320],
        place[:, 320:640],
        place[:, 640:],
        along[:, :192],
        along[:, 384:],
        twice,
        eye_320,
        spread,
        layers,
        ordered,
    ]
    fixed = np.zeros((sum(len(block) for block in blocks), 320), np.float32)
    at = 0
    for block in blocks:
        fixed[at : at + len(block), : block.shape[1]] = block
        at += len(block)
    early = np.zeros((800, 512), np.float32)
    early[:320], early[320:640], early[640:, :320] = columns_high, columns_low, layers
    return early.astype(jnp.bfloat16), fixed.astype(jnp.bfloat16)


SELECT_VOLUME, SELECT_A, SELECT_B, SELECT_LAYERS = (
    slice(0, 320),
    slice(320, 640),
    slice(640, 960),
    slice(960, 1120),
)
SELECT, PLACE_A, PLACE_B, PLACE_C = slice(0, 1120), slice(1120, 1440), slice(1440, 1760), slice(1760, 2080)
ALONG, ALONG_HIGH, ALONG_LOW = slice(2080, 2208), slice(2080, 2144), slice(2144, 2208)
TWICE = slice(2208, 2272)
EYE, SPREAD, LAYERS = slice(2272, 2592), slice(2592, 2912), slice(2912, 3072)
ORDERED = slice(3072, 3136)
SIDE, SPAN, MIRROR, FLIP = 80, 184, 240, 244


def dot(a, b):
    return lax.dot_general(a, b, (((1,), (0,)), ((), ())), preferred_element_type=F32)


def dot_nt(a, b):
    return lax.dot_general(a, b, (((1,), (1,)), ((), ())), preferred_element_type=F32)


def split(x):
    high = x.astype(BF16)
    return high, (x - high.astype(F32)).astype(BF16)


def split_3(x):
    high = x.astype(BF16)
    rest = x - high.astype(F32)
    middle = rest.astype(BF16)
    return high, middle, (rest - middle.astype(F32)).astype(BF16)


def lanes(shape):
    return lax.broadcasted_iota(jnp.int32, shape, len(shape) - 1)


def rows(shape):
    return lax.broadcasted_iota(jnp.int32, shape, len(shape) - 2)


def roll(x, amount):
    return pltpu.roll(x, amount % 128, 1)


def pair_lanes(x):
    high = x.astype(BF16).astype(F32)
    return jnp.where(lanes(x.shape) < 64, high, roll(x - high, 64)).astype(BF16)


def left_cat(x):
    high, low = split(x)
    return jnp.concatenate([high, high, low], axis=1)


def right_cat(x):
    high, low = split(x)
    return jnp.concatenate([high, low, high], axis=0)


def pack_kernel(flow, plane_out, up_out, down_out, last_out, first_out):
    at = pl.multiple_of((1 - lax.axis_index("gx")) * 48, 16)
    plane_out[...] = flow[pl.ds(at, 16)]
    for i in range(4):
        down_out[8 * i : 8 * i + 8] = flow[16 * i : 16 * i + 8]
        up_out[8 * i : 8 * i + 8] = flow[16 * i + 8 : 16 * i + 16]
    for line in range(LINES):
        first_out[line : line + 1] = flow[8 * line : 8 * line + 1]
        last_out[line : line + 1] = flow[8 * line + 7 : 8 * line + 8]


def prepare_kernel(
    inverse,
    early_in,
    fixed_in,
    flow_in,
    volume_in,
    side_in,
    span_in,
    mirror_in,
    flip_in,
    high_out,
    low_out,
    rows_high,
    rows_low,
    fwd_out,
    bwd_out,
    tables,
    own_out,
    volume_out,
    held,
    early,
    fixed,
    flow,
    volume_jacobian,
    side_jacobian,
    span_jacobian,
    mirror_face,
    edge_flip,
    flux,
    arrived,
):
    pairs = [
        (volume_in, volume_jacobian),
        (side_in, side_jacobian),
        (span_in, span_jacobian),
        (mirror_in, mirror_face),
        (flip_in, edge_flip),
        (flow_in, flow),
        (fixed_in.at[SELECT], fixed.at[SELECT]),
        (fixed_in.at[ALONG], fixed.at[ALONG]),
    ]
    pairs += [(inverse.at[lax.rem(lax.axis_index("span"), LINES)], held), (early_in, early)]
    copies = [
        pltpu.make_async_copy(source, target, arrived.at[at])
        for at, (source, target) in enumerate(pairs)
    ]
    for copy in copies:
        copy.start()
    for copy in copies[:5]:
        copy.wait()
    for line in range(LINES):
        here = slice(8 * line, 8 * line + 8)
        tables[0:75, here] = volume_jacobian[line // 2, :, line % 2, :]
        tables[SIDE : SIDE + 100, here] = side_jacobian[line].reshape(100, 8)
        tables[SPAN : SPAN + 50, here] = LIFT * span_jacobian[line].reshape(50, 8)
        tables[MIRROR : MIRROR + 4, here] = mirror_face[line].astype(F32)
        tables[FLIP : FLIP + 4, here] = edge_flip[line].astype(F32)
    for copy in copies[5:8]:
        copy.wait()

    padded = jnp.concatenate([flow[...], jnp.zeros((64, 320), F32)], axis=0)
    own = sum(dot_nt(fixed[SELECT], part) for part in split(padded))
    own_out[...] = own[320:]
    by_variable = slabs_of(own[0:320], 64)
    for d in range(3):
        mixed = mix(lambda w, v: tables[d * 25 + w * 5 + v : d * 25 + w * 5 + v + 1, :], by_variable)
        for w in range(5):
            flux[d * 64 : d * 64 + 64, w * 128 : w * 128 + 128] = mixed[w]
    flux_high, flux_low = split(flux[...])
    volume = dot(fixed[ALONG_HIGH, 0:192], flux_high) + dot(fixed[ALONG_HIGH, 0:192], flux_low)
    volume = volume + dot(fixed[ALONG_LOW, 0:192], flux_high)
    for w in range(5):
        volume_out[w * 64 : w * 64 + 64] = volume[:, w * 128 : w * 128 + 128]

    for copy in copies[8:]:
        copy.wait()
    high_out[...], low_out[...] = split(held[...])
    layers = early[640:800, 0:320]
    rows_high[...] = dot(layers, high_out[...]).astype(BF16)
    rows_low[...] = dot(layers, low_out[...]).astype(BF16)
    both = dot(rows_high[...], early[0:320]) + dot(rows_low[...], early[320:640])
    both = both.astype(BF16)
    fwd_out[...] = both[:, :256]
    bwd_out[...] = both[80:, 256:]


def unpack(left, right):
    lane = lanes((80, 128))
    forward = jnp.where(lane < 88, roll(right, 88), 0.0)
    cross = jnp.where(lane < 88, left, 0.0)
    back = jnp.where(lane < 40, roll(left, 40), jnp.where(lane < 80, roll(right, 40), 0.0))
    return forward, cross, back


def mix(coefficient, slabs):
    out = []
    for w in range(5):
        total = coefficient(w, 0) * slabs[0]
        for v in range(1, 5):
            total = total + coefficient(w, v) * slabs[v]
        out.append(total)
    return out


def slabs_of(x, size):
    return [x[v * size : (v + 1) * size] for v in range(5)]


def sweep_kernel(
    flow,
    plane,
    gy_low,
    gy_high,
    below,
    above,
    source,
    pseudo,
    tables,
    own_in,
    volume_in,
    fixed,
    residual_out,
    sent_out,
    extended,
):
    gx_at, gy_at = lax.axis_index("gx"), lax.axis_index("gy")
    first_lo = (gx_at > 0).astype(F32)
    second_lo = (gy_at > 0).astype(F32)
    second_hi = (gy_at < lax.axis_size("gy") - 1).astype(F32)
    u = flow[...]
    nothing = jnp.zeros((64, 320), F32)
    extended[0:64] = nothing
    extended[64:80] = plane[...] * (1.0 - first_lo)
    extended[80:112] = nothing[:32]
    extended[112:128] = plane[...] * first_lo
    for i in range(4):
        extended[128 + 16 * i : 136 + 16 * i] = gy_low[8 * i : 8 * i + 8] * second_lo
        extended[136 + 16 * i : 144 + 16 * i] = gy_high[8 * i : 8 * i + 8] * second_hi
    extended[192:256] = nothing
    position = rows((8, 320))
    for line in range(LINES):
        extended[256 + 8 * line : 264 + 8 * line] = jnp.where(
            position == 0,
            below[line : line + 1],
            jnp.where(position == 7, above[line : line + 1], 0.0),
        )
    extended[320:384] = nothing

    def outside(chosen, at):
        return sum(dot_nt(fixed[chosen], part) for part in split(extended[at : at + 128]))

    near_a = own_in[0:320] + outside(SELECT_A, 0)
    near_b, far_b = own_in[320:640], outside(SELECT_B, 128)
    far_layers = outside(SELECT_LAYERS, 256)
    lane = lanes((1, 128))
    table = lambda r: tables[r : r + 1, :]
    pieces = []

    for f in range(4):
        near = near_a if f < 2 else near_b
        candidates = [near[80 * n : 80 * n + 80] for n in range(4)]
        outer = [far_b[80 * n : 80 * n + 80] for n in range(4)]
        own = candidates[2 * (f % 2)]
        if f == 0:
            shifted = [roll(x, 16) for x in candidates]
        elif f == 1:
            shifted = [roll(x, -16) for x in candidates]
        elif f == 2:
            shifted = [
                jnp.where((lane // 8) % 2 == 1, roll(x, 8), y) for x, y in zip(candidates, outer)
            ]
        else:
            shifted = [
                jnp.where((lane // 8) % 2 == 0, roll(x, -8), y) for x, y in zip(candidates, outer)
            ]
        mirrored = table(MIRROR + f) > 0.5
        flipped = table(FLIP + f) > 0.5
        neighbour = jnp.where(
            flipped,
            jnp.where(mirrored, shifted[3], shifted[1]),
            jnp.where(mirrored, shifted[2], shifted[0]),
        )
        jump = LIFT * (neighbour - own)
        pieces += mix(lambda w, v: table(SIDE + (w * 5 + v) * 4 + f), slabs_of(jump, 16))

    top, bottom = own_in[640:720], own_in[720:800]
    outer_top, outer_bottom = far_layers[0:80], far_layers[80:160]
    lower_jump = jnp.where(lane % 8 == 0, outer_top, roll(top, 1)) - bottom
    upper_jump = jnp.where(lane % 8 == 7, outer_bottom, roll(bottom, -1)) - top
    pieces += mix(lambda w, v: table(SPAN + (w * 5 + v) * 2), slabs_of(lower_jump, 16))
    pieces += mix(lambda w, v: table(SPAN + (w * 5 + v) * 2 + 1), slabs_of(upper_jump, 16))
    pieces = [
        pair_lanes(volume_in[...]),
        pair_lanes(jnp.concatenate(pieces[:20], axis=0)),
        pair_lanes(jnp.concatenate(pieces[20:], axis=0)),
    ]
    operator = dot(fixed[PLACE_A], pieces[0]) + dot(fixed[PLACE_B], pieces[1])
    operator = operator + dot(fixed[PLACE_C, 0:160], pieces[2])
    operator_high, operator_low = split(operator)
    twice = fixed[TWICE, 0:128]
    operator_rows = dot_nt(twice, operator_high) + dot_nt(twice, operator_low)
    residual = source[...] - (pseudo[...] * u + operator_rows)
    residual_out[...] = residual

    turned = [jnp.zeros((64, 128), F32), tables[SPAN : SPAN + 56], jnp.zeros((8, 128), F32)]
    sent_out[:, 256:384] = jnp.transpose(jnp.concatenate(turned, axis=0))[:64]
    sent_out[:, 0:320] = residual


def maps_kernel(
    received,
    rows_high,
    rows_low,
    fwd,
    bwd,
    fixed,
    z_both,
    v_both,
    t_out,
    w_out,
    whole_out,
    short_out,
    turned_out,
    wide,
    started,
    t_state,
    w_state,
    bottoms,
    maps,
):
    last = jnp.concatenate([received[:, 256:384], jnp.zeros((64, 128), F32)], axis=0)
    jacobians = jnp.transpose(last)[64:114]
    high, low = split(received[:, 0:320])
    turned = dot_nt(fixed[EYE], jnp.concatenate([high, low], axis=0))
    turned_out[...] = turned + roll(turned, 64)
    turned = turned.astype(BF16)
    traces = dot(rows_high[...], turned) + dot(rows_low[...], turned)
    traces = traces + roll(traces, 64)
    trace_lane = lanes((160, 128))
    small_lane, small_row = lanes((80, 128)), rows((80, 128))
    for e in range(SEG):
        for k in range(SEG):
            at = e * SEG + k
            wide[e, k] = jnp.broadcast_to(jacobians[:, at : at + 1], (50, 128))
        moved = roll(traces, 80 - 8 * e)
        started[e] = jnp.where((trace_lane >= 80) & (trace_lane < 88), moved, 0.0)
        t_state[e] = jnp.where(small_lane == small_row, 1.0, 0.0)
        w_state[e] = jnp.where(lanes((80, 256)) == rows((80, 256)) + 88, 1.0, 0.0)

    def coupled(e, k, side, state):
        out = mix(lambda w, v: wide[e, k, pl.ds((w * 5 + v) * 2 + side, 1)], slabs_of(state, 16))
        return jnp.concatenate(out, axis=0)

    def forward(k, carry):
        mine = small_lane == 80 + k
        for pair in range(0, SEG, 2):
            cats = []
            for e in (pair, pair + 1):
                z_hi, z_lo = split(coupled(e, k, 0, t_state[e]))
                z_both[e, k, :, 0:128] = z_hi
                z_both[e, k, :, 128:256] = z_lo
                cats.append(jnp.concatenate([z_hi, z_lo, z_hi], axis=0))
            both = dot(fwd[:, 0:240], jnp.concatenate(cats, axis=1))
            for e, y in ((pair, both[:, :128]), (pair + 1, both[:, 128:])):
                t_state[e] = y[:80] + jnp.where(mine, started[e, 0:80], 0.0)
                bottoms[e, k] = y[80:] + jnp.where(mine, started[e, 80:160], 0.0)
        return carry

    lax.fori_loop(0, SEG, forward, 0, unroll=True)

    def backward(step, carry):
        k = SEG - 1 - step
        for e in range(SEG):
            z = [coupled(e, k, 1, w_state[e, :, half]) for half in (slice(0, 128), slice(128, 256))]
            z_hi, z_lo = split(jnp.concatenate(z, axis=1))
            v_both[e, k, :, 0:256] = z_hi
            v_both[e, k, :, 256:512] = z_lo
            y = dot(bwd[:, 0:240], jnp.concatenate([z_hi, z_lo, z_hi], axis=0))
            w_state[e, :, 0:128] = y[:, :128] + bottoms[e, k]
            w_state[e, :, 128:256] = y[:, 128:]
        return carry

    lax.fori_loop(0, SEG, backward, 0, unroll=True)
    for e in range(SEG):
        maps[e, :, 0:128] = w_state[e, :, 0:128]
        maps[e, :, 128:256] = w_state[e, :, 128:256] + roll(t_state[e], 40)
    compose(maps, t_out, w_out, whole_out, short_out)


def compose(maps, t_out, w_out, whole_out, short_out):
    tall_lane, tall_row = lanes((128, 128)), rows((128, 128))
    zero = jnp.zeros((48, 128), F32)
    parts = [unpack(maps[e, :, 0:128], maps[e, :, 128:256]) for e in range(SEG)]
    fixed = jnp.where((tall_row < 80) & (tall_lane == tall_row), 1.0, 0.0)
    ones = jnp.where((tall_row >= 80) & (tall_row < 88) & (tall_lane == 80), 1.0, 0.0)
    state = fixed + ones
    coupled = []
    for e in range(SEG):
        t_out[e] = state
        y = dot(left_cat(jnp.concatenate(parts[e][:2], axis=0)), right_cat(state))
        coupled.append(y[80:])
        state = jnp.concatenate([y[:80], ones[80:]], axis=0)
    last = state[:80]
    w0 = jnp.where(tall_lane == tall_row + 88, 1.0, 0.0)
    w1 = jnp.where((tall_lane == tall_row - 40) & (tall_row < 80), 1.0, 0.0)
    for e in range(SEG - 1, -1, -1):
        w_out[e, :, 0:128] = w0[:80]
        w_out[e, :, 128:256] = w1[:80]
        w = jnp.concatenate([right_cat(w0), right_cat(w1)], axis=1)
        y = dot(left_cat(parts[e][2]), w)
        w0 = jnp.concatenate([y[:, :128] + coupled[e], zero], axis=0)
        w1 = jnp.concatenate([y[:, 128:], zero], axis=0)
    whole_out[:, 0:128] = w0[:80]
    whole_out[:, 128:256] = w1[:80] + roll(last, 40)
    groups = lax.axis_size("span") // SEG
    short_out[...] = jnp.where(lax.axis_index("span") // SEG == groups - 1, w0[:80], last)


def against_pair(x):
    high, low = split(x)
    upper = jnp.concatenate([high, high], axis=1)
    return jnp.concatenate([upper, jnp.concatenate([low, jnp.zeros_like(low)], axis=1)], axis=0)


def fuse_kernel(
    z_both, v_both, t_in, w_in, turned, high, low, fixed, r_out, q_out, base_out, gs_high, gs_low
):
    for e in range(SEG):
        state = t_in[e]
        r = dot_nt(against_pair(jnp.transpose(state)[:96]), z_both[e].reshape(640, 256))
        r_out[e] = r[:88] + r[96:184]
        first = jnp.concatenate([state[:88], jnp.zeros((88, 128), F32)], axis=1)
        both = jnp.concatenate([first, w_in[e], jnp.zeros((88, 256), F32)], axis=0)
        q = dot_nt(against_pair(jnp.transpose(both)[:176]), v_both[e].reshape(640, 512))
        q_out[e] = q[:168] + q[176:344]
    load = pair_lanes(turned[...])
    total_high, total_low = split(dot(high[...], load) + dot(low[...], load))
    twice = fixed[TWICE, 0:128]
    base_out[...] = dot_nt(twice, total_high) + dot_nt(twice, total_low)
    gs_high[...] = dot(high[...], fixed[SPREAD, 0:256]).astype(BF16)
    gs_low[...] = dot(low[...], fixed[SPREAD, 0:256]).astype(BF16)


def by_element(x):
    tiles = [x[:, 128 * n : 128 * n + 128] for n in range(5)]
    lane = lanes((8, 128))
    out = []
    for k in range(SEG):
        at, shift = divmod(80 * k, 128)
        y = roll(tiles[at], -shift)
        if shift + 80 > 128:
            y = jnp.where(lane < 128 - shift, y, roll(tiles[at + 1], -shift))
        out.append(jnp.where(lane < 80, y, 0.0))
    return jnp.concatenate(out, axis=0)


def solve_kernel(*refs):
    *parts, r_in, q_in, base, gs_high, gs_low, fixed, out, forwards, crosses, backs_in = refs
    groups = len(parts)
    mine = lax.axis_index("span") // SEG
    lane = lanes((80, 128))
    for distance, part in enumerate(parts):
        group = lax.rem(mine - distance + groups, groups)
        if distance == 1:
            pieces = part[...], part[...], part[...]
        else:
            pieces = unpack(part[:, 0:128], part[:, 128:256])
        forwards[group], crosses[group], backs_in[group] = pieces
    one = jnp.where(rows((128, 128)) == 80, 1.0, 0.0)
    zero = jnp.zeros((48, 128), F32)
    traces = [one]
    for group in range(groups - 1):
        y = dot(left_cat(forwards[group]), right_cat(traces[-1]))
        traces.append(jnp.concatenate([y, zero], axis=0) + one)
    backs = [jnp.zeros((128, 128), F32)]
    for group in range(groups - 1, 0, -1):
        y = dot(left_cat(crosses[group]), right_cat(traces[group]))
        if group < groups - 1:
            y = y + dot(left_cat(backs_in[group]), right_cat(backs[0]))
        backs.insert(0, jnp.concatenate([y, zero], axis=0))
    trace, back = traces[0], backs[0]
    for group in range(1, groups):
        trace = jnp.where(mine == group, traces[group], trace)
        back = jnp.where(mine == group, backs[group], back)
    lower_in = jnp.concatenate([trace[:88]] * 5, axis=1)
    upper_in = jnp.concatenate([lower_in, jnp.concatenate([back[:80]] * 5, axis=1)], axis=0)
    lower = [jnp.sum(r_in[e] * lower_in, axis=0, keepdims=True) for e in range(SEG)]
    upper = [jnp.sum(q_in[e] * upper_in, axis=0, keepdims=True) for e in range(SEG)]
    coupled = [by_element(jnp.concatenate(x, axis=0)) for x in (lower, upper)]
    high, low = split(jnp.concatenate(coupled, axis=1))
    coupled = jnp.concatenate([high, low], axis=0)
    total = dot_nt(gs_high[...], coupled) + dot_nt(gs_low[...], coupled)
    total_high, total_low = split(total)
    ordered = fixed[ORDERED, 0:128]
    out[:, 0:320] = base[...] + dot_nt(ordered, total_high) + dot_nt(ordered, total_low)
    out[:, 320:384] = jnp.zeros((64, 64), F32)


def finish_kernel(incoming, flow, out):
    out[...] = flow[...] + incoming[:, 0:320]


def call(kernel, out_shape, in_specs, scratch=(), limit=16, flops=0, moved=0, name=None):
    return pl.pallas_call(
        kernel,
        out_shape=out_shape,
        in_specs=in_specs,
        out_specs=jax.tree.map(lambda _: pl.BlockSpec(memory_space=pltpu.VMEM), out_shape),
        scratch_shapes=list(scratch),
        compiler_params=pltpu.CompilerParams(vmem_limit_bytes=limit * 1024 * 1024),
        cost_estimate=pl.CostEstimate(flops=flops, bytes_accessed=moved, transcendentals=0),
        name=name,
    )


VM = pl.BlockSpec(memory_space=pltpu.VMEM)
HBM = pl.BlockSpec(memory_space=pltpu.HBM)


def shape(*dims, dtype=F32):
    return jax.ShapeDtypeStruct(dims, dtype)


def on_device(
    flow_state,
    source_term,
    pseudo_time,
    volume_jacobian,
    side_jacobian,
    span_jacobian,
    line_inverse,
    mirror_face,
    edge_flip,
):
    early, fixed = (jnp.asarray(value) for value in constants())
    groups = lax.axis_size("span") // SEG

    def ring(value, axis, step):
        count = lax.axis_size(axis)
        return lax.ppermute(value, axis, [(i, (i + step) % count) for i in range(count)])

    flow = flow_state.reshape(64, 320)
    plane, up, down, last, first = call(
        pack_kernel,
        (shape(16, 320), shape(32, 320), shape(32, 320), shape(8, 320), shape(8, 320)),
        [VM],
        limit=4,
        name="pack",
    )(flow)
    with jax.named_scope("halo"):
        below, above = ring(last, "span", 1), ring(first, "span", -1)
        gy_low, gy_high = ring(up, "gy", 1), ring(down, "gy", -1)
        plane = ring(plane, "gx", 1)

    inverse = line_inverse.reshape(LINES, 320, 320)
    natural = [
        volume_jacobian.transpose(0, 3, 4, 5, 1, 2).reshape(4, 75, 2, SEG),
        side_jacobian.transpose(0, 1, 4, 5, 3, 2).reshape(LINES, 25, 4, SEG),
        span_jacobian.transpose(0, 1, 4, 5, 3, 2).reshape(LINES, 25, 2, SEG),
        mirror_face.transpose(0, 1, 3, 2).reshape(LINES, 4, SEG),
        edge_flip.transpose(0, 1, 3, 2).reshape(LINES, 4, SEG),
    ]
    high, low, rows_high, rows_low, fwd, bwd, tables, own, volume = call(
        prepare_kernel,
        (
            shape(320, 320, dtype=BF16),
            shape(320, 320, dtype=BF16),
            shape(160, 320, dtype=BF16),
            shape(160, 320, dtype=BF16),
            shape(160, 256, dtype=BF16),
            shape(80, 256, dtype=BF16),
            shape(248, 128),
            shape(800, 128),
            shape(320, 128),
        ),
        [HBM] * 9,
        scratch=[
            pltpu.VMEM((320, 320), F32),
            pltpu.VMEM(early.shape, BF16),
            pltpu.VMEM(fixed.shape, BF16),
            pltpu.VMEM(flow.shape, F32),
        ]
        + [pltpu.VMEM(x.shape, x.dtype) for x in natural]
        + [pltpu.VMEM((192, 640), F32), pltpu.SemaphoreType.DMA((10,))],
        limit=28,
        flops=4_000_000_000,
        moved=8_000_000,
        name="prepare",
    )(
        *(
            pltpu.with_memory_space_constraint(x, pltpu.HBM)
            for x in (inverse, early, fixed, flow, *natural)
        )
    )

    residual, sent = call(
        sweep_kernel,
        (shape(64, 320), shape(64, 384)),
        [VM] * 12,
        scratch=[pltpu.VMEM((384, 320), F32)],
        limit=24,
        flops=3_000_000_000,
        moved=8_000_000,
        name="sweep",
    )(
        flow,
        plane,
        gy_low,
        gy_high,
        below,
        above,
        source_term.reshape(64, 320),
        pseudo_time.reshape(64, 320),
        tables,
        own,
        volume,
        fixed,
    )

    within = [[SEG * g + m for m in range(SEG)] for g in range(groups)]

    def exchange(value):
        value = value.reshape(SEG, 8, 384)
        value = lax.all_to_all(value, "span", 0, 0, axis_index_groups=within, tiled=True)
        return value.reshape(64, 384)

    z_both, v_both, t_maps, w_maps, whole, short, turned = call(
        maps_kernel,
        (
            shape(SEG, SEG, 80, 256, dtype=BF16),
            shape(SEG, SEG, 80, 512, dtype=BF16),
            shape(SEG, 128, 128),
            shape(SEG, 80, 256),
            shape(80, 256),
            shape(80, 128),
            shape(320, 128),
        ),
        [VM] * 6,
        scratch=[
            pltpu.VMEM((SEG, SEG, 50, 128), F32),
            pltpu.VMEM((SEG, 160, 128), F32),
            pltpu.VMEM((SEG, 80, 128), F32),
            pltpu.VMEM((SEG, 80, 256), F32),
            pltpu.VMEM((SEG, SEG, 80, 128), F32),
            pltpu.VMEM((SEG, 80, 256), F32),
        ],
        limit=28,
        name="maps",
    )(exchange(sent), rows_high, rows_low, fwd, bwd, fixed)
    wholes = [whole] + [
        ring(short if distance == 1 else whole, "span", SEG * distance)
        for distance in range(1, groups)
    ]
    fused = call(
        fuse_kernel,
        (
            shape(SEG, 88, 640),
            shape(SEG, 168, 640),
            shape(64, 320),
            shape(320, 256, dtype=BF16),
            shape(320, 256, dtype=BF16),
        ),
        [VM] * 8,
        limit=24,
        flops=5_000_000_000,
        moved=12_000_000,
        name="fuse",
    )(z_both, v_both, t_maps, w_maps, turned, high, low, fixed)
    answers = call(
        solve_kernel,
        shape(64, 384),
        [VM] * (groups + 6),
        scratch=[pltpu.VMEM((groups, 80, 128), F32)] * 3,
        limit=16,
        name="solve",
    )(*wholes, *fused, fixed)
    updated = call(finish_kernel, shape(64, 320), [VM] * 2, limit=4, name="finish")(
        exchange(answers), flow
    )
    return updated.reshape(flow_state.shape), residual.reshape(flow_state.shape)


def solution(mesh):
    lines = P("gx", "gy", "span", None)
    blocks = P("gx", "gy", "span", None, None, None)
    return jax.shard_map(
        on_device,
        mesh=mesh,
        in_specs=(lines, lines, lines, blocks, blocks, blocks, P("gx", "gy", None, None), lines, lines),
        out_specs=(lines, lines),
        check_vma=False,
    )
```

```python
import functools

import jax
import jax.numpy as jnp
import numpy as np
from jax import lax
from jax.experimental import pallas as pl
from jax.experimental.pallas import tpu as pltpu
from jax.sharding import PartitionSpec as P

LIFT = 6.0
F32 = jnp.float32
BF16 = jnp.bfloat16
LINES = 8
SEG = 8


def derivative_matrix():
    points = np.array([-1.0, -1.0 / np.sqrt(5.0), 1.0 / np.sqrt(5.0), 1.0])
    matrix = np.zeros((4, 4))
    for target in range(4):
        for source in range(4):
            if target != source:
                numerator = 1.0
                denominator = 1.0
                for other in range(4):
                    if other != source and other != target:
                        numerator *= points[target] - points[other]
                    if other != source:
                        denominator *= points[source] - points[other]
                matrix[target, source] = numerator / denominator
    for target in range(4):
        matrix[target, target] = -np.sum(matrix[target])
    return matrix


def entry(a, b, c, v):
    return ((4 * a + b) * 4 + c) * 5 + v


@functools.cache
def constants():
    select = np.zeros((1120, 320), np.float32)
    place = np.zeros((320, 800), np.float32)
    layers = np.zeros((160, 320), np.float32)
    for v in range(5):
        for a in range(4):
            for b in range(4):
                for c in range(4):
                    row = v * 64 + a * 16 + b * 4 + c
                    select[row, entry(a, b, c, v)] = 1
                    place[entry(a, b, c, v), row] = 1
        for e in range(4):
            for c in range(4):
                row = v * 16 + e * 4 + c
                for side, plane in enumerate((0, 3)):
                    for flip in range(2):
                        along = 3 - e if flip else e
                        block = (side * 2 + flip) * 80
                        select[320 + block + row, entry(plane, along, c, v)] = 1
                        select[640 + block + row, entry(along, plane, c, v)] = 1
                    place[entry(plane, e, c, v), 320 + 80 * side + row] = -1
                    place[entry(e, plane, c, v), 480 + 80 * side + row] = -1
        for a in range(4):
            for b in range(4):
                row = v * 16 + a * 4 + b
                select[960 + row, entry(a, b, 3, v)] = 1
                select[1040 + row, entry(a, b, 0, v)] = 1
                place[entry(a, b, 0, v), 640 + row] = -1
                place[entry(a, b, 3, v), 720 + row] = -1
                layers[row, entry(a, b, 3, v)] = 1
                layers[80 + row, entry(a, b, 0, v)] = 1
    top, bottom = layers[:80].T, layers[80:].T
    columns_high = np.zeros((320, 512), np.float32)
    columns_low = np.zeros((320, 512), np.float32)
    for base, chosen in ((0, bottom), (256, top)):
        columns_high[:, base : base + 80] = chosen
        columns_high[:, base + 80 : base + 160] = chosen
        columns_low[:, base + 160 : base + 240] = chosen
    spread = np.zeros((320, 256))
    spread[:, :80], spread[:, 128:208] = bottom, top
    eye, d = np.eye(4), derivative_matrix()
    along = np.concatenate(
        [
            np.kron(np.kron(d, eye), eye),
            np.kron(np.kron(eye, d), eye),
            np.kron(np.kron(eye, eye), d),
        ],
        axis=1,
    )
    high = along.astype(jnp.bfloat16).astype(np.float64)
    along = np.concatenate([high, high, along - high], axis=1)
    twice = np.concatenate([np.eye(64), np.eye(64)], axis=1)
    ordered = np.zeros((64, 128))
    for e in range(8):
        for k in range(8):
            ordered[8 * e + k, [8 * k + e, 64 + 8 * k + e]] = 1
    eye_320 = np.eye(320)
    blocks = [
        select,
        place[:, :320],
        place[:, 320:640],
        place[:, 640:],
        along[:, :192],
        along[:, 384:],
        twice,
        eye_320,
        spread,
        layers,
        ordered,
    ]
    fixed = np.zeros((sum(len(block) for block in blocks), 320), np.float32)
    at = 0
    for block in blocks:
        fixed[at : at + len(block), : block.shape[1]] = block
        at += len(block)
    early = np.zeros((800, 512), np.float32)
    early[:320], early[320:640], early[640:, :320] = columns_high, columns_low, layers
    return early.astype(jnp.bfloat16), fixed.astype(jnp.bfloat16)


SELECT_VOLUME, SELECT_A, SELECT_B, SELECT_LAYERS = (
    slice(0, 320),
    slice(320, 640),
    slice(640, 960),
    slice(960, 1120),
)
SELECT, PLACE_A, PLACE_B, PLACE_C = slice(0, 1120), slice(1120, 1440), slice(1440, 1760), slice(1760, 2080)
ALONG, ALONG_HIGH, ALONG_LOW = slice(2080, 2208), slice(2080, 2144), slice(2144, 2208)
TWICE = slice(2208, 2272)
EYE, SPREAD, LAYERS = slice(2272, 2592), slice(2592, 2912), slice(2912, 3072)
ORDERED = slice(3072, 3136)
SIDE, SPAN, MIRROR, FLIP = 80, 184, 240, 244


def dot(a, b):
    return lax.dot_general(a, b, (((1,), (0,)), ((), ())), preferred_element_type=F32)


def dot_nt(a, b):
    return lax.dot_general(a, b, (((1,), (1,)), ((), ())), preferred_element_type=F32)


def split(x):
    high = x.astype(BF16)
    return high, (x - high.astype(F32)).astype(BF16)


def split_3(x):
    high = x.astype(BF16)
    rest = x - high.astype(F32)
    middle = rest.astype(BF16)
    return high, middle, (rest - middle.astype(F32)).astype(BF16)


def lanes(shape):
    return lax.broadcasted_iota(jnp.int32, shape, len(shape) - 1)


def rows(shape):
    return lax.broadcasted_iota(jnp.int32, shape, len(shape) - 2)


def roll(x, amount):
    return pltpu.roll(x, amount % 128, 1)


def pair_lanes(x):
    high = x.astype(BF16).astype(F32)
    return jnp.where(lanes(x.shape) < 64, high, roll(x - high, 64)).astype(BF16)


def left_cat(x):
    high, low = split(x)
    return jnp.concatenate([high, high, low], axis=1)


def right_cat(x):
    high, low = split(x)
    return jnp.concatenate([high, low, high], axis=0)


def pack_kernel(flow, plane_out, up_out, down_out, last_out, first_out):
    at = pl.multiple_of((1 - lax.axis_index("gx")) * 48, 16)
    plane_out[...] = flow[pl.ds(at, 16)]
    for i in range(4):
        down_out[8 * i : 8 * i + 8] = flow[16 * i : 16 * i + 8]
        up_out[8 * i : 8 * i + 8] = flow[16 * i + 8 : 16 * i + 16]
    for line in range(LINES):
        first_out[line : line + 1] = flow[8 * line : 8 * line + 1]
        last_out[line : line + 1] = flow[8 * line + 7 : 8 * line + 8]


def prepare_kernel(
    inverse,
    early_in,
    fixed_in,
    flow_in,
    volume_in,
    side_in,
    span_in,
    mirror_in,
    flip_in,
    high_out,
    low_out,
    rows_high,
    rows_low,
    fwd_out,
    bwd_out,
    tables,
    own_out,
    volume_out,
    held,
    early,
    fixed,
    flow,
    volume_jacobian,
    side_jacobian,
    span_jacobian,
    mirror_face,
    edge_flip,
    flux,
    arrived,
):
    pairs = [
        (volume_in, volume_jacobian),
        (side_in, side_jacobian),
        (span_in, span_jacobian),
        (mirror_in, mirror_face),
        (flip_in, edge_flip),
        (flow_in, flow),
        (fixed_in.at[SELECT], fixed.at[SELECT]),
        (fixed_in.at[ALONG], fixed.at[ALONG]),
    ]
    pairs += [(inverse.at[lax.rem(lax.axis_index("span"), LINES)], held), (early_in, early)]
    copies = [
        pltpu.make_async_copy(source, target, arrived.at[at])
        for at, (source, target) in enumerate(pairs)
    ]
    for copy in copies:
        copy.start()
    for copy in copies[:5]:
        copy.wait()
    for line in range(LINES):
        here = slice(8 * line, 8 * line + 8)
        tables[0:75, here] = volume_jacobian[line // 2, :, line % 2, :]
        tables[SIDE : SIDE + 100, here] = side_jacobian[line].reshape(100, 8)
        tables[SPAN : SPAN + 50, here] = LIFT * span_jacobian[line].reshape(50, 8)
        tables[MIRROR : MIRROR + 4, here] = mirror_face[line].astype(F32)
        tables[FLIP : FLIP + 4, here] = edge_flip[line].astype(F32)
    for copy in copies[5:8]:
        copy.wait()

    padded = jnp.concatenate([flow[...], jnp.zeros((64, 320), F32)], axis=0)
    own = sum(dot_nt(fixed[SELECT], part) for part in split(padded))
    own_out[...] = own[320:]
    by_variable = slabs_of(own[0:320], 64)
    for d in range(3):
        mixed = mix(lambda w, v: tables[d * 25 + w * 5 + v : d * 25 + w * 5 + v + 1, :], by_variable)
        for w in range(5):
            flux[d * 64 : d * 64 + 64, w * 128 : w * 128 + 128] = mixed[w]
    flux_high, flux_low = split(flux[...])
    volume = dot(fixed[ALONG_HIGH, 0:192], flux_high) + dot(fixed[ALONG_HIGH, 0:192], flux_low)
    volume = volume + dot(fixed[ALONG_LOW, 0:192], flux_high)
    for w in range(5):
        volume_out[w * 64 : w * 64 + 64] = volume[:, w * 128 : w * 128 + 128]

    for copy in copies[8:]:
        copy.wait()
    high_out[...], low_out[...] = split(held[...])
    layers = early[640:800, 0:320]
    rows_high[...] = dot(layers, high_out[...]).astype(BF16)
    rows_low[...] = dot(layers, low_out[...]).astype(BF16)
    both = dot(rows_high[...], early[0:320]) + dot(rows_low[...], early[320:640])
    both = both.astype(BF16)
    fwd_out[...] = both[:, :256]
    bwd_out[...] = both[80:, 256:]


def unpack(left, right):
    lane = lanes((80, 128))
    forward = jnp.where(lane < 88, roll(right, 88), 0.0)
    cross = jnp.where(lane < 88, left, 0.0)
    back = jnp.where(lane < 40, roll(left, 40), jnp.where(lane < 80, roll(right, 40), 0.0))
    return forward, cross, back


def mix(coefficient, slabs):
    out = []
    for w in range(5):
        total = coefficient(w, 0) * slabs[0]
        for v in range(1, 5):
            total = total + coefficient(w, v) * slabs[v]
        out.append(total)
    return out


def slabs_of(x, size):
    return [x[v * size : (v + 1) * size] for v in range(5)]


def outside(fixed, chosen, values):
    return sum(dot_nt(fixed[chosen], part) for part in split(values))


def faces_kernel(plane, gy_low, gy_high, tables, own_in, volume_in, fixed, operator_out, extended):
    gx_at, gy_at = lax.axis_index("gx"), lax.axis_index("gy")
    first_lo = (gx_at > 0).astype(F32)
    second_lo = (gy_at > 0).astype(F32)
    second_hi = (gy_at < lax.axis_size("gy") - 1).astype(F32)
    nothing = jnp.zeros((64, 320), F32)
    extended[0:64] = nothing
    extended[64:80] = plane[...] * (1.0 - first_lo)
    extended[80:112] = nothing[:32]
    extended[112:128] = plane[...] * first_lo
    for i in range(4):
        extended[128 + 16 * i : 136 + 16 * i] = gy_low[8 * i : 8 * i + 8] * second_lo
        extended[136 + 16 * i : 144 + 16 * i] = gy_high[8 * i : 8 * i + 8] * second_hi
    extended[192:256] = nothing
    near_a = own_in[0:320] + outside(fixed, SELECT_A, extended[0:128])
    near_b, far_b = own_in[320:640], outside(fixed, SELECT_B, extended[128:256])
    lane = lanes((1, 128))
    table = lambda r: tables[r : r + 1, :]
    pieces = []

    for f in range(4):
        near = near_a if f < 2 else near_b
        candidates = [near[80 * n : 80 * n + 80] for n in range(4)]
        outer = [far_b[80 * n : 80 * n + 80] for n in range(4)]
        own = candidates[2 * (f % 2)]
        if f == 0:
            shifted = [roll(x, 16) for x in candidates]
        elif f == 1:
            shifted = [roll(x, -16) for x in candidates]
        elif f == 2:
            shifted = [
                jnp.where((lane // 8) % 2 == 1, roll(x, 8), y) for x, y in zip(candidates, outer)
            ]
        else:
            shifted = [
                jnp.where((lane // 8) % 2 == 0, roll(x, -8), y) for x, y in zip(candidates, outer)
            ]
        mirrored = table(MIRROR + f) > 0.5
        flipped = table(FLIP + f) > 0.5
        neighbour = jnp.where(
            flipped,
            jnp.where(mirrored, shifted[3], shifted[1]),
            jnp.where(mirrored, shifted[2], shifted[0]),
        )
        jump = LIFT * (neighbour - own)
        pieces += mix(lambda w, v: table(SIDE + (w * 5 + v) * 4 + f), slabs_of(jump, 16))

    operator = dot(fixed[PLACE_A], pair_lanes(volume_in[...]))
    operator_out[...] = operator + dot(fixed[PLACE_B], pair_lanes(jnp.concatenate(pieces, axis=0)))


def sweep_kernel(
    flow, below, above, source, pseudo, tables, own_in, operator_in, fixed, residual_out, sent_out, extended
):
    position = rows((8, 320))
    for line in range(LINES):
        extended[8 * line : 8 * line + 8] = jnp.where(
            position == 0,
            below[line : line + 1],
            jnp.where(position == 7, above[line : line + 1], 0.0),
        )
    extended[64:128] = jnp.zeros((64, 320), F32)
    far_layers = outside(fixed, SELECT_LAYERS, extended[...])
    lane = lanes((1, 128))
    table = lambda r: tables[r : r + 1, :]
    pieces = []
    top, bottom = own_in[640:720], own_in[720:800]
    outer_top, outer_bottom = far_layers[0:80], far_layers[80:160]
    lower_jump = jnp.where(lane % 8 == 0, outer_top, roll(top, 1)) - bottom
    upper_jump = jnp.where(lane % 8 == 7, outer_bottom, roll(bottom, -1)) - top
    pieces += mix(lambda w, v: table(SPAN + (w * 5 + v) * 2), slabs_of(lower_jump, 16))
    pieces += mix(lambda w, v: table(SPAN + (w * 5 + v) * 2 + 1), slabs_of(upper_jump, 16))
    pieces = pair_lanes(jnp.concatenate(pieces, axis=0))
    operator = operator_in[...] + dot(fixed[PLACE_C, 0:160], pieces)
    operator_high, operator_low = split(operator)
    twice = fixed[TWICE, 0:128]
    operator_rows = dot_nt(twice, operator_high) + dot_nt(twice, operator_low)
    residual = source[...] - (pseudo[...] * flow[...] + operator_rows)
    residual_out[...] = residual

    turned = [jnp.zeros((64, 128), F32), tables[SPAN : SPAN + 56], jnp.zeros((8, 128), F32)]
    sent_out[:, 256:384] = jnp.transpose(jnp.concatenate(turned, axis=0))[:64]
    sent_out[:, 0:320] = residual


def maps_kernel(
    received,
    rows_high,
    rows_low,
    fwd,
    bwd,
    fixed,
    z_both,
    v_both,
    t_out,
    w_out,
    whole_out,
    short_out,
    turned_out,
    wide,
    started,
    t_state,
    w_state,
    bottoms,
):
    last = jnp.concatenate([received[:, 256:384], jnp.zeros((64, 128), F32)], axis=0)
    jacobians = jnp.transpose(last)[64:114]
    high, low = split(received[:, 0:320])
    turned = dot_nt(fixed[EYE], jnp.concatenate([high, low], axis=0))
    turned_out[...] = turned + roll(turned, 64)
    turned = turned.astype(BF16)
    traces = dot(rows_high[...], turned) + dot(rows_low[...], turned)
    traces = traces + roll(traces, 64)
    trace_lane = lanes((160, 128))
    small_lane, small_row = lanes((80, 128)), rows((80, 128))
    for e in range(SEG):
        for k in range(SEG):
            at = e * SEG + k
            wide[e, k] = jnp.broadcast_to(jacobians[:, at : at + 1], (50, 128))
        moved = roll(traces, 80 - 8 * e)
        started[e] = jnp.where((trace_lane >= 80) & (trace_lane < 88), moved, 0.0)
        t_state[e] = jnp.where(small_lane == small_row, 1.0, 0.0)
        w_state[e] = jnp.where(lanes((80, 256)) == rows((80, 256)) + 88, 1.0, 0.0)

    def coupled(e, k, side, state):
        out = mix(lambda w, v: wide[e, k, pl.ds((w * 5 + v) * 2 + side, 1)], slabs_of(state, 16))
        return jnp.concatenate(out, axis=0)

    for k in range(SEG):
        mine = small_lane == 80 + k
        for pair in range(0, SEG, 2):
            cats = []
            for e in (pair, pair + 1):
                z_hi, z_lo = split(coupled(e, k, 0, t_state[e]))
                z_both[e, k, :, 0:128] = z_hi
                z_both[e, k, :, 128:256] = z_lo
                cats.append(jnp.concatenate([z_hi, z_lo, z_hi], axis=0))
            both = dot(fwd[:, 0:240], jnp.concatenate(cats, axis=1))
            for e, y in ((pair, both[:, :128]), (pair + 1, both[:, 128:])):
                t_state[e] = y[:80] + jnp.where(mine, started[e, 0:80], 0.0)
                bottoms[e, k] = y[80:] + jnp.where(mine, started[e, 80:160], 0.0)

    tall_lane, tall_row = lanes((128, 128)), rows((128, 128))
    ones = jnp.where((tall_row >= 80) & (tall_row < 88) & (tall_lane == 80), 1.0, 0.0)
    state = jnp.where((tall_row < 80) & (tall_lane == tall_row), 1.0, 0.0) + ones
    states = []
    for step in range(SEG):
        k = SEG - 1 - step
        for e in range(SEG):
            z = [coupled(e, k, 1, w_state[e, :, half]) for half in (slice(0, 128), slice(128, 256))]
            z_hi, z_lo = split(jnp.concatenate(z, axis=1))
            v_both[e, k, :, 0:256] = z_hi
            v_both[e, k, :, 256:512] = z_lo
            y = dot(bwd[:, 0:240], jnp.concatenate([z_hi, z_lo, z_hi], axis=0))
            w_state[e, :, 0:128] = y[:, :128] + bottoms[e, k]
            w_state[e, :, 128:256] = y[:, 128:]
        t_out[step] = state
        states.append(right_cat(state))
        y = dot(left_cat(t_state[step]), states[-1])
        state = jnp.concatenate([y, ones[80:]], axis=0)

    parts = [unpack(w_state[e, :, 0:128], w_state[e, :, 128:256])[1:] for e in range(SEG)]
    crossed = [dot(left_cat(parts[e][0]), states[e]) for e in range(SEG)]
    lefts = [left_cat(parts[e][1]) for e in range(SEG)]
    zero = jnp.zeros((48, 128), F32)
    w0 = jnp.where(tall_lane == tall_row + 88, 1.0, 0.0)
    w1 = jnp.where((tall_lane == tall_row - 40) & (tall_row < 80), 1.0, 0.0)
    for e in range(SEG - 1, -1, -1):
        w_out[e, :, 0:128] = w0[:80]
        w_out[e, :, 128:256] = w1[:80]
        y = dot(lefts[e], jnp.concatenate([right_cat(w0), right_cat(w1)], axis=1))
        w0 = jnp.concatenate([y[:, :128] + crossed[e], zero], axis=0)
        w1 = jnp.concatenate([y[:, 128:], zero], axis=0)
    whole_out[:, 0:128] = w0[:80]
    whole_out[:, 128:256] = w1[:80] + roll(state[:80], 40)
    groups = lax.axis_size("span") // SEG
    last = lax.axis_index("span") // SEG == groups - 1
    short_out[...] = jnp.where(last, w0[:80], state[:80])


def against_pair(x):
    high, low = split(x)
    upper = jnp.concatenate([high, high], axis=1)
    return jnp.concatenate([upper, jnp.concatenate([low, jnp.zeros_like(low)], axis=1)], axis=0)


def fuse_kernel(
    z_both, v_both, t_in, w_in, turned, high, low, fixed, r_out, q_out, base_out, gs_high, gs_low
):
    for e in range(SEG):
        state = t_in[e]
        r = dot_nt(against_pair(jnp.transpose(state)[:96]), z_both[e].reshape(640, 256))
        r_out[e] = r[:88] + r[96:184]
        first = jnp.concatenate([state[:88], jnp.zeros((88, 128), F32)], axis=1)
        both = jnp.concatenate([first, w_in[e], jnp.zeros((88, 256), F32)], axis=0)
        q = dot_nt(against_pair(jnp.transpose(both)[:176]), v_both[e].reshape(640, 512))
        q_out[e] = q[:168] + q[176:344]
    load = pair_lanes(turned[...])
    total_high, total_low = split(dot(high[...], load) + dot(low[...], load))
    twice = fixed[TWICE, 0:128]
    base_out[...] = dot_nt(twice, total_high) + dot_nt(twice, total_low)
    gs_high[...] = dot(high[...], fixed[SPREAD, 0:256]).astype(BF16)
    gs_low[...] = dot(low[...], fixed[SPREAD, 0:256]).astype(BF16)


def by_element(x):
    tiles = [x[:, 128 * n : 128 * n + 128] for n in range(5)]
    lane = lanes((8, 128))
    out = []
    for k in range(SEG):
        at, shift = divmod(80 * k, 128)
        y = roll(tiles[at], -shift)
        if shift + 80 > 128:
            y = jnp.where(lane < 128 - shift, y, roll(tiles[at + 1], -shift))
        out.append(jnp.where(lane < 80, y, 0.0))
    return jnp.concatenate(out, axis=0)


def solve_kernel(*refs):
    *parts, r_in, q_in, base, gs_high, gs_low, fixed, out, forwards, crosses, backs_in = refs
    groups = len(parts)
    mine = lax.axis_index("span") // SEG
    lane = lanes((80, 128))
    for distance, part in enumerate(parts):
        group = lax.rem(mine - distance + groups, groups)
        if distance == 1:
            pieces = part[...], part[...], part[...]
        else:
            pieces = unpack(part[:, 0:128], part[:, 128:256])
        forwards[group], crosses[group], backs_in[group] = pieces
    one = jnp.where(rows((128, 128)) == 80, 1.0, 0.0)
    zero = jnp.zeros((48, 128), F32)
    traces = [one]
    for group in range(groups - 1):
        y = dot(left_cat(forwards[group]), right_cat(traces[-1]))
        traces.append(jnp.concatenate([y, zero], axis=0) + one)
    backs = [jnp.zeros((128, 128), F32)]
    for group in range(groups - 1, 0, -1):
        y = dot(left_cat(crosses[group]), right_cat(traces[group]))
        if group < groups - 1:
            y = y + dot(left_cat(backs_in[group]), right_cat(backs[0]))
        backs.insert(0, jnp.concatenate([y, zero], axis=0))
    trace, back = traces[0], backs[0]
    for group in range(1, groups):
        trace = jnp.where(mine == group, traces[group], trace)
        back = jnp.where(mine == group, backs[group], back)
    lower_in = jnp.concatenate([trace[:88]] * 5, axis=1)
    upper_in = jnp.concatenate([lower_in, jnp.concatenate([back[:80]] * 5, axis=1)], axis=0)
    lower = [jnp.sum(r_in[e] * lower_in, axis=0, keepdims=True) for e in range(SEG)]
    upper = [jnp.sum(q_in[e] * upper_in, axis=0, keepdims=True) for e in range(SEG)]
    coupled = [by_element(jnp.concatenate(x, axis=0)) for x in (lower, upper)]
    high, low = split(jnp.concatenate(coupled, axis=1))
    coupled = jnp.concatenate([high, low], axis=0)
    total = dot_nt(gs_high[...], coupled) + dot_nt(gs_low[...], coupled)
    total_high, total_low = split(total)
    ordered = fixed[ORDERED, 0:128]
    out[:, 0:320] = base[...] + dot_nt(ordered, total_high) + dot_nt(ordered, total_low)
    out[:, 320:384] = jnp.zeros((64, 64), F32)


def finish_kernel(incoming, flow, out):
    out[...] = flow[...] + incoming[:, 0:320]


def call(kernel, out_shape, in_specs, scratch=(), limit=16, flops=0, moved=0, name=None):
    return pl.pallas_call(
        kernel,
        out_shape=out_shape,
        in_specs=in_specs,
        out_specs=jax.tree.map(lambda _: pl.BlockSpec(memory_space=pltpu.VMEM), out_shape),
        scratch_shapes=list(scratch),
        compiler_params=pltpu.CompilerParams(vmem_limit_bytes=limit * 1024 * 1024),
        cost_estimate=pl.CostEstimate(flops=flops, bytes_accessed=moved, transcendentals=0),
        name=name,
    )


VM = pl.BlockSpec(memory_space=pltpu.VMEM)
HBM = pl.BlockSpec(memory_space=pltpu.HBM)


def shape(*dims, dtype=F32):
    return jax.ShapeDtypeStruct(dims, dtype)


def on_device(
    flow_state,
    source_term,
    pseudo_time,
    volume_jacobian,
    side_jacobian,
    span_jacobian,
    line_inverse,
    mirror_face,
    edge_flip,
):
    early, fixed = (jnp.asarray(value) for value in constants())
    groups = lax.axis_size("span") // SEG

    def ring(value, axis, step):
        count = lax.axis_size(axis)
        return lax.ppermute(value, axis, [(i, (i + step) % count) for i in range(count)])

    flow = flow_state.reshape(64, 320)
    plane, up, down, last, first = call(
        pack_kernel,
        (shape(16, 320), shape(32, 320), shape(32, 320), shape(8, 320), shape(8, 320)),
        [VM],
        limit=4,
        name="pack",
    )(flow)
    with jax.named_scope("halo"):
        below, above = ring(last, "span", 1), ring(first, "span", -1)
        gy_low, gy_high = ring(up, "gy", 1), ring(down, "gy", -1)
        plane = ring(plane, "gx", 1)

    inverse = line_inverse.reshape(LINES, 320, 320)
    natural = [
        volume_jacobian.transpose(0, 3, 4, 5, 1, 2).reshape(4, 75, 2, SEG),
        side_jacobian.transpose(0, 1, 4, 5, 3, 2).reshape(LINES, 25, 4, SEG),
        span_jacobian.transpose(0, 1, 4, 5, 3, 2).reshape(LINES, 25, 2, SEG),
        mirror_face.transpose(0, 1, 3, 2).reshape(LINES, 4, SEG),
        edge_flip.transpose(0, 1, 3, 2).reshape(LINES, 4, SEG),
    ]
    high, low, rows_high, rows_low, fwd, bwd, tables, own, volume = call(
        prepare_kernel,
        (
            shape(320, 320, dtype=BF16),
            shape(320, 320, dtype=BF16),
            shape(160, 320, dtype=BF16),
            shape(160, 320, dtype=BF16),
            shape(160, 256, dtype=BF16),
            shape(80, 256, dtype=BF16),
            shape(248, 128),
            shape(800, 128),
            shape(320, 128),
        ),
        [HBM] * 9,
        scratch=[
            pltpu.VMEM((320, 320), F32),
            pltpu.VMEM(early.shape, BF16),
            pltpu.VMEM(fixed.shape, BF16),
            pltpu.VMEM(flow.shape, F32),
        ]
        + [pltpu.VMEM(x.shape, x.dtype) for x in natural]
        + [pltpu.VMEM((192, 640), F32), pltpu.SemaphoreType.DMA((10,))],
        limit=28,
        flops=4_000_000_000,
        moved=8_000_000,
        name="prepare",
    )(
        *(
            pltpu.with_memory_space_constraint(x, pltpu.HBM)
            for x in (inverse, early, fixed, flow, *natural)
        )
    )

    operator = call(
        faces_kernel,
        shape(320, 128),
        [VM] * 7,
        scratch=[pltpu.VMEM((256, 320), F32)],
        limit=16,
        flops=1_000_000_000,
        moved=3_000_000,
        name="faces",
    )(plane, gy_low, gy_high, tables, own, volume, fixed)
    residual, sent = call(
        sweep_kernel,
        (shape(64, 320), shape(64, 384)),
        [VM] * 9,
        scratch=[pltpu.VMEM((128, 320), F32)],
        limit=16,
        flops=1_000_000_000,
        moved=3_000_000,
        name="sweep",
    )(
        flow,
        below,
        above,
        source_term.reshape(64, 320),
        pseudo_time.reshape(64, 320),
        tables,
        own,
        operator,
        fixed,
    )

    within = [[SEG * g + m for m in range(SEG)] for g in range(groups)]

    def exchange(value):
        value = value.reshape(SEG, 8, 384)
        value = lax.all_to_all(value, "span", 0, 0, axis_index_groups=within, tiled=True)
        return value.reshape(64, 384)

    z_both, v_both, t_maps, w_maps, whole, short, turned = call(
        maps_kernel,
        (
            shape(SEG, SEG, 80, 256, dtype=BF16),
            shape(SEG, SEG, 80, 512, dtype=BF16),
            shape(SEG, 128, 128),
            shape(SEG, 80, 256),
            shape(80, 256),
            shape(80, 128),
            shape(320, 128),
        ),
        [VM] * 6,
        scratch=[
            pltpu.VMEM((SEG, SEG, 50, 128), F32),
            pltpu.VMEM((SEG, 160, 128), F32),
            pltpu.VMEM((SEG, 80, 128), F32),
            pltpu.VMEM((SEG, 80, 256), F32),
            pltpu.VMEM((SEG, SEG, 80, 128), F32),
        ],
        limit=28,
        name="maps",
    )(exchange(sent), rows_high, rows_low, fwd, bwd, fixed)
    wholes = [whole] + [
        ring(short if distance == 1 else whole, "span", SEG * distance)
        for distance in range(1, groups)
    ]
    fused = call(
        fuse_kernel,
        (
            shape(SEG, 88, 640),
            shape(SEG, 168, 640),
            shape(64, 320),
            shape(320, 256, dtype=BF16),
            shape(320, 256, dtype=BF16),
        ),
        [VM] * 8,
        limit=24,
        flops=5_000_000_000,
        moved=12_000_000,
        name="fuse",
    )(z_both, v_both, t_maps, w_maps, turned, high, low, fixed)
    answers = call(
        solve_kernel,
        shape(64, 384),
        [VM] * (groups + 6),
        scratch=[pltpu.VMEM((groups, 80, 128), F32)] * 3,
        limit=16,
        name="solve",
    )(*wholes, *fused, fixed)
    updated = call(finish_kernel, shape(64, 320), [VM] * 2, limit=4, name="finish")(
        exchange(answers), flow
    )
    return updated.reshape(flow_state.shape), residual.reshape(flow_state.shape)


def solution(mesh):
    lines = P("gx", "gy", "span", None)
    blocks = P("gx", "gy", "span", None, None, None)
    return jax.shard_map(
        on_device,
        mesh=mesh,
        in_specs=(lines, lines, lines, blocks, blocks, blocks, P("gx", "gy", None, None), lines, lines),
        out_specs=(lines, lines),
        check_vma=False,
    )
```

```python
import functools

import jax
import jax.numpy as jnp
import numpy as np
from jax import lax
from jax.experimental import pallas as pl
from jax.experimental.pallas import tpu as pltpu
from jax.sharding import PartitionSpec as P

LIFT = 6.0
F32 = jnp.float32
BF16 = jnp.bfloat16
LINES = 8
SEG = 8


def derivative_matrix():
    points = np.array([-1.0, -1.0 / np.sqrt(5.0), 1.0 / np.sqrt(5.0), 1.0])
    matrix = np.zeros((4, 4))
    for target in range(4):
        for source in range(4):
            if target != source:
                numerator = 1.0
                denominator = 1.0
                for other in range(4):
                    if other != source and other != target:
                        numerator *= points[target] - points[other]
                    if other != source:
                        denominator *= points[source] - points[other]
                matrix[target, source] = numerator / denominator
    for target in range(4):
        matrix[target, target] = -np.sum(matrix[target])
    return matrix


def entry(a, b, c, v):
    return ((4 * a + b) * 4 + c) * 5 + v


@functools.cache
def constants():
    select = np.zeros((1120, 320), np.float32)
    place = np.zeros((320, 800), np.float32)
    layers = np.zeros((160, 320), np.float32)
    for v in range(5):
        for a in range(4):
            for b in range(4):
                for c in range(4):
                    row = v * 64 + a * 16 + b * 4 + c
                    select[row, entry(a, b, c, v)] = 1
                    place[entry(a, b, c, v), row] = 1
        for e in range(4):
            for c in range(4):
                row = v * 16 + e * 4 + c
                for side, plane in enumerate((0, 3)):
                    for flip in range(2):
                        along = 3 - e if flip else e
                        block = (side * 2 + flip) * 80
                        select[320 + block + row, entry(plane, along, c, v)] = 1
                        select[640 + block + row, entry(along, plane, c, v)] = 1
                    place[entry(plane, e, c, v), 320 + 80 * side + row] = -1
                    place[entry(e, plane, c, v), 480 + 80 * side + row] = -1
        for a in range(4):
            for b in range(4):
                row = v * 16 + a * 4 + b
                select[960 + row, entry(a, b, 3, v)] = 1
                select[1040 + row, entry(a, b, 0, v)] = 1
                place[entry(a, b, 0, v), 640 + row] = -1
                place[entry(a, b, 3, v), 720 + row] = -1
                layers[row, entry(a, b, 3, v)] = 1
                layers[80 + row, entry(a, b, 0, v)] = 1
    top, bottom = layers[:80].T, layers[80:].T
    columns_high = np.zeros((320, 512), np.float32)
    columns_low = np.zeros((320, 512), np.float32)
    for base, chosen in ((0, bottom), (256, top)):
        columns_high[:, base : base + 80] = chosen
        columns_high[:, base + 80 : base + 160] = chosen
        columns_low[:, base + 160 : base + 240] = chosen
    spread = np.zeros((320, 256))
    spread[:, :80], spread[:, 128:208] = bottom, top
    eye, d = np.eye(4), derivative_matrix()
    along = np.concatenate(
        [
            np.kron(np.kron(d, eye), eye),
            np.kron(np.kron(eye, d), eye),
            np.kron(np.kron(eye, eye), d),
        ],
        axis=1,
    )
    high = along.astype(jnp.bfloat16).astype(np.float64)
    along = np.concatenate([high, high, along - high], axis=1)
    twice = np.concatenate([np.eye(64), np.eye(64)], axis=1)
    ordered = np.zeros((64, 128))
    for e in range(8):
        for k in range(8):
            ordered[8 * e + k, [8 * k + e, 64 + 8 * k + e]] = 1
    eye_320 = np.eye(320)
    blocks = [
        select,
        place[:, :320],
        place[:, 320:640],
        place[:, 640:],
        along[:, :192],
        along[:, 384:],
        twice,
        eye_320,
        spread,
        layers,
        ordered,
    ]
    fixed = np.zeros((sum(len(block) for block in blocks), 320), np.float32)
    at = 0
    for block in blocks:
        fixed[at : at + len(block), : block.shape[1]] = block
        at += len(block)
    early = np.zeros((800, 512), np.float32)
    early[:320], early[320:640], early[640:, :320] = columns_high, columns_low, layers
    return early.astype(jnp.bfloat16), fixed.astype(jnp.bfloat16)


SELECT_VOLUME, SELECT_A, SELECT_B, SELECT_LAYERS = (
    slice(0, 320),
    slice(320, 640),
    slice(640, 960),
    slice(960, 1120),
)
SELECT, PLACE_A, PLACE_B, PLACE_C = slice(0, 1120), slice(1120, 1440), slice(1440, 1760), slice(1760, 2080)
ALONG, ALONG_HIGH, ALONG_LOW = slice(2080, 2208), slice(2080, 2144), slice(2144, 2208)
TWICE = slice(2208, 2272)
EYE, SPREAD, LAYERS = slice(2272, 2592), slice(2592, 2912), slice(2912, 3072)
ORDERED = slice(3072, 3136)
SIDE, SPAN, MIRROR, FLIP = 80, 184, 240, 244


def dot(a, b):
    return lax.dot_general(a, b, (((1,), (0,)), ((), ())), preferred_element_type=F32)


def dot_nt(a, b):
    return lax.dot_general(a, b, (((1,), (1,)), ((), ())), preferred_element_type=F32)


def split(x):
    high = x.astype(BF16)
    return high, (x - high.astype(F32)).astype(BF16)


def split_3(x):
    high = x.astype(BF16)
    rest = x - high.astype(F32)
    middle = rest.astype(BF16)
    return high, middle, (rest - middle.astype(F32)).astype(BF16)


def lanes(shape):
    return lax.broadcasted_iota(jnp.int32, shape, len(shape) - 1)


def rows(shape):
    return lax.broadcasted_iota(jnp.int32, shape, len(shape) - 2)


def roll(x, amount):
    return pltpu.roll(x, amount % 128, 1)


def pair_lanes(x):
    high = x.astype(BF16).astype(F32)
    return jnp.where(lanes(x.shape) < 64, high, roll(x - high, 64)).astype(BF16)


def left_cat(x):
    high, low = split(x)
    return jnp.concatenate([high, high, low], axis=1)


def right_cat(x):
    high, low = split(x)
    return jnp.concatenate([high, low, high], axis=0)


def pack_kernel(flow, plane_out, up_out, down_out, last_out, first_out):
    at = pl.multiple_of((1 - lax.axis_index("gx")) * 48, 16)
    plane_out[...] = flow[pl.ds(at, 16)]
    for i in range(4):
        down_out[8 * i : 8 * i + 8] = flow[16 * i : 16 * i + 8]
        up_out[8 * i : 8 * i + 8] = flow[16 * i + 8 : 16 * i + 16]
    for line in range(LINES):
        first_out[line : line + 1] = flow[8 * line : 8 * line + 1]
        last_out[line : line + 1] = flow[8 * line + 7 : 8 * line + 8]


def chosen_of(matrix, values):
    both = dot_nt(matrix, jnp.concatenate(split(values), axis=0))
    return both + roll(both, 64)


def prepare_kernel(
    inverse,
    early_in,
    fixed_in,
    flow_in,
    volume_in,
    side_in,
    span_in,
    mirror_in,
    flip_in,
    high_out,
    low_out,
    rows_high,
    rows_low,
    fwd_out,
    bwd_out,
    tables,
    own_out,
    volume_out,
    held,
    early,
    fixed,
    flow,
    volume_jacobian,
    side_jacobian,
    span_jacobian,
    mirror_face,
    edge_flip,
    flux,
    arrived,
):
    pairs = [
        (volume_in, volume_jacobian),
        (side_in, side_jacobian),
        (span_in, span_jacobian),
        (mirror_in, mirror_face),
        (flip_in, edge_flip),
        (flow_in, flow),
        (fixed_in.at[SELECT], fixed.at[SELECT]),
        (fixed_in.at[ALONG], fixed.at[ALONG]),
    ]
    pairs += [(inverse.at[lax.rem(lax.axis_index("span"), LINES)], held), (early_in, early)]
    copies = [
        pltpu.make_async_copy(source, target, arrived.at[at])
        for at, (source, target) in enumerate(pairs)
    ]
    for copy in copies:
        copy.start()
    for copy in copies[:5]:
        copy.wait()
    for line in range(LINES):
        here = slice(8 * line, 8 * line + 8)
        tables[0:75, here] = volume_jacobian[line // 2, :, line % 2, :]
        tables[SIDE : SIDE + 100, here] = side_jacobian[line].reshape(100, 8)
        tables[SPAN : SPAN + 50, here] = LIFT * span_jacobian[line].reshape(50, 8)
        tables[MIRROR : MIRROR + 4, here] = mirror_face[line].astype(F32)
        tables[FLIP : FLIP + 4, here] = edge_flip[line].astype(F32)
    for copy in copies[5:8]:
        copy.wait()

    own = chosen_of(fixed[SELECT], flow[...])
    own_out[...] = jnp.where(lanes((800, 128)) < 64, own[320:], 0.0)
    by_variable = slabs_of(own[0:320], 64)
    for d in range(3):
        mixed = mix(lambda w, v: tables[d * 25 + w * 5 + v : d * 25 + w * 5 + v + 1, :], by_variable)
        for w in range(5):
            flux[d * 64 : d * 64 + 64, w * 128 : w * 128 + 128] = mixed[w]
    flux_high, flux_low = split(flux[...])
    volume = dot(fixed[ALONG_HIGH, 0:192], flux_high) + dot(fixed[ALONG_HIGH, 0:192], flux_low)
    volume = volume + dot(fixed[ALONG_LOW, 0:192], flux_high)
    for w in range(5):
        volume_out[w * 64 : w * 64 + 64] = volume[:, w * 128 : w * 128 + 128]

    for copy in copies[8:]:
        copy.wait()
    high_out[...], low_out[...] = split(held[...])
    layers = early[640:800, 0:320]
    rows_high[...] = dot(layers, high_out[...]).astype(BF16)
    rows_low[...] = dot(layers, low_out[...]).astype(BF16)
    both = dot(rows_high[...], early[0:320]) + dot(rows_low[...], early[320:640])
    both = both.astype(BF16)
    fwd_out[...] = both[:, :256]
    bwd_out[...] = both[80:, 256:]


def unpack(left, right):
    lane = lanes((80, 128))
    forward = jnp.where(lane < 88, roll(right, 88), 0.0)
    cross = jnp.where(lane < 88, left, 0.0)
    back = jnp.where(lane < 40, roll(left, 40), jnp.where(lane < 80, roll(right, 40), 0.0))
    return forward, cross, back


def mix(coefficient, slabs):
    out = []
    for w in range(5):
        total = coefficient(w, 0) * slabs[0]
        for v in range(1, 5):
            total = total + coefficient(w, v) * slabs[v]
        out.append(total)
    return out


def slabs_of(x, size):
    return [x[v * size : (v + 1) * size] for v in range(5)]


def span_kernel(below, above, tables, own_in, volume_in, fixed, operator_out, extended):
    position = rows((8, 320))
    for line in range(LINES):
        extended[8 * line : 8 * line + 8] = jnp.where(
            position == 0,
            below[line : line + 1],
            jnp.where(position == 7, above[line : line + 1], 0.0),
        )
    far_layers = chosen_of(fixed[SELECT_LAYERS], extended[...])
    lane = lanes((1, 128))
    table = lambda r: tables[r : r + 1, :]
    pieces = []
    top, bottom = own_in[640:720], own_in[720:800]
    outer_top, outer_bottom = far_layers[0:80], far_layers[80:160]
    lower_jump = jnp.where(lane % 8 == 0, outer_top, roll(top, 1)) - bottom
    upper_jump = jnp.where(lane % 8 == 7, outer_bottom, roll(bottom, -1)) - top
    pieces += mix(lambda w, v: table(SPAN + (w * 5 + v) * 2), slabs_of(lower_jump, 16))
    pieces += mix(lambda w, v: table(SPAN + (w * 5 + v) * 2 + 1), slabs_of(upper_jump, 16))
    operator = dot(fixed[PLACE_A], pair_lanes(volume_in[...]))
    pieces = pair_lanes(jnp.concatenate(pieces, axis=0))
    operator_out[...] = operator + dot(fixed[PLACE_C, 0:160], pieces)


def sweep_kernel(
    flow,
    plane,
    gy_low,
    gy_high,
    source,
    pseudo,
    tables,
    own_in,
    operator_in,
    fixed,
    residual_out,
    sent_out,
    extended,
):
    gx_at, gy_at = lax.axis_index("gx"), lax.axis_index("gy")
    first_lo = (gx_at > 0).astype(F32)
    second_lo = (gy_at > 0).astype(F32)
    second_hi = (gy_at < lax.axis_size("gy") - 1).astype(F32)
    extended[0:64] = jnp.zeros((64, 320), F32)
    extended[64:80] = plane[...] * (1.0 - first_lo)
    extended[80:112] = jnp.zeros((32, 320), F32)
    extended[112:128] = plane[...] * first_lo
    for i in range(4):
        extended[128 + 16 * i : 136 + 16 * i] = gy_low[8 * i : 8 * i + 8] * second_lo
        extended[136 + 16 * i : 144 + 16 * i] = gy_high[8 * i : 8 * i + 8] * second_hi
    near_a = sum(dot_nt(fixed[SELECT_A], part) for part in split(extended[0:128])) + own_in[0:320]
    near_b, far_b = own_in[320:640], chosen_of(fixed[SELECT_B], extended[128:192])
    lane = lanes((1, 128))
    table = lambda r: tables[r : r + 1, :]
    pieces = []

    for f in range(4):
        near = near_a if f < 2 else near_b
        candidates = [near[80 * n : 80 * n + 80] for n in range(4)]
        outer = [far_b[80 * n : 80 * n + 80] for n in range(4)]
        own = candidates[2 * (f % 2)]
        if f == 0:
            shifted = [roll(x, 16) for x in candidates]
        elif f == 1:
            shifted = [roll(x, -16) for x in candidates]
        elif f == 2:
            shifted = [
                jnp.where((lane // 8) % 2 == 1, roll(x, 8), y) for x, y in zip(candidates, outer)
            ]
        else:
            shifted = [
                jnp.where((lane // 8) % 2 == 0, roll(x, -8), y) for x, y in zip(candidates, outer)
            ]
        mirrored = table(MIRROR + f) > 0.5
        flipped = table(FLIP + f) > 0.5
        neighbour = jnp.where(
            flipped,
            jnp.where(mirrored, shifted[3], shifted[1]),
            jnp.where(mirrored, shifted[2], shifted[0]),
        )
        jump = LIFT * (neighbour - own)
        pieces += mix(lambda w, v: table(SIDE + (w * 5 + v) * 4 + f), slabs_of(jump, 16))

    pieces = pair_lanes(jnp.concatenate(pieces, axis=0))
    operator = operator_in[...] + dot(fixed[PLACE_B], pieces)
    operator_high, operator_low = split(operator)
    twice = fixed[TWICE, 0:128]
    operator_rows = dot_nt(twice, operator_high) + dot_nt(twice, operator_low)
    residual = source[...] - (pseudo[...] * flow[...] + operator_rows)
    residual_out[...] = residual

    turned = [jnp.zeros((64, 128), F32), tables[SPAN : SPAN + 56], jnp.zeros((8, 128), F32)]
    sent_out[:, 256:384] = jnp.transpose(jnp.concatenate(turned, axis=0))[:64]
    sent_out[:, 0:320] = residual


def maps_kernel(
    received,
    rows_high,
    rows_low,
    fwd,
    bwd,
    fixed,
    z_both,
    v_both,
    t_out,
    crossed_out,
    lefts_out,
    whole_out,
    short_out,
    turned_out,
    wide,
    started,
    t_state,
    w_state,
    bottoms,
):
    last = jnp.concatenate([received[:, 256:384], jnp.zeros((64, 128), F32)], axis=0)
    jacobians = jnp.transpose(last)[64:114]
    high, low = split(received[:, 0:320])
    turned = dot_nt(fixed[EYE], jnp.concatenate([high, low], axis=0))
    turned_out[...] = turned + roll(turned, 64)
    turned = turned.astype(BF16)
    traces = dot(rows_high[...], turned) + dot(rows_low[...], turned)
    traces = traces + roll(traces, 64)
    trace_lane = lanes((160, 128))
    small_lane, small_row = lanes((80, 128)), rows((80, 128))
    for e in range(SEG):
        for k in range(SEG):
            at = e * SEG + k
            wide[e, k] = jnp.broadcast_to(jacobians[:, at : at + 1], (50, 128))
        moved = roll(traces, 80 - 8 * e)
        started[e] = jnp.where((trace_lane >= 80) & (trace_lane < 88), moved, 0.0)

    def coupled(e, k, side, state):
        out = mix(lambda w, v: wide[e, k, pl.ds((w * 5 + v) * 2 + side, 1)], slabs_of(state, 16))
        return jnp.concatenate(out, axis=0)

    diagonal = (small_lane[:16] % 16 == small_row[:16]) & (small_lane[:16] < 80)

    def coupled_identity(e, k, side):
        out = []
        for w in range(5):
            line = [wide[e, k, pl.ds((w * 5 + v) * 2 + side, 1)] for v in range(5)]
            row = line[4]
            for v in range(3, -1, -1):
                row = jnp.where(small_lane[:1] < 16 * v + 16, line[v], row)
            out.append(jnp.where(diagonal, row, 0.0))
        return jnp.concatenate(out, axis=0)

    for k in range(SEG):
        mine = small_lane == 80 + k
        for pair in range(0, SEG, 2):
            cats = []
            for e in (pair, pair + 1):
                z = coupled(e, k, 0, t_state[e]) if k else coupled_identity(e, k, 0)
                z_hi, z_lo = split(z)
                z_both[e, k, :, 0:128] = z_hi
                z_both[e, k, :, 128:256] = z_lo
                cats.append(jnp.concatenate([z_hi, z_lo, z_hi], axis=0))
            both = dot(fwd[:, 0:240], jnp.concatenate(cats, axis=1))
            for e, y in ((pair, both[:, :128]), (pair + 1, both[:, 128:])):
                t_state[e] = y[:80] + jnp.where(mine, started[e, 0:80], 0.0)
                bottoms[e, k] = y[80:] + jnp.where(mine, started[e, 80:160], 0.0)

    tall_lane, tall_row = lanes((128, 128)), rows((128, 128))
    ones = jnp.where((tall_row >= 80) & (tall_row < 88) & (tall_lane == 80), 1.0, 0.0)
    state = jnp.where((tall_row < 80) & (tall_lane == tall_row), 1.0, 0.0) + ones
    states = []
    for step in range(SEG):
        k = SEG - 1 - step
        for e in range(SEG):
            if step:
                halves = (w_state[e, :, 0:128], w_state[e, :, 128:256])
                z = [coupled(e, k, 1, half) for half in halves]
            else:
                z = coupled_identity(e, k, 1)
                z = [
                    jnp.where(small_lane >= 88, roll(z, 88), 0.0),
                    jnp.where(small_lane < 40, roll(z, 88), 0.0),
                ]
            z_hi, z_lo = split(jnp.concatenate(z, axis=1))
            v_both[e, k, :, 0:256] = z_hi
            v_both[e, k, :, 256:512] = z_lo
            y = dot(bwd[:, 0:240], jnp.concatenate([z_hi, z_lo, z_hi], axis=0))
            w_state[e, :, 0:128] = y[:, :128] + bottoms[e, k]
            w_state[e, :, 128:256] = y[:, 128:]
        t_out[step] = state
        states.append(right_cat(state))
        y = dot(left_cat(t_state[step]), states[-1])
        state = jnp.concatenate([y, ones[80:]], axis=0)

    maps = []
    for e in range(SEG):
        left, right = w_state[e, :, 0:128], w_state[e, :, 128:256]
        _, cross, back = unpack(left, right)
        crossed = dot(left_cat(cross), states[e])
        lefts_out[e] = left_cat(back)
        crossed_out[e] = crossed
        maps.append((crossed + jnp.where(small_lane < 88, 0.0, left), right))
    zero = jnp.zeros((48, 128), F32)
    lefts = [lefts_out[e] for e in range(SEG)]
    while len(maps) > 1:
        joined = []
        for at in range(0, len(maps), 2):
            after = [right_cat(jnp.concatenate([x, zero], axis=0)) for x in maps[at + 1]]
            y = dot(lefts[at], jnp.concatenate(after, axis=1))
            kept = jnp.where(small_lane < 88, maps[at][0], 0.0)
            joined.append((y[:, :128] + kept, y[:, 128:]))
        maps = joined
        lefts = [left_cat(unpack(*both)[2]) for both in maps]
    whole_out[:, 0:128] = maps[0][0]
    whole_out[:, 128:256] = maps[0][1] + roll(state[:80], 40)
    groups = lax.axis_size("span") // SEG
    last = lax.axis_index("span") // SEG == groups - 1
    short_out[...] = jnp.where(last, maps[0][0], state[:80])


def against_pair(x):
    high, low = split(x)
    upper = jnp.concatenate([high, high], axis=1)
    return jnp.concatenate([upper, jnp.concatenate([low, jnp.zeros_like(low)], axis=1)], axis=0)


def fuse_kernel(
    z_both, v_both, t_in, crossed, lefts, turned, high, low, fixed, r_out, q_out, base_out, gs_high, gs_low
):
    tall_lane, tall_row = lanes((128, 128)), rows((128, 128))
    zero = jnp.zeros((48, 128), F32)
    w0 = jnp.where(tall_lane == tall_row + 88, 1.0, 0.0)
    w1 = jnp.where((tall_lane == tall_row - 40) & (tall_row < 80), 1.0, 0.0)
    for e in range(SEG - 1, -1, -1):
        behind = jnp.concatenate([w0[:80], w1[:80]], axis=1)
        if e > 0:
            y = dot(lefts[e], jnp.concatenate([right_cat(w0), right_cat(w1)], axis=1))
            w0 = jnp.concatenate([y[:, :128] + crossed[e], zero], axis=0)
            w1 = jnp.concatenate([y[:, 128:], zero], axis=0)
        state = t_in[e]
        r = dot_nt(against_pair(jnp.transpose(state)[:96]), z_both[e].reshape(640, 256))
        r_out[e] = r[:88] + r[96:184]
        first = jnp.concatenate([state[:88], jnp.zeros((88, 128), F32)], axis=1)
        both = jnp.concatenate([first, behind, jnp.zeros((88, 256), F32)], axis=0)
        q = dot_nt(against_pair(jnp.transpose(both)[:176]), v_both[e].reshape(640, 512))
        q_out[e] = q[:168] + q[176:344]
    load = pair_lanes(turned[...])
    total_high, total_low = split(dot(high[...], load) + dot(low[...], load))
    twice = fixed[TWICE, 0:128]
    base_out[...] = dot_nt(twice, total_high) + dot_nt(twice, total_low)
    gs_high[...] = dot(high[...], fixed[SPREAD, 0:256]).astype(BF16)
    gs_low[...] = dot(low[...], fixed[SPREAD, 0:256]).astype(BF16)


def by_element(x):
    tiles = [x[:, 128 * n : 128 * n + 128] for n in range(5)]
    lane = lanes((8, 128))
    out = []
    for k in range(SEG):
        at, shift = divmod(80 * k, 128)
        y = roll(tiles[at], -shift)
        if shift + 80 > 128:
            y = jnp.where(lane < 128 - shift, y, roll(tiles[at + 1], -shift))
        out.append(jnp.where(lane < 80, y, 0.0))
    return jnp.concatenate(out, axis=0)


def solve_kernel(*refs):
    *parts, r_in, q_in, base, gs_high, gs_low, fixed, out, forwards, crosses, backs_in = refs
    groups = len(parts)
    mine = lax.axis_index("span") // SEG
    lane = lanes((80, 128))
    for distance, part in enumerate(parts):
        group = lax.rem(mine - distance + groups, groups)
        if distance == 1:
            pieces = part[...], part[...], part[...]
        else:
            pieces = unpack(part[:, 0:128], part[:, 128:256])
        forwards[group], crosses[group], backs_in[group] = pieces
    one = jnp.where(rows((128, 128)) == 80, 1.0, 0.0)
    zero = jnp.zeros((48, 128), F32)
    traces = [one]
    for group in range(groups - 1):
        y = dot(left_cat(forwards[group]), right_cat(traces[-1]))
        traces.append(jnp.concatenate([y, zero], axis=0) + one)
    backs = [jnp.zeros((128, 128), F32)]
    for group in range(groups - 1, 0, -1):
        y = dot(left_cat(crosses[group]), right_cat(traces[group]))
        if group < groups - 1:
            y = y + dot(left_cat(backs_in[group]), right_cat(backs[0]))
        backs.insert(0, jnp.concatenate([y, zero], axis=0))
    trace, back = traces[0], backs[0]
    for group in range(1, groups):
        trace = jnp.where(mine == group, traces[group], trace)
        back = jnp.where(mine == group, backs[group], back)
    lower_in = jnp.concatenate([trace[:88]] * 5, axis=1)
    upper_in = jnp.concatenate([lower_in, jnp.concatenate([back[:80]] * 5, axis=1)], axis=0)
    lower = [jnp.sum(r_in[e] * lower_in, axis=0, keepdims=True) for e in range(SEG)]
    upper = [jnp.sum(q_in[e] * upper_in, axis=0, keepdims=True) for e in range(SEG)]
    coupled = [by_element(jnp.concatenate(x, axis=0)) for x in (lower, upper)]
    high, low = split(jnp.concatenate(coupled, axis=1))
    coupled = jnp.concatenate([high, low], axis=0)
    total = dot_nt(gs_high[...], coupled) + dot_nt(gs_low[...], coupled)
    total_high, total_low = split(total)
    ordered = fixed[ORDERED, 0:128]
    out[:, 0:320] = base[...] + dot_nt(ordered, total_high) + dot_nt(ordered, total_low)
    out[:, 320:384] = jnp.zeros((64, 64), F32)


def finish_kernel(incoming, flow, out):
    out[...] = flow[...] + incoming[:, 0:320]


def call(kernel, out_shape, in_specs, scratch=(), limit=16, flops=0, moved=0, name=None):
    return pl.pallas_call(
        kernel,
        out_shape=out_shape,
        in_specs=in_specs,
        out_specs=jax.tree.map(lambda _: pl.BlockSpec(memory_space=pltpu.VMEM), out_shape),
        scratch_shapes=list(scratch),
        compiler_params=pltpu.CompilerParams(vmem_limit_bytes=limit * 1024 * 1024),
        cost_estimate=pl.CostEstimate(flops=flops, bytes_accessed=moved, transcendentals=0),
        name=name,
    )


VM = pl.BlockSpec(memory_space=pltpu.VMEM)
HBM = pl.BlockSpec(memory_space=pltpu.HBM)


def shape(*dims, dtype=F32):
    return jax.ShapeDtypeStruct(dims, dtype)


def on_device(
    flow_state,
    source_term,
    pseudo_time,
    volume_jacobian,
    side_jacobian,
    span_jacobian,
    line_inverse,
    mirror_face,
    edge_flip,
):
    early, fixed = (jnp.asarray(value) for value in constants())
    groups = lax.axis_size("span") // SEG

    def ring(value, axis, step):
        count = lax.axis_size(axis)
        return lax.ppermute(value, axis, [(i, (i + step) % count) for i in range(count)])

    flow = flow_state.reshape(64, 320)
    plane, up, down, last, first = call(
        pack_kernel,
        (shape(16, 320), shape(32, 320), shape(32, 320), shape(8, 320), shape(8, 320)),
        [VM],
        limit=4,
        name="pack",
    )(flow)
    with jax.named_scope("halo"):
        below, above = ring(last, "span", 1), ring(first, "span", -1)
        gy_low, gy_high = ring(up, "gy", 1), ring(down, "gy", -1)
        plane = ring(plane, "gx", 1)

    inverse = line_inverse.reshape(LINES, 320, 320)
    natural = [
        volume_jacobian.transpose(0, 3, 4, 5, 1, 2).reshape(4, 75, 2, SEG),
        side_jacobian.transpose(0, 1, 4, 5, 3, 2).reshape(LINES, 25, 4, SEG),
        span_jacobian.transpose(0, 1, 4, 5, 3, 2).reshape(LINES, 25, 2, SEG),
        mirror_face.transpose(0, 1, 3, 2).reshape(LINES, 4, SEG),
        edge_flip.transpose(0, 1, 3, 2).reshape(LINES, 4, SEG),
    ]
    high, low, rows_high, rows_low, fwd, bwd, tables, own, volume = call(
        prepare_kernel,
        (
            shape(320, 320, dtype=BF16),
            shape(320, 320, dtype=BF16),
            shape(160, 320, dtype=BF16),
            shape(160, 320, dtype=BF16),
            shape(160, 256, dtype=BF16),
            shape(80, 256, dtype=BF16),
            shape(248, 128),
            shape(800, 128),
            shape(320, 128),
        ),
        [HBM] * 9,
        scratch=[
            pltpu.VMEM((320, 320), F32),
            pltpu.VMEM(early.shape, BF16),
            pltpu.VMEM(fixed.shape, BF16),
            pltpu.VMEM(flow.shape, F32),
        ]
        + [pltpu.VMEM(x.shape, x.dtype) for x in natural]
        + [pltpu.VMEM((192, 640), F32), pltpu.SemaphoreType.DMA((10,))],
        limit=28,
        flops=4_000_000_000,
        moved=8_000_000,
        name="prepare",
    )(
        *(
            pltpu.with_memory_space_constraint(x, pltpu.HBM)
            for x in (inverse, early, fixed, flow, *natural)
        )
    )

    operator = call(
        span_kernel,
        shape(320, 128),
        [VM] * 6,
        scratch=[pltpu.VMEM((64, 320), F32)],
        limit=16,
        flops=1_000_000_000,
        moved=3_000_000,
        name="span",
    )(below, above, tables, own, volume, fixed)
    residual, sent = call(
        sweep_kernel,
        (shape(64, 320), shape(64, 384)),
        [VM] * 10,
        scratch=[pltpu.VMEM((192, 320), F32)],
        limit=16,
        flops=1_000_000_000,
        moved=3_000_000,
        name="sweep",
    )(
        flow,
        plane,
        gy_low,
        gy_high,
        source_term.reshape(64, 320),
        pseudo_time.reshape(64, 320),
        tables,
        own,
        operator,
        fixed,
    )

    within = [[SEG * g + m for m in range(SEG)] for g in range(groups)]

    def exchange(value):
        value = value.reshape(SEG, 8, 384)
        value = lax.all_to_all(value, "span", 0, 0, axis_index_groups=within, tiled=True)
        return value.reshape(64, 384)

    z_both, v_both, t_maps, crossed, lefts, whole, short, turned = call(
        maps_kernel,
        (
            shape(SEG, SEG, 80, 256, dtype=BF16),
            shape(SEG, SEG, 80, 512, dtype=BF16),
            shape(SEG, 128, 128),
            shape(SEG, 80, 128),
            shape(SEG, 80, 384, dtype=BF16),
            shape(80, 256),
            shape(80, 128),
            shape(320, 128),
        ),
        [VM] * 6,
        scratch=[
            pltpu.VMEM((SEG, SEG, 50, 128), F32),
            pltpu.VMEM((SEG, 160, 128), F32),
            pltpu.VMEM((SEG, 80, 128), F32),
            pltpu.VMEM((SEG, 80, 256), F32),
            pltpu.VMEM((SEG, SEG, 80, 128), F32),
        ],
        limit=28,
        name="maps",
    )(exchange(sent), rows_high, rows_low, fwd, bwd, fixed)
    wholes = [whole] + [
        ring(short if distance == 1 else whole, "span", SEG * distance)
        for distance in range(1, groups)
    ]
    fused = call(
        fuse_kernel,
        (
            shape(SEG, 88, 640),
            shape(SEG, 168, 640),
            shape(64, 320),
            shape(320, 256, dtype=BF16),
            shape(320, 256, dtype=BF16),
        ),
        [VM] * 9,
        limit=24,
        flops=5_000_000_000,
        moved=12_000_000,
        name="fuse",
    )(z_both, v_both, t_maps, crossed, lefts, turned, high, low, fixed)
    answers = call(
        solve_kernel,
        shape(64, 384),
        [VM] * (groups + 6),
        scratch=[pltpu.VMEM((groups, 80, 128), F32)] * 3,
        limit=16,
        name="solve",
    )(*wholes, *fused, fixed)
    updated = call(finish_kernel, shape(64, 320), [VM] * 2, limit=4, name="finish")(
        exchange(answers), flow
    )
    return updated.reshape(flow_state.shape), residual.reshape(flow_state.shape)


def solution(mesh):
    lines = P("gx", "gy", "span", None)
    blocks = P("gx", "gy", "span", None, None, None)
    return jax.shard_map(
        on_device,
        mesh=mesh,
        in_specs=(lines, lines, lines, blocks, blocks, blocks, P("gx", "gy", None, None), lines, lines),
        out_specs=(lines, lines),
        check_vma=False,
    )
```

```python
import functools

import jax
import jax.numpy as jnp
import numpy as np
from jax import lax
from jax.experimental import pallas as pl
from jax.experimental.pallas import tpu as pltpu
from jax.sharding import PartitionSpec as P

LIFT = 6.0
F32 = jnp.float32
BF16 = jnp.bfloat16
LINES = 8
SEG = 8


def derivative_matrix():
    points = np.array([-1.0, -1.0 / np.sqrt(5.0), 1.0 / np.sqrt(5.0), 1.0])
    matrix = np.zeros((4, 4))
    for target in range(4):
        for source in range(4):
            if target != source:
                numerator = 1.0
                denominator = 1.0
                for other in range(4):
                    if other != source and other != target:
                        numerator *= points[target] - points[other]
                    if other != source:
                        denominator *= points[source] - points[other]
                matrix[target, source] = numerator / denominator
    for target in range(4):
        matrix[target, target] = -np.sum(matrix[target])
    return matrix


def entry(a, b, c, v):
    return ((4 * a + b) * 4 + c) * 5 + v


@functools.cache
def constants():
    select = np.zeros((1120, 320), np.float32)
    place = np.zeros((320, 800), np.float32)
    layers = np.zeros((160, 320), np.float32)
    for v in range(5):
        for a in range(4):
            for b in range(4):
                for c in range(4):
                    row = v * 64 + a * 16 + b * 4 + c
                    select[row, entry(a, b, c, v)] = 1
                    place[entry(a, b, c, v), row] = 1
        for e in range(4):
            for c in range(4):
                row = v * 16 + e * 4 + c
                for side, plane in enumerate((0, 3)):
                    for flip in range(2):
                        along = 3 - e if flip else e
                        block = (side * 2 + flip) * 80
                        select[320 + block + row, entry(plane, along, c, v)] = 1
                        select[640 + block + row, entry(along, plane, c, v)] = 1
                    place[entry(plane, e, c, v), 320 + 80 * side + row] = -1
                    place[entry(e, plane, c, v), 480 + 80 * side + row] = -1
        for a in range(4):
            for b in range(4):
                row = v * 16 + a * 4 + b
                select[960 + row, entry(a, b, 3, v)] = 1
                select[1040 + row, entry(a, b, 0, v)] = 1
                place[entry(a, b, 0, v), 640 + row] = -1
                place[entry(a, b, 3, v), 720 + row] = -1
                layers[row, entry(a, b, 3, v)] = 1
                layers[80 + row, entry(a, b, 0, v)] = 1
    top, bottom = layers[:80].T, layers[80:].T
    columns_high = np.zeros((320, 512), np.float32)
    columns_low = np.zeros((320, 512), np.float32)
    for base, chosen in ((0, bottom), (256, top)):
        columns_high[:, base : base + 80] = chosen
        columns_high[:, base + 80 : base + 160] = chosen
        columns_low[:, base + 160 : base + 240] = chosen
    spread = np.zeros((320, 256))
    spread[:, :80], spread[:, 128:208] = bottom, top
    eye, d = np.eye(4), derivative_matrix()
    along = np.concatenate(
        [
            np.kron(np.kron(d, eye), eye),
            np.kron(np.kron(eye, d), eye),
            np.kron(np.kron(eye, eye), d),
        ],
        axis=1,
    )
    high = along.astype(jnp.bfloat16).astype(np.float64)
    along = np.concatenate([high, high, along - high], axis=1)
    twice = np.concatenate([np.eye(64), np.eye(64)], axis=1)
    ordered = np.zeros((64, 128))
    for e in range(8):
        for k in range(8):
            ordered[8 * e + k, [8 * k + e, 64 + 8 * k + e]] = 1
    eye_320 = np.eye(320)
    blocks = [
        select,
        place[:, :320],
        place[:, 320:640],
        place[:, 640:],
        along[:, :192],
        along[:, 384:],
        twice,
        eye_320,
        spread,
        layers,
        ordered,
    ]
    fixed = np.zeros((sum(len(block) for block in blocks), 320), np.float32)
    at = 0
    for block in blocks:
        fixed[at : at + len(block), : block.shape[1]] = block
        at += len(block)
    early = np.zeros((800, 512), np.float32)
    early[:320], early[320:640], early[640:, :320] = columns_high, columns_low, layers
    return early.astype(jnp.bfloat16), fixed.astype(jnp.bfloat16)


SELECT_VOLUME, SELECT_A, SELECT_B, SELECT_LAYERS = (
    slice(0, 320),
    slice(320, 640),
    slice(640, 960),
    slice(960, 1120),
)
SELECT, PLACE_A, PLACE_B, PLACE_C = slice(0, 1120), slice(1120, 1440), slice(1440, 1760), slice(1760, 2080)
ALONG, ALONG_HIGH, ALONG_LOW = slice(2080, 2208), slice(2080, 2144), slice(2144, 2208)
TWICE = slice(2208, 2272)
EYE, SPREAD, LAYERS = slice(2272, 2592), slice(2592, 2912), slice(2912, 3072)
ORDERED = slice(3072, 3136)
SIDE, SPAN, MIRROR, FLIP = 80, 184, 240, 244


def dot(a, b):
    return lax.dot_general(a, b, (((1,), (0,)), ((), ())), preferred_element_type=F32)


def dot_nt(a, b):
    return lax.dot_general(a, b, (((1,), (1,)), ((), ())), preferred_element_type=F32)


def split(x):
    high = x.astype(BF16)
    return high, (x - high.astype(F32)).astype(BF16)


def split_3(x):
    high = x.astype(BF16)
    rest = x - high.astype(F32)
    middle = rest.astype(BF16)
    return high, middle, (rest - middle.astype(F32)).astype(BF16)


def lanes(shape):
    return lax.broadcasted_iota(jnp.int32, shape, len(shape) - 1)


def rows(shape):
    return lax.broadcasted_iota(jnp.int32, shape, len(shape) - 2)


def roll(x, amount):
    return pltpu.roll(x, amount % 128, 1)


def pair_lanes(x):
    high = x.astype(BF16).astype(F32)
    return jnp.where(lanes(x.shape) < 64, high, roll(x - high, 64)).astype(BF16)


def left_cat(x):
    high, low = split(x)
    return jnp.concatenate([high, high, low], axis=1)


def right_cat(x):
    high, low = split(x)
    return jnp.concatenate([high, low, high], axis=0)


def pack_kernel(flow_in, plane_out, up_out, down_out, last_out, first_out, flow, arrived):
    copy = pltpu.make_async_copy(flow_in, flow, arrived)
    copy.start()
    copy.wait()
    at = pl.multiple_of((1 - lax.axis_index("gx")) * 48, 16)
    plane_out[...] = flow[pl.ds(at, 16)]
    for i in range(4):
        down_out[8 * i : 8 * i + 8] = flow[16 * i : 16 * i + 8]
        up_out[8 * i : 8 * i + 8] = flow[16 * i + 8 : 16 * i + 16]
    for line in range(LINES):
        first_out[line : line + 1] = flow[8 * line : 8 * line + 1]
        last_out[line : line + 1] = flow[8 * line + 7 : 8 * line + 8]


def chosen_of(matrix, values):
    both = dot_nt(matrix, jnp.concatenate(split(values), axis=0))
    return both + roll(both, 64)


def prepare_kernel(
    inverse,
    early_in,
    fixed_in,
    flow_in,
    volume_in,
    side_in,
    span_in,
    mirror_in,
    flip_in,
    high_out,
    low_out,
    rows_high,
    rows_low,
    fwd_out,
    bwd_out,
    tables,
    own_out,
    volume_out,
    held,
    early,
    fixed,
    flow,
    volume_jacobian,
    side_jacobian,
    span_jacobian,
    mirror_face,
    edge_flip,
    flux,
    arrived,
):
    pairs = [
        (volume_in, volume_jacobian),
        (side_in, side_jacobian),
        (span_in, span_jacobian),
        (mirror_in, mirror_face),
        (flip_in, edge_flip),
        (flow_in, flow),
        (fixed_in.at[SELECT], fixed.at[SELECT]),
        (fixed_in.at[ALONG], fixed.at[ALONG]),
    ]
    pairs += [(inverse.at[lax.rem(lax.axis_index("span"), LINES)], held), (early_in, early)]
    copies = [
        pltpu.make_async_copy(source, target, arrived.at[at])
        for at, (source, target) in enumerate(pairs)
    ]
    for copy in copies:
        copy.start()
    for copy in copies[:5]:
        copy.wait()
    for line in range(LINES):
        here = slice(8 * line, 8 * line + 8)
        tables[0:75, here] = volume_jacobian[line // 2, :, line % 2, :]
        tables[SIDE : SIDE + 100, here] = side_jacobian[line].reshape(100, 8)
        tables[SPAN : SPAN + 50, here] = LIFT * span_jacobian[line].reshape(50, 8)
        tables[MIRROR : MIRROR + 4, here] = mirror_face[line].astype(F32)
        tables[FLIP : FLIP + 4, here] = edge_flip[line].astype(F32)
    for copy in copies[5:8]:
        copy.wait()

    own = chosen_of(fixed[SELECT], flow[...])
    own_out[...] = jnp.where(lanes((800, 128)) < 64, own[320:], 0.0)
    by_variable = slabs_of(own[0:320], 64)
    for d in range(3):
        mixed = mix(lambda w, v: tables[d * 25 + w * 5 + v : d * 25 + w * 5 + v + 1, :], by_variable)
        for w in range(5):
            flux[d * 64 : d * 64 + 64, w * 128 : w * 128 + 128] = mixed[w]
    flux_high, flux_low = split(flux[...])
    volume = dot(fixed[ALONG_HIGH, 0:192], flux_high) + dot(fixed[ALONG_HIGH, 0:192], flux_low)
    volume = volume + dot(fixed[ALONG_LOW, 0:192], flux_high)
    for w in range(5):
        volume_out[w * 64 : w * 64 + 64] = volume[:, w * 128 : w * 128 + 128]

    for copy in copies[8:]:
        copy.wait()
    high_out[...], low_out[...] = split(held[...])
    layers = early[640:800, 0:320]
    rows_high[...] = dot(layers, high_out[...]).astype(BF16)
    rows_low[...] = dot(layers, low_out[...]).astype(BF16)
    both = dot(rows_high[...], early[0:320]) + dot(rows_low[...], early[320:640])
    both = both.astype(BF16)
    fwd_out[...] = both[:, :256]
    bwd_out[...] = both[80:, 256:]


def unpack(left, right):
    lane = lanes((80, 128))
    forward = jnp.where(lane < 88, roll(right, 88), 0.0)
    cross = jnp.where(lane < 88, left, 0.0)
    back = jnp.where(lane < 40, roll(left, 40), jnp.where(lane < 80, roll(right, 40), 0.0))
    return forward, cross, back


def mix(coefficient, slabs):
    out = []
    for w in range(5):
        total = coefficient(w, 0) * slabs[0]
        for v in range(1, 5):
            total = total + coefficient(w, v) * slabs[v]
        out.append(total)
    return out


def slabs_of(x, size):
    return [x[v * size : (v + 1) * size] for v in range(5)]


def span_kernel(below, above, tables, own_in, volume_in, fixed, operator_out, extended):
    position = rows((8, 320))
    for line in range(LINES):
        extended[8 * line : 8 * line + 8] = jnp.where(
            position == 0,
            below[line : line + 1],
            jnp.where(position == 7, above[line : line + 1], 0.0),
        )
    far_layers = chosen_of(fixed[SELECT_LAYERS], extended[...])
    lane = lanes((1, 128))
    table = lambda r: tables[r : r + 1, :]
    pieces = []
    top, bottom = own_in[640:720], own_in[720:800]
    outer_top, outer_bottom = far_layers[0:80], far_layers[80:160]
    lower_jump = jnp.where(lane % 8 == 0, outer_top, roll(top, 1)) - bottom
    upper_jump = jnp.where(lane % 8 == 7, outer_bottom, roll(bottom, -1)) - top
    pieces += mix(lambda w, v: table(SPAN + (w * 5 + v) * 2), slabs_of(lower_jump, 16))
    pieces += mix(lambda w, v: table(SPAN + (w * 5 + v) * 2 + 1), slabs_of(upper_jump, 16))
    operator = dot(fixed[PLACE_A], pair_lanes(volume_in[...]))
    pieces = pair_lanes(jnp.concatenate(pieces, axis=0))
    operator_out[...] = operator + dot(fixed[PLACE_C, 0:160], pieces)


def sweep_kernel(
    flow,
    plane,
    gy_low,
    gy_high,
    source,
    pseudo,
    tables,
    own_in,
    operator_in,
    fixed,
    residual_out,
    sent_out,
    extended,
):
    gx_at, gy_at = lax.axis_index("gx"), lax.axis_index("gy")
    first_lo = (gx_at > 0).astype(F32)
    second_lo = (gy_at > 0).astype(F32)
    second_hi = (gy_at < lax.axis_size("gy") - 1).astype(F32)
    extended[0:64] = jnp.zeros((64, 320), F32)
    extended[64:80] = plane[...] * (1.0 - first_lo)
    extended[80:112] = jnp.zeros((32, 320), F32)
    extended[112:128] = plane[...] * first_lo
    for i in range(4):
        extended[128 + 16 * i : 136 + 16 * i] = gy_low[8 * i : 8 * i + 8] * second_lo
        extended[136 + 16 * i : 144 + 16 * i] = gy_high[8 * i : 8 * i + 8] * second_hi
    near_a = sum(dot_nt(fixed[SELECT_A], part) for part in split(extended[0:128])) + own_in[0:320]
    near_b, far_b = own_in[320:640], chosen_of(fixed[SELECT_B], extended[128:192])
    lane = lanes((1, 128))
    table = lambda r: tables[r : r + 1, :]
    pieces = []

    for f in range(4):
        near = near_a if f < 2 else near_b
        candidates = [near[80 * n : 80 * n + 80] for n in range(4)]
        outer = [far_b[80 * n : 80 * n + 80] for n in range(4)]
        own = candidates[2 * (f % 2)]
        if f == 0:
            shifted = [roll(x, 16) for x in candidates]
        elif f == 1:
            shifted = [roll(x, -16) for x in candidates]
        elif f == 2:
            shifted = [
                jnp.where((lane // 8) % 2 == 1, roll(x, 8), y) for x, y in zip(candidates, outer)
            ]
        else:
            shifted = [
                jnp.where((lane // 8) % 2 == 0, roll(x, -8), y) for x, y in zip(candidates, outer)
            ]
        mirrored = table(MIRROR + f) > 0.5
        flipped = table(FLIP + f) > 0.5
        neighbour = jnp.where(
            flipped,
            jnp.where(mirrored, shifted[3], shifted[1]),
            jnp.where(mirrored, shifted[2], shifted[0]),
        )
        jump = LIFT * (neighbour - own)
        pieces += mix(lambda w, v: table(SIDE + (w * 5 + v) * 4 + f), slabs_of(jump, 16))

    pieces = pair_lanes(jnp.concatenate(pieces, axis=0))
    operator = operator_in[...] + dot(fixed[PLACE_B], pieces)
    operator_high, operator_low = split(operator)
    twice = fixed[TWICE, 0:128]
    operator_rows = dot_nt(twice, operator_high) + dot_nt(twice, operator_low)
    residual = source[...] - (pseudo[...] * flow[...] + operator_rows)
    residual_out[...] = residual

    turned = [jnp.zeros((64, 128), F32), tables[SPAN : SPAN + 56], jnp.zeros((8, 128), F32)]
    sent_out[:, 256:384] = jnp.transpose(jnp.concatenate(turned, axis=0))[:64]
    sent_out[:, 0:320] = residual


def maps_kernel(
    received,
    rows_high,
    rows_low,
    fwd,
    bwd,
    fixed,
    z_both,
    v_both,
    t_out,
    crossed_out,
    lefts_out,
    whole_out,
    short_out,
    turned_out,
    wide,
    started,
    t_state,
    w_state,
    bottoms,
):
    last = jnp.concatenate([received[:, 256:384], jnp.zeros((64, 128), F32)], axis=0)
    jacobians = jnp.transpose(last)[64:114]
    high, low = split(received[:, 0:320])
    turned = dot_nt(fixed[EYE], jnp.concatenate([high, low], axis=0))
    turned_out[...] = turned + roll(turned, 64)
    turned = turned.astype(BF16)
    traces = dot(rows_high[...], turned) + dot(rows_low[...], turned)
    traces = traces + roll(traces, 64)
    trace_lane = lanes((160, 128))
    small_lane, small_row = lanes((80, 128)), rows((80, 128))
    for e in range(SEG):
        for k in range(SEG):
            at = e * SEG + k
            wide[e, k] = jnp.broadcast_to(jacobians[:, at : at + 1], (50, 128))
        moved = roll(traces, 80 - 8 * e)
        started[e] = jnp.where((trace_lane >= 80) & (trace_lane < 88), moved, 0.0)

    def coupled(e, k, side, state):
        out = mix(lambda w, v: wide[e, k, pl.ds((w * 5 + v) * 2 + side, 1)], slabs_of(state, 16))
        return jnp.concatenate(out, axis=0)

    diagonal = (small_lane[:16] % 16 == small_row[:16]) & (small_lane[:16] < 80)

    def coupled_identity(e, k, side):
        out = []
        for w in range(5):
            line = [wide[e, k, pl.ds((w * 5 + v) * 2 + side, 1)] for v in range(5)]
            row = line[4]
            for v in range(3, -1, -1):
                row = jnp.where(small_lane[:1] < 16 * v + 16, line[v], row)
            out.append(jnp.where(diagonal, row, 0.0))
        return jnp.concatenate(out, axis=0)

    for k in range(SEG):
        mine = small_lane == 80 + k
        for pair in range(0, SEG, 2):
            cats = []
            for e in (pair, pair + 1):
                z = coupled(e, k, 0, t_state[e]) if k else coupled_identity(e, k, 0)
                z_hi, z_lo = split(z)
                z_both[e, k, :, 0:128] = z_hi
                z_both[e, k, :, 128:256] = z_lo
                cats.append(jnp.concatenate([z_hi, z_lo, z_hi], axis=0))
            both = dot(fwd[:, 0:240], jnp.concatenate(cats, axis=1))
            for e, y in ((pair, both[:, :128]), (pair + 1, both[:, 128:])):
                t_state[e] = y[:80] + jnp.where(mine, started[e, 0:80], 0.0)
                bottoms[e, k] = y[80:] + jnp.where(mine, started[e, 80:160], 0.0)

    tall_lane, tall_row = lanes((128, 128)), rows((128, 128))
    ones = jnp.where((tall_row >= 80) & (tall_row < 88) & (tall_lane == 80), 1.0, 0.0)
    state = jnp.where((tall_row < 80) & (tall_lane == tall_row), 1.0, 0.0) + ones
    states = []
    for step in range(SEG):
        k = SEG - 1 - step
        for e in range(SEG):
            if step:
                halves = (w_state[e, :, 0:128], w_state[e, :, 128:256])
                z = [coupled(e, k, 1, half) for half in halves]
            else:
                z = coupled_identity(e, k, 1)
                z = [
                    jnp.where(small_lane >= 88, roll(z, 88), 0.0),
                    jnp.where(small_lane < 40, roll(z, 88), 0.0),
                ]
            z_hi, z_lo = split(jnp.concatenate(z, axis=1))
            v_both[e, k, :, 0:256] = z_hi
            v_both[e, k, :, 256:512] = z_lo
            y = dot(bwd[:, 0:240], jnp.concatenate([z_hi, z_lo, z_hi], axis=0))
            w_state[e, :, 0:128] = y[:, :128] + bottoms[e, k]
            w_state[e, :, 128:256] = y[:, 128:]
        t_out[step] = state
        states.append(right_cat(state))
        y = dot(left_cat(t_state[step]), states[-1])
        state = jnp.concatenate([y, ones[80:]], axis=0)

    maps = []
    for e in range(SEG):
        left, right = w_state[e, :, 0:128], w_state[e, :, 128:256]
        _, cross, back = unpack(left, right)
        crossed = dot(left_cat(cross), states[e])
        lefts_out[e] = left_cat(back)
        crossed_out[e] = crossed
        maps.append((crossed + jnp.where(small_lane < 88, 0.0, left), right))
    zero = jnp.zeros((48, 128), F32)
    lefts = [lefts_out[e] for e in range(SEG)]
    while len(maps) > 1:
        joined = []
        for at in range(0, len(maps), 2):
            after = [right_cat(jnp.concatenate([x, zero], axis=0)) for x in maps[at + 1]]
            y = dot(lefts[at], jnp.concatenate(after, axis=1))
            kept = jnp.where(small_lane < 88, maps[at][0], 0.0)
            joined.append((y[:, :128] + kept, y[:, 128:]))
        maps = joined
        lefts = [left_cat(unpack(*both)[2]) for both in maps]
    whole_out[:, 0:128] = maps[0][0]
    whole_out[:, 128:256] = maps[0][1] + roll(state[:80], 40)
    groups = lax.axis_size("span") // SEG
    last = lax.axis_index("span") // SEG == groups - 1
    short_out[...] = jnp.where(last, maps[0][0], state[:80])


def against_pair(x):
    high, low = split(x)
    upper = jnp.concatenate([high, high], axis=1)
    return jnp.concatenate([upper, jnp.concatenate([low, jnp.zeros_like(low)], axis=1)], axis=0)


def fuse_kernel(
    z_both, v_both, t_in, crossed, lefts, turned, high, low, fixed, r_out, q_out, base_out, gs_high, gs_low
):
    tall_lane, tall_row = lanes((128, 128)), rows((128, 128))
    zero = jnp.zeros((48, 128), F32)
    w0 = jnp.where(tall_lane == tall_row + 88, 1.0, 0.0)
    w1 = jnp.where((tall_lane == tall_row - 40) & (tall_row < 80), 1.0, 0.0)
    for e in range(SEG - 1, -1, -1):
        behind = jnp.concatenate([w0[:80], w1[:80]], axis=1)
        if e > 0:
            y = dot(lefts[e], jnp.concatenate([right_cat(w0), right_cat(w1)], axis=1))
            w0 = jnp.concatenate([y[:, :128] + crossed[e], zero], axis=0)
            w1 = jnp.concatenate([y[:, 128:], zero], axis=0)
        state = t_in[e]
        r = dot_nt(against_pair(jnp.transpose(state)[:96]), z_both[e].reshape(640, 256))
        r_out[e] = r[:88] + r[96:184]
        first = jnp.concatenate([state[:88], jnp.zeros((88, 128), F32)], axis=1)
        both = jnp.concatenate([first, behind, jnp.zeros((88, 256), F32)], axis=0)
        q = dot_nt(against_pair(jnp.transpose(both)[:176]), v_both[e].reshape(640, 512))
        q_out[e] = q[:168] + q[176:344]
    load = pair_lanes(turned[...])
    total_high, total_low = split(dot(high[...], load) + dot(low[...], load))
    twice = fixed[TWICE, 0:128]
    base_out[...] = dot_nt(twice, total_high) + dot_nt(twice, total_low)
    gs_high[...] = dot(high[...], fixed[SPREAD, 0:256]).astype(BF16)
    gs_low[...] = dot(low[...], fixed[SPREAD, 0:256]).astype(BF16)


def by_element(x):
    tiles = [x[:, 128 * n : 128 * n + 128] for n in range(5)]
    lane = lanes((8, 128))
    out = []
    for k in range(SEG):
        at, shift = divmod(80 * k, 128)
        y = roll(tiles[at], -shift)
        if shift + 80 > 128:
            y = jnp.where(lane < 128 - shift, y, roll(tiles[at + 1], -shift))
        out.append(jnp.where(lane < 80, y, 0.0))
    return jnp.concatenate(out, axis=0)


def solve_kernel(*refs):
    *parts, r_in, q_in, base, gs_high, gs_low, fixed, out, forwards, crosses, backs_in = refs
    groups = len(parts)
    mine = lax.axis_index("span") // SEG
    lane = lanes((80, 128))
    for distance, part in enumerate(parts):
        group = lax.rem(mine - distance + groups, groups)
        if distance == 1:
            pieces = part[...], part[...], part[...]
        else:
            pieces = unpack(part[:, 0:128], part[:, 128:256])
        forwards[group], crosses[group], backs_in[group] = pieces
    one = jnp.where(rows((128, 128)) == 80, 1.0, 0.0)
    zero = jnp.zeros((48, 128), F32)
    traces = [one]
    for group in range(groups - 1):
        y = dot(left_cat(forwards[group]), right_cat(traces[-1]))
        traces.append(jnp.concatenate([y, zero], axis=0) + one)
    backs = [jnp.zeros((128, 128), F32)]
    for group in range(groups - 1, 0, -1):
        y = dot(left_cat(crosses[group]), right_cat(traces[group]))
        if group < groups - 1:
            y = y + dot(left_cat(backs_in[group]), right_cat(backs[0]))
        backs.insert(0, jnp.concatenate([y, zero], axis=0))
    trace, back = traces[0], backs[0]
    for group in range(1, groups):
        trace = jnp.where(mine == group, traces[group], trace)
        back = jnp.where(mine == group, backs[group], back)
    lower_in = jnp.concatenate([trace[:88]] * 5, axis=1)
    upper_in = jnp.concatenate([lower_in, jnp.concatenate([back[:80]] * 5, axis=1)], axis=0)
    lower = [jnp.sum(r_in[e] * lower_in, axis=0, keepdims=True) for e in range(SEG)]
    upper = [jnp.sum(q_in[e] * upper_in, axis=0, keepdims=True) for e in range(SEG)]
    coupled = [by_element(jnp.concatenate(x, axis=0)) for x in (lower, upper)]
    high, low = split(jnp.concatenate(coupled, axis=1))
    coupled = jnp.concatenate([high, low], axis=0)
    total = dot_nt(gs_high[...], coupled) + dot_nt(gs_low[...], coupled)
    total_high, total_low = split(total)
    ordered = fixed[ORDERED, 0:128]
    out[:, 0:320] = base[...] + dot_nt(ordered, total_high) + dot_nt(ordered, total_low)
    out[:, 320:384] = jnp.zeros((64, 64), F32)


def finish_kernel(incoming, flow, out):
    out[...] = flow[...] + incoming[:, 0:320]


def call(kernel, out_shape, in_specs, scratch=(), limit=16, flops=0, moved=0, name=None):
    return pl.pallas_call(
        kernel,
        out_shape=out_shape,
        in_specs=in_specs,
        out_specs=jax.tree.map(lambda _: pl.BlockSpec(memory_space=pltpu.VMEM), out_shape),
        scratch_shapes=list(scratch),
        compiler_params=pltpu.CompilerParams(vmem_limit_bytes=limit * 1024 * 1024),
        cost_estimate=pl.CostEstimate(flops=flops, bytes_accessed=moved, transcendentals=0),
        name=name,
    )


VM = pl.BlockSpec(memory_space=pltpu.VMEM)
HBM = pl.BlockSpec(memory_space=pltpu.HBM)


def shape(*dims, dtype=F32):
    return jax.ShapeDtypeStruct(dims, dtype)


def on_device(
    flow_state,
    source_term,
    pseudo_time,
    volume_jacobian,
    side_jacobian,
    span_jacobian,
    line_inverse,
    mirror_face,
    edge_flip,
):
    early, fixed = (jnp.asarray(value) for value in constants())
    groups = lax.axis_size("span") // SEG

    def ring(value, axis, step):
        count = lax.axis_size(axis)
        return lax.ppermute(value, axis, [(i, (i + step) % count) for i in range(count)])

    flow = flow_state.reshape(64, 320)
    plane, up, down, last, first = call(
        pack_kernel,
        (shape(16, 320), shape(32, 320), shape(32, 320), shape(8, 320), shape(8, 320)),
        [HBM],
        scratch=[pltpu.VMEM((64, 320), F32), pltpu.SemaphoreType.DMA(())],
        limit=4,
        name="pack",
    )(pltpu.with_memory_space_constraint(flow, pltpu.HBM))
    with jax.named_scope("halo"):
        below, above = ring(last, "span", 1), ring(first, "span", -1)
        gy_low, gy_high = ring(up, "gy", 1), ring(down, "gy", -1)
        plane = ring(plane, "gx", 1)

    inverse = line_inverse.reshape(LINES, 320, 320)
    natural = [
        volume_jacobian.transpose(0, 3, 4, 5, 1, 2).reshape(4, 75, 2, SEG),
        side_jacobian.transpose(0, 1, 4, 5, 3, 2).reshape(LINES, 25, 4, SEG),
        span_jacobian.transpose(0, 1, 4, 5, 3, 2).reshape(LINES, 25, 2, SEG),
        mirror_face.transpose(0, 1, 3, 2).reshape(LINES, 4, SEG),
        edge_flip.transpose(0, 1, 3, 2).reshape(LINES, 4, SEG),
    ]
    high, low, rows_high, rows_low, fwd, bwd, tables, own, volume = call(
        prepare_kernel,
        (
            shape(320, 320, dtype=BF16),
            shape(320, 320, dtype=BF16),
            shape(160, 320, dtype=BF16),
            shape(160, 320, dtype=BF16),
            shape(160, 256, dtype=BF16),
            shape(80, 256, dtype=BF16),
            shape(248, 128),
            shape(800, 128),
            shape(320, 128),
        ),
        [HBM] * 9,
        scratch=[
            pltpu.VMEM((320, 320), F32),
            pltpu.VMEM(early.shape, BF16),
            pltpu.VMEM(fixed.shape, BF16),
            pltpu.VMEM(flow.shape, F32),
        ]
        + [pltpu.VMEM(x.shape, x.dtype) for x in natural]
        + [pltpu.VMEM((192, 640), F32), pltpu.SemaphoreType.DMA((10,))],
        limit=28,
        flops=4_000_000_000,
        moved=8_000_000,
        name="prepare",
    )(
        *(
            pltpu.with_memory_space_constraint(x, pltpu.HBM)
            for x in (inverse, early, fixed, flow, *natural)
        )
    )

    operator = call(
        span_kernel,
        shape(320, 128),
        [VM] * 6,
        scratch=[pltpu.VMEM((64, 320), F32)],
        limit=16,
        flops=1_000_000_000,
        moved=3_000_000,
        name="span",
    )(below, above, tables, own, volume, fixed)
    residual, sent = call(
        sweep_kernel,
        (shape(64, 320), shape(64, 384)),
        [VM] * 10,
        scratch=[pltpu.VMEM((192, 320), F32)],
        limit=16,
        flops=1_000_000_000,
        moved=3_000_000,
        name="sweep",
    )(
        flow,
        plane,
        gy_low,
        gy_high,
        source_term.reshape(64, 320),
        pseudo_time.reshape(64, 320),
        tables,
        own,
        operator,
        fixed,
    )

    within = [[SEG * g + m for m in range(SEG)] for g in range(groups)]

    def exchange(value):
        value = value.reshape(SEG, 8, 384)
        value = lax.all_to_all(value, "span", 0, 0, axis_index_groups=within, tiled=True)
        return value.reshape(64, 384)

    z_both, v_both, t_maps, crossed, lefts, whole, short, turned = call(
        maps_kernel,
        (
            shape(SEG, SEG, 80, 256, dtype=BF16),
            shape(SEG, SEG, 80, 512, dtype=BF16),
            shape(SEG, 128, 128),
            shape(SEG, 80, 128),
            shape(SEG, 80, 384, dtype=BF16),
            shape(80, 256),
            shape(80, 128),
            shape(320, 128),
        ),
        [VM] * 6,
        scratch=[
            pltpu.VMEM((SEG, SEG, 50, 128), F32),
            pltpu.VMEM((SEG, 160, 128), F32),
            pltpu.VMEM((SEG, 80, 128), F32),
            pltpu.VMEM((SEG, 80, 256), F32),
            pltpu.VMEM((SEG, SEG, 80, 128), F32),
        ],
        limit=28,
        name="maps",
    )(exchange(sent), rows_high, rows_low, fwd, bwd, fixed)
    wholes = [whole] + [
        ring(short if distance == 1 else whole, "span", SEG * distance)
        for distance in range(1, groups)
    ]
    fused = call(
        fuse_kernel,
        (
            shape(SEG, 88, 640),
            shape(SEG, 168, 640),
            shape(64, 320),
            shape(320, 256, dtype=BF16),
            shape(320, 256, dtype=BF16),
        ),
        [VM] * 9,
        limit=24,
        flops=5_000_000_000,
        moved=12_000_000,
        name="fuse",
    )(z_both, v_both, t_maps, crossed, lefts, turned, high, low, fixed)
    answers = call(
        solve_kernel,
        shape(64, 384),
        [VM] * (groups + 6),
        scratch=[pltpu.VMEM((groups, 80, 128), F32)] * 3,
        limit=16,
        name="solve",
    )(*wholes, *fused, fixed)
    updated = call(finish_kernel, shape(64, 320), [VM] * 2, limit=4, name="finish")(
        exchange(answers), flow
    )
    return updated.reshape(flow_state.shape), residual.reshape(flow_state.shape)


def solution(mesh):
    lines = P("gx", "gy", "span", None)
    blocks = P("gx", "gy", "span", None, None, None)
    return jax.shard_map(
        on_device,
        mesh=mesh,
        in_specs=(lines, lines, lines, blocks, blocks, blocks, P("gx", "gy", None, None), lines, lines),
        out_specs=(lines, lines),
        check_vma=False,
    )
```
